256 devices in a mesh: rows: 32 (over x, z), cols: 8 (over y, core).
Axes of the slice: x: 4, y: 4, z: 8, core: 2. Of those that a mesh axis runs over, the one named last changes fastest.
Arguments:
- cost: bfloat16 [32768, 8192], P('rows', 'cols'), may hold values from -12 to 12.45
- src_label: int32 [32768], P('rows'), may hold values from 0 to 63
- tgt_label: int32 [8192], P('cols'), may hold values from 0 to 63
- class_mask: int32 [64, 64], replicated, may hold values from 0 to 1, as said below
- g_start: float32 [8192], P('cols'), may hold values from -1.5 to 1.5
- f_bar: float32 [32768], P('rows'), may hold values from -6 to 6
- g_bar: float32 [8192], P('cols'), may hold values from -6 to 6
- src_emb: bfloat16 [32768, 1024], P('rows'), may hold values from -6 to 6
- tgt_emb: bfloat16 [8192, 1024], P('cols'), may hold values from -6 to 6
Outputs:
- g_start_bar: float32 [8192], P('cols')
- grad_x: float32 [1024, 32768], P('cols', 'rows')
- grad_y: float32 [1024, 8192], P('rows', 'cols')
The draws below stay inside these ranges and needn't reach their ends.
Inputs may be any that keep to these rules, and one draw needn't show every extreme that they name: Every class may be matched with itself: class_mask[c, c] = 1; other entries are 0 or 1.
All inputs are finite; a program needn't handle non-finite values.
Results may differ from the reference program's by a relative error of at most 0.003.
Values sent between devices are 32-bit elements; how exact they have to be, the bound alone decides.
No kernel may reach another device: no remote copies, remote signals or barrier semaphores. Data moves between devices by JAX's collectives and lax.ppermute only.
A program may use at most 64 MiB of HBM per device.

```python
import math
import jax
import jax.numpy as jnp
from jax import lax

D = 1024
CLASSES = 64
K = 3
NS = 32768
NT = 8192


def draw_cost(key, part):
    key = jax.random.fold_in(key, 11)
    keys = jax.random.split(key, 1)
    base = jnp.clip(0.25 * jax.random.normal(keys[0], (NS, NT), jnp.float32), -1.0, 1.0)
    return base.astype(jnp.bfloat16)


def draw_class_mask(key, part):
    key = jax.random.fold_in(key, 12)
    random_bits = jax.random.randint(key, (CLASSES, CLASSES), 0, 2).astype(jnp.int32)
    return jnp.maximum(random_bits, jnp.eye(CLASSES, dtype=jnp.int32))


def touch_ends(array, stream_key, low, top_value):
    longest = array.shape.index(max(array.shape))
    spots = []
    for shift in (0, 1):
        where = [jax.random.randint(jax.random.fold_in(stream_key, axis), (), 0, length) for axis, length in enumerate(array.shape)]
        where[longest] = (where[longest] + shift) % array.shape[longest]
        spots.append(tuple(where))
    return array.at[spots[0]].set(low).at[spots[1]].set(top_value)


def shard_levels(stream_key, dims, pieces, smallest, largest):
    gain, own = 1.0, jax.random.fold_in(stream_key, 6)
    for axis_at, shards_of in pieces:
        heights = jnp.exp(jax.random.uniform(jax.random.fold_in(own, axis_at), (shards_of,), jnp.float32, smallest / len(pieces), largest / len(pieces)))
        gain = gain * jnp.repeat(heights, dims[axis_at] // shards_of).reshape([-1 if axis == axis_at else 1 for axis in range(len(dims))])
    return gain


def noise(rng, dims, scale, bound, shards=(), kind=jnp.bfloat16):
    gain = shard_levels(rng, dims, shards, -0.22, 0.18) if shards else 1.0
    result = jax.random.normal(rng, dims, jnp.float32) * scale * gain
    return jnp.minimum(jnp.maximum(result, -bound), bound).astype(kind)


def setup_inputs(seed: int = 0) -> dict:
    key_list = jax.random.split(jax.random.key(seed), 10)
    return {
        "cost": draw_cost(jax.random.fold_in(key_list[9], 71), 0),
        "src_label": touch_ends(jax.random.randint(key_list[1], (NS,), 0, CLASSES), jax.random.fold_in(key_list[1], 1), 0, CLASSES - 1).astype(jnp.int32),
        "tgt_label": touch_ends(jax.random.randint(key_list[2], (NT,), 0, CLASSES), jax.random.fold_in(key_list[2], 1), 0, CLASSES - 1).astype(jnp.int32),
        "class_mask": draw_class_mask(jax.random.fold_in(key_list[9], 71), 0),
        "g_start": noise(key_list[4], (NT,), 0.25, 1.5, ((0, 8),), jnp.float32),
        "f_bar": noise(key_list[5], (NS,), 1.0, 6.0, ((0, 32),), jnp.float32),
        "g_bar": noise(key_list[6], (NT,), 1.0, 6.0, ((0, 8),), jnp.float32),
        "src_emb": noise(key_list[7], (NS, D), 1.0, 6.0, ((0, 32),)),
        "tgt_emb": noise(key_list[8], (NT, D), 1.0, 6.0, ((0, 8),)),
    }


EPSILON = 0.05
PENALTY = 1.0


def reference(cost, src_label, tgt_label, class_mask, g_start, f_bar, g_bar, src_emb, tgt_emb):
    block_rows = math.gcd(NS, 1024)
    blocks = NS // block_rows
    log_source = -math.log(NS)
    log_target = -math.log(NT)
    block_ids = jnp.arange(blocks, dtype=jnp.int32)

    def shifted_block(block):
        start = (block * block_rows).astype(jnp.int32)
        piece = lax.dynamic_slice_in_dim(cost, start, block_rows, 0).astype(jnp.float32)
        labels = lax.dynamic_slice_in_dim(src_label, start, block_rows, 0)
        allowed = class_mask[labels][:, tgt_label].astype(jnp.float32)
        return piece + PENALTY * (1.0 - allowed), start

    def row_update(col_dual):
        def row_block(block):
            shifted, start = shifted_block(block)
            scores = (col_dual[None, :] - shifted) / EPSILON
            highest = jnp.max(scores, axis=1)
            summed = jnp.sum(jnp.exp(scores - highest[:, None]), axis=1)
            return EPSILON * log_source - EPSILON * (highest + jnp.log(summed))
        return lax.map(row_block, block_ids).reshape(NS)

    def col_update(row_dual):
        def accumulate(carry, block):
            highest, summed = carry
            shifted, start = shifted_block(block)
            part = lax.dynamic_slice_in_dim(row_dual, start, block_rows, 0)
            scores = (part[:, None] - shifted) / EPSILON
            newest = jnp.maximum(highest, jnp.max(scores, axis=0))
            summed = summed * jnp.exp(highest - newest) + jnp.sum(jnp.exp(scores - newest[None, :]), axis=0)
            return (newest, summed), None
        start_carry = (jnp.full((NT,), -jnp.inf, jnp.float32), jnp.zeros((NT,), jnp.float32))
        (highest, summed), unused = lax.scan(accumulate, start_carry, block_ids)
        return EPSILON * log_target - EPSILON * (highest + jnp.log(summed))

    col_duals = [g_start]
    row_duals = []
    for section in range(K):
        row_duals.append(row_update(col_duals[-1]))
        col_duals.append(col_update(row_duals[-1]))

    row_grads = [None] * K
    col_grads = [None] * (K + 1)
    col_grads[K] = g_bar
    for section in reversed(range(K)):
        row_now = row_duals[section]
        col_now = col_duals[section + 1]
        col_prev = col_duals[section]
        col_grad = col_grads[section + 1]
        outer = f_bar if section == K - 1 else jnp.zeros_like(f_bar)

        def row_block(block):
            shifted, start = shifted_block(block)
            part = lax.dynamic_slice_in_dim(row_now, start, block_rows, 0)
            plan_q = jnp.exp((part[:, None] + col_now[None, :] - shifted) / EPSILON - log_target)
            return jnp.sum(plan_q * col_grad[None, :], axis=1)

        row_grad = outer - lax.map(row_block, block_ids).reshape(NS)

        def accumulate(carry, block):
            shifted, start = shifted_block(block)
            part = lax.dynamic_slice_in_dim(row_now, start, block_rows, 0)
            weights = lax.dynamic_slice_in_dim(row_grad, start, block_rows, 0)
            plan_r = jnp.exp((part[:, None] + col_prev[None, :] - shifted) / EPSILON - log_source)
            return carry + jnp.sum(plan_r * weights[:, None], axis=0), None

        summed, unused = lax.scan(accumulate, jnp.zeros((NT,), jnp.float32), block_ids)
        row_grads[section] = row_grad
        col_grads[section] = -summed

    def final(carry, block):
        shifted, start = shifted_block(block)
        cost_grad = jnp.zeros_like(shifted)
        for section in reversed(range(K)):
            part = lax.dynamic_slice_in_dim(row_duals[section], start, block_rows, 0)
            weights = lax.dynamic_slice_in_dim(row_grads[section], start, block_rows, 0)
            plan_q = jnp.exp((part[:, None] + col_duals[section + 1][None, :] - shifted) / EPSILON - log_target)
            plan_r = jnp.exp((part[:, None] + col_duals[section][None, :] - shifted) / EPSILON - log_source)
            cost_grad = cost_grad + plan_q * col_grads[section + 1][None, :] + plan_r * weights[:, None]
        rounded = cost_grad.astype(jnp.bfloat16)
        x_part = lax.dynamic_slice_in_dim(src_emb, start, block_rows, 0)
        x_block = -jnp.dot(rounded, tgt_emb, preferred_element_type=jnp.float32)
        carry = carry - jnp.dot(x_part.T, rounded, preferred_element_type=jnp.float32)
        return carry, x_block

    grad_y, x_blocks = lax.scan(final, jnp.zeros((D, NT), jnp.float32), block_ids)
    grad_x = x_blocks.reshape(NS, D).T
    return col_grads[0], grad_x, grad_y
```

```python
import math

import jax
import jax.numpy as jnp
from jax import lax
from jax.sharding import PartitionSpec as P

K = 3


EPSILON = 0.05
PENALTY = 1.0


def gathered(value, axis):
    count = lax.axis_size(axis)
    copies = jnp.broadcast_to(value.reshape(1, 8, -1), (count, 8, value.shape[0] // 8))
    return lax.all_to_all(copies, axis, 0, 0, tiled=True).reshape(count, -1)


def total(value, axis):
    return jnp.sum(gathered(value, axis), axis=0)


def log_total(scores, reduced, axis):
    highest = jnp.max(scores, axis=reduced, keepdims=True)
    summed = jnp.sum(jnp.exp(scores - highest), axis=reduced)
    local = highest.reshape(-1) + jnp.log(summed)
    parts = gathered(local, axis)
    top = jnp.max(parts, axis=0)
    return top + jnp.log(jnp.sum(jnp.exp(parts - top[None, :]), axis=0))


def body(cost, src_label, tgt_label, class_mask, g_start, f_bar, g_bar, src_emb, tgt_emb):
    row_count = lax.axis_size("rows")
    col_count = lax.axis_size("cols")
    src_rows, tgt_cols = cost.shape
    width = src_emb.shape[1]
    log_source = -math.log(src_rows * row_count)
    log_target = -math.log(tgt_cols * col_count)
    class_ids = jnp.arange(class_mask.shape[0], dtype=jnp.int32)
    src_hot = (src_label[:, None] == class_ids[None, :]).astype(jnp.bfloat16)
    tgt_hot = (tgt_label[:, None] == class_ids[None, :]).astype(jnp.bfloat16)
    src_allowed = jnp.dot(
        src_hot, class_mask.astype(jnp.bfloat16), preferred_element_type=jnp.float32
    ).astype(jnp.bfloat16)
    allowed = lax.dot_general(
        src_allowed, tgt_hot, (((1,), (1,)), ((), ())), preferred_element_type=jnp.float32
    )
    shifted = cost.astype(jnp.float32) + PENALTY * (1.0 - allowed)
    col_duals = [g_start]
    row_duals = []
    for section in range(K):
        row_scores = (col_duals[-1][None, :] - shifted) / EPSILON
        row_duals.append(EPSILON * log_source - EPSILON * log_total(row_scores, 1, "cols"))
        scores = (row_duals[-1][:, None] - shifted) / EPSILON
        col_duals.append(EPSILON * log_target - EPSILON * log_total(scores, 0, "rows"))
    cost_grad = jnp.zeros_like(shifted)
    col_grad = g_bar
    for section in reversed(range(K)):
        row_now = row_duals[section]
        outer = f_bar if section == K - 1 else jnp.zeros_like(f_bar)
        plan_q = jnp.exp(
            (row_now[:, None] + col_duals[section + 1][None, :] - shifted) / EPSILON - log_target
        )
        partial_value = jnp.sum(plan_q * col_grad[None, :], axis=1)
        row_grad = outer - total(partial_value, "cols")
        plan_r = jnp.exp(
            (row_now[:, None] + col_duals[section][None, :] - shifted) / EPSILON - log_source
        )
        next_partial = jnp.sum(plan_r * row_grad[:, None], axis=0)
        cost_grad = cost_grad + plan_q * col_grad[None, :] + plan_r * row_grad[:, None]
        if section:
            col_grad = -total(next_partial, "rows")
    rounded = cost_grad.astype(jnp.bfloat16)
    x_count, z_count = 4, row_count // 4
    owned = width // row_count
    src_ordered = src_emb.reshape(src_rows, x_count, z_count, owned).transpose(0, 2, 1, 3)
    along_z = [[x * z_count + z for z in range(z_count)] for x in range(x_count)]
    along_x = [[x * z_count + z for x in range(x_count)] for z in range(z_count)]
    y_part = -lax.dot_general(
        src_ordered.reshape(src_rows, width),
        rounded,
        (((0,), (0,)), ((), ())),
        preferred_element_type=jnp.float32,
    )
    y_part = lax.psum_scatter(
        y_part, "rows", scatter_dimension=0, tiled=True, axis_index_groups=along_z
    )
    x_part = -lax.dot_general(
        tgt_emb, rounded, (((0,), (1,)), ((), ())), preferred_element_type=jnp.float32
    )
    x_blocks = lax.all_to_all(
        x_part.reshape(col_count, width // col_count, src_rows), "cols", 0, 0, tiled=True
    )
    grad_x = jnp.sum(x_blocks, axis=0)
    g_start_bar = -total(next_partial, "rows")
    y_blocks = lax.all_to_all(
        y_part.reshape(x_count, owned, tgt_cols), "rows", 0, 0, tiled=True, axis_index_groups=along_x
    )
    grad_y = jnp.sum(y_blocks, axis=0)
    return (g_start_bar, grad_x, grad_y)


def solution(mesh):
    placed = (
        P("rows", "cols"),
        P("rows"),
        P("cols"),
        P(),
        P("cols"),
        P("rows"),
        P("cols"),
        P("rows", None),
        P("cols", None),
    )
    return jax.shard_map(
        body,
        mesh=mesh,
        in_specs=placed,
        out_specs=(P("cols"), P("cols", "rows"), P("rows", "cols")),
        check_vma=False,
    )
```

```python
import functools
import math

import jax
import jax.numpy as jnp
from jax import lax
from jax.experimental import pallas as pl
from jax.experimental.pallas import tpu as pltpu
from jax.sharding import PartitionSpec as P

K = 3


EPSILON = 0.05
PENALTY = 1.0
SCALE = 1.0 / (EPSILON * math.log(2.0))
LANES = 128
STRIP = 32
REACH = 40.0
VMEM_BYTES = 40 * 2**20
F32 = jnp.float32


def eye():
    return lax.broadcasted_iota(jnp.int32, (LANES, LANES), 0) == lax.broadcasted_iota(
        jnp.int32, (LANES, LANES), 1
    )


def to_column(row):
    return jnp.sum(jnp.where(eye(), row, 0.0), axis=1, keepdims=True)


def to_row(column):
    return jnp.sum(jnp.where(eye(), column, 0.0), axis=0, keepdims=True)


def log_combined(parts):
    top = jnp.max(parts, axis=0)
    return top + jnp.log2(jnp.sum(jnp.exp2(parts - top[None]), axis=0))


def spread(copies_ref, value):
    copies_ref[...] = jnp.broadcast_to(value[None], copies_ref.shape)


def groups_of(ref):
    return ref.shape[0]


def row_sums(base_ref, weight_ref, out_ref):
    for s in range(groups_of(out_ref)):
        held = None
        for c in range(groups_of(weight_ref)):
            tile = base_ref[s * LANES : (s + 1) * LANES, c * LANES : (c + 1) * LANES]
            term = tile * weight_ref[c : c + 1, :]
            held = term if held is None else held + term
        out_ref[s : s + 1, :] = to_row(jnp.sum(held, axis=1, keepdims=True))


def col_sums(base_ref, weight_ref, out_ref):
    held = [None] * groups_of(out_ref)
    for s in range(groups_of(weight_ref)):
        column = jnp.broadcast_to(to_column(weight_ref[s : s + 1, :]), (LANES, LANES))
        for c in range(len(held)):
            tile = base_ref[s * LANES : (s + 1) * LANES, c * LANES : (c + 1) * LANES]
            term = jnp.sum((tile * column).reshape(LANES // 8, 8, LANES), axis=0)
            held[c] = term if held[c] is None else held[c] + term
    for c, term in enumerate(held):
        out_ref[c : c + 1, :] = jnp.sum(term, axis=0, keepdims=True)


def strip_logs(scores):
    highest = jnp.max(scores, axis=1, keepdims=True)
    powers = jnp.exp2(scores - highest)
    return highest, powers, highest + jnp.log2(jnp.sum(powers, axis=1, keepdims=True))


def wide(ref):
    return jnp.concatenate([ref[c : c + 1, :] for c in range(groups_of(ref))], axis=1)


def load_rows(score_hbm, tile_ref, sem, group):
    copy = pltpu.make_async_copy(
        score_hbm.at[pl.ds(pl.multiple_of(group * LANES, LANES), LANES), :], tile_ref, sem
    )
    copy.start()
    copy.wait()


def slow_row_logs(score_hbm, tile_ref, sem, col_ref, out_ref):
    @pl.loop(0, groups_of(out_ref))
    def _(group):
        load_rows(score_hbm, tile_ref, sem, group)
        logs = []
        for q in range(LANES // STRIP):
            logs.append(strip_logs(tile_ref[q * STRIP : (q + 1) * STRIP, :] + wide(col_ref))[2])
        out_ref[pl.ds(group, 1), :] = to_row(jnp.concatenate(logs, axis=0))


def slow_col_logs(score_hbm, tile_ref, sem, row_ref, out_ref):
    count = groups_of(out_ref)
    tops = tuple(jnp.full((1, LANES), -1e30, F32) for _ in range(count))

    def highest(group, tops):
        load_rows(score_hbm, tile_ref, sem, group)
        column = to_column(row_ref[pl.ds(group, 1), :])
        return tuple(
            jnp.maximum(
                tops[c],
                jnp.max(
                    tile_ref[:, c * LANES : (c + 1) * LANES] + column, axis=0, keepdims=True
                ),
            )
            for c in range(count)
        )

    tops = lax.fori_loop(0, groups_of(row_ref), highest, tops)
    sums = tuple(jnp.zeros((1, LANES), F32) for _ in range(count))

    def summed(group, sums):
        load_rows(score_hbm, tile_ref, sem, group)
        column = to_column(row_ref[pl.ds(group, 1), :])
        return tuple(
            sums[c]
            + jnp.sum(
                jnp.exp2(tile_ref[:, c * LANES : (c + 1) * LANES] + column - tops[c]),
                axis=0,
                keepdims=True,
            )
            for c in range(count)
        )

    sums = lax.fori_loop(0, groups_of(row_ref), summed, sums)
    for c in range(count):
        out_ref[c : c + 1, :] = tops[c] + jnp.log2(sums[c])


def slow_row_weighted(score_hbm, tile_ref, sem, row_ref, col_ref, weight_ref, out_ref):
    @pl.loop(0, groups_of(out_ref))
    def _(group):
        load_rows(score_hbm, tile_ref, sem, group)
        column = to_column(row_ref[pl.ds(group, 1), :])
        sums = []
        for q in range(LANES // STRIP):
            part = slice(q * STRIP, (q + 1) * STRIP)
            plan = jnp.exp2(tile_ref[part, :] + column[part] + wide(col_ref))
            sums.append(jnp.sum(plan * wide(weight_ref), axis=1, keepdims=True))
        out_ref[pl.ds(group, 1), :] = to_row(jnp.concatenate(sums, axis=0))


def slow_col_weighted(score_hbm, tile_ref, sem, row_ref, col_ref, weight_ref, out_ref):
    count = groups_of(out_ref)
    sums = tuple(jnp.zeros((1, LANES), F32) for _ in range(count))

    def summed(group, sums):
        load_rows(score_hbm, tile_ref, sem, group)
        column = to_column(row_ref[pl.ds(group, 1), :])
        weight = to_column(weight_ref[pl.ds(group, 1), :])
        return tuple(
            sums[c]
            + jnp.sum(
                weight
                * jnp.exp2(
                    tile_ref[:, c * LANES : (c + 1) * LANES] + column + col_ref[c : c + 1, :]
                ),
                axis=0,
                keepdims=True,
            )
            for c in range(count)
        )

    sums = lax.fori_loop(0, groups_of(row_ref), summed, sums)
    for c in range(count):
        out_ref[c : c + 1, :] = sums[c]


def first_kernel(
    cost_ref, src_ref, tgt_ref, mask_ref, dual_ref, score_ref, base_ref, top_ref, copies_ref,
    allowed_ref, log_ref,
):
    classes = mask_ref.shape[0]
    mask = mask_ref[...].astype(F32).astype(jnp.bfloat16)
    ids = lax.broadcasted_iota(jnp.int32, (classes, LANES), 0)
    hot = jnp.concatenate(
        [
            jnp.where(tgt_ref[c : c + 1, :] == ids, 1.0, 0.0).astype(jnp.bfloat16)
            for c in range(groups_of(tgt_ref))
        ],
        axis=1,
    )
    allowed_of = jnp.dot(mask, hot, preferred_element_type=F32).astype(jnp.bfloat16)
    lane_ids = lax.broadcasted_iota(jnp.int32, (LANES, classes), 1).astype(F32)
    dual = wide(dual_ref) - PENALTY * SCALE
    for s in range(groups_of(log_ref)):
        label = to_column(src_ref[s : s + 1, :].astype(F32))
        src_hot = jnp.where(label == lane_ids, 1.0, 0.0).astype(jnp.bfloat16)
        allowed_ref[...] = jnp.dot(src_hot, allowed_of, preferred_element_type=F32)
        tops, logs = [], []
        for q in range(LANES // STRIP):
            rows = slice(s * LANES + q * STRIP, s * LANES + (q + 1) * STRIP)
            shifted = cost_ref[rows, :].astype(F32) - PENALTY * allowed_ref[
                q * STRIP : (q + 1) * STRIP, :
            ]
            scores = dual - shifted * SCALE
            highest, powers, log = strip_logs(scores)
            score_ref[rows, :] = scores
            base_ref[rows, :] = powers
            tops.append(highest)
            logs.append(log)
        top_ref[s : s + 1, :] = to_row(jnp.concatenate(tops, axis=0))
        log_ref[s : s + 1, :] = to_row(jnp.concatenate(logs, axis=0))
    spread(copies_ref, log_ref[...])


def rebase_kernel(
    log_target, parts_ref, score_ref, base_ref, top_ref, dual_ref, copies_ref, log_ref
):
    dual_ref[...] = log_target - log_combined(parts_ref[...])
    dual = wide(dual_ref)
    for s in range(groups_of(log_ref)):
        tops, logs = [], []
        for q in range(LANES // STRIP):
            rows = slice(s * LANES + q * STRIP, s * LANES + (q + 1) * STRIP)
            highest, powers, log = strip_logs(score_ref[rows, :] + dual)
            base_ref[rows, :] = powers
            tops.append(highest)
            logs.append(log)
        top_ref[s : s + 1, :] = to_row(jnp.concatenate(tops, axis=0))
        log_ref[s : s + 1, :] = to_row(jnp.concatenate(logs, axis=0))
    spread(copies_ref, log_ref[...])


def row_log_kernel(
    log_target, parts_ref, top_ref, base_dual_ref, base_ref, score_hbm, dual_ref, copies_ref,
    weight_ref, sum_ref, tile_ref, sem,
):
    dual_ref[...] = log_target - log_combined(parts_ref[...])
    lead = dual_ref[...] - base_dual_ref[...]
    near = jnp.max(jnp.abs(lead)) <= REACH

    @pl.when(near)
    def _():
        weight_ref[...] = jnp.exp2(lead)
        row_sums(base_ref, weight_ref, sum_ref)
        sum_ref[...] = top_ref[...] + jnp.log2(sum_ref[...])

    @pl.when(jnp.logical_not(near))
    def _():
        slow_row_logs(score_hbm, tile_ref, sem, dual_ref, sum_ref)

    spread(copies_ref, sum_ref[...])


def col_log_kernel(
    log_source, parts_ref, top_ref, base_dual_ref, base_ref, score_hbm, dual_ref, copies_ref,
    weight_ref, sum_ref, tile_ref, sem,
):
    dual_ref[...] = log_source - log_combined(parts_ref[...])
    lead = dual_ref[...] + top_ref[...]
    weight_ref[...] = jnp.exp2(jnp.minimum(lead, 100.0))
    col_sums(base_ref, weight_ref, sum_ref)
    most = jnp.max(lead)
    near = jnp.logical_and(
        most <= 60.0,
        jnp.min(jnp.log2(jnp.maximum(sum_ref[...], 1e-37))) >= jnp.maximum(most, -15.0) - 85.0,
    )

    @pl.when(near)
    def _():
        sum_ref[...] = jnp.log2(sum_ref[...]) - base_dual_ref[...]

    @pl.when(jnp.logical_not(near))
    def _():
        slow_col_logs(score_hbm, tile_ref, sem, dual_ref, sum_ref)

    spread(copies_ref, sum_ref[...])


def row_plan_kernel(
    log_target, first, parts_ref, grad_ref, dual_in_ref, row_dual_ref, top_ref, base_dual_ref,
    base_ref, score_hbm, out_ref, copies_ref, weight_ref, col_ref, sum_ref, tile_ref, sem,
):
    if first:
        dual = log_target - log_combined(parts_ref[...])
        grad = grad_ref[...]
        out_ref[...] = dual
    else:
        dual = dual_in_ref[...]
        grad = -jnp.sum(parts_ref[...], axis=0)
        out_ref[...] = grad
    lead = dual - base_dual_ref[...]
    row_lead = row_dual_ref[...] + top_ref[...]
    near = jnp.logical_and(jnp.max(jnp.abs(lead)) <= REACH, jnp.max(row_lead) <= 60.0)

    @pl.when(near)
    def _():
        weight_ref[...] = jnp.exp2(lead - log_target) * grad
        row_sums(base_ref, weight_ref, sum_ref)
        sum_ref[...] = sum_ref[...] * jnp.exp2(row_lead)

    @pl.when(jnp.logical_not(near))
    def _():
        col_ref[...] = dual - log_target
        weight_ref[...] = grad
        slow_row_weighted(score_hbm, tile_ref, sem, row_dual_ref, col_ref, weight_ref, sum_ref)

    spread(copies_ref, sum_ref[...])


def col_plan_kernel(
    log_source, parts_ref, outer_ref, dual_ref, row_dual_ref, top_ref, base_dual_ref, base_ref,
    score_hbm, out_ref, copies_ref, weight_ref, col_ref, sum_ref, tile_ref, sem,
):
    grad = outer_ref[...] - jnp.sum(parts_ref[...], axis=0)
    out_ref[...] = grad
    lead = dual_ref[...] - base_dual_ref[...]
    row_lead = row_dual_ref[...] + top_ref[...]
    near = jnp.logical_and(jnp.max(jnp.abs(lead)) <= REACH, jnp.max(row_lead) <= 60.0)

    @pl.when(near)
    def _():
        weight_ref[...] = jnp.exp2(row_lead) * grad
        col_sums(base_ref, weight_ref, sum_ref)
        sum_ref[...] = sum_ref[...] * jnp.exp2(lead - log_source)

    @pl.when(jnp.logical_not(near))
    def _():
        col_ref[...] = dual_ref[...] - log_source
        weight_ref[...] = grad
        slow_col_weighted(score_hbm, tile_ref, sem, row_dual_ref, col_ref, weight_ref, sum_ref)

    spread(copies_ref, sum_ref[...])


def grad_kernel(
    log_source, log_target,
    parts_ref, row1, row2, row3, col1, col2, col3, fbar2, fbar3, gbar1, gbar2, gbar3,
    start_top_ref, top_ref, start_base_ref, base_ref, score_hbm, out_ref,
    rows_ref, cols_ref, tile_ref, sem,
):
    fbar1 = -jnp.sum(parts_ref[...], axis=0)
    leads = [col2[...] - col1[...], col3[...] - col1[...]]
    row_leads = [ref[...] + top_ref[...] for ref in (row1, row2, row3)]
    near = jnp.logical_and(
        jnp.maximum(jnp.max(jnp.abs(leads[0])), jnp.max(jnp.abs(leads[1]))) <= REACH,
        jnp.max(row_leads[2]) <= 60.0,
    )
    count = groups_of(col1)

    @pl.when(near)
    def _():
        rows_ref[0] = -jnp.exp2(row1[...] + start_top_ref[...] - log_source) * fbar1
        rows_ref[1] = -jnp.exp2(row_leads[0])
        rows_ref[2] = -jnp.exp2(row_leads[1])
        rows_ref[3] = -jnp.exp2(row_leads[2])
        rows_ref[4] = rows_ref[2] * fbar2[...]
        rows_ref[5] = rows_ref[3] * fbar3[...]
        cols_ref[1] = jnp.exp2(jnp.full_like(leads[0], -log_target)) * gbar1[...]
        cols_ref[2] = jnp.exp2(leads[0] - log_target) * gbar2[...]
        cols_ref[3] = jnp.exp2(leads[1] - log_target) * gbar3[...]
        cols_ref[4] = jnp.exp2(jnp.full_like(leads[0], -log_source))
        cols_ref[5] = jnp.exp2(leads[0] - log_source)
        for s in range(groups_of(row1)):
            columns = [to_column(rows_ref[k, s : s + 1, :]) for k in range(6)]
            for q in range(LANES // STRIP):
                rows = slice(s * LANES + q * STRIP, s * LANES + (q + 1) * STRIP)
                strips = [
                    jnp.broadcast_to(part[q * STRIP : (q + 1) * STRIP], (STRIP, LANES))
                    for part in columns
                ]
                for c in range(count):
                    lanes = slice(c * LANES, (c + 1) * LANES)
                    weight = strips[1] * cols_ref[1, c : c + 1, :]
                    for k in range(2, 6):
                        weight = weight + strips[k] * cols_ref[k, c : c + 1, :]
                    value = base_ref[rows, lanes] * weight + start_base_ref[rows, lanes] * strips[0]
                    out_ref[rows, lanes] = value.astype(jnp.bfloat16)

    @pl.when(jnp.logical_not(near))
    def _():
        zero = jnp.zeros_like(fbar1)
        for k, (row, value) in enumerate(((row1, fbar1), (row2, fbar2[...]), (row3, fbar3[...]))):
            rows_ref[k] = row[...]
            rows_ref[3 + k] = value
        for k, (col, value) in enumerate(
            ((zero, None), (col1[...], gbar1), (col2[...], gbar2), (col3[...], gbar3))
        ):
            cols_ref[k] = col
            if value is not None:
                cols_ref[3 + k] = value[...]

        @pl.loop(0, groups_of(row1))
        def _(group):
            load_rows(score_hbm, tile_ref, sem, group)
            columns = [to_column(rows_ref[k, pl.ds(group, 1), :]) for k in range(6)]
            for c in range(count):
                lanes = slice(c * LANES, (c + 1) * LANES)
                value = jnp.zeros((LANES, LANES), F32)
                for k in reversed(range(3)):
                    scores = tile_ref[:, lanes] + columns[k]
                    plan_q = jnp.exp2(scores + (cols_ref[k + 1, c : c + 1, :] - log_target))
                    plan_r = jnp.exp2(scores + (cols_ref[k, c : c + 1, :] - log_source))
                    value = value + plan_q * cols_ref[4 + k, c : c + 1, :]
                    value = value + plan_r * columns[3 + k]
                start = pl.multiple_of(group * LANES, LANES)
                out_ref[pl.ds(start, LANES), lanes] = (-value).astype(jnp.bfloat16)


def call(kernel, arguments, outs, scratch=(), in_hbm=(), flops=0, name=None):
    specs = [
        pl.BlockSpec(memory_space=pl.ANY if at in in_hbm else pltpu.VMEM)
        for at in range(len(arguments))
    ]
    return pl.pallas_call(
        kernel,
        out_shape=outs,
        in_specs=specs,
        out_specs=[pl.BlockSpec(memory_space=pltpu.VMEM)] * len(outs),
        scratch_shapes=list(scratch),
        compiler_params=pltpu.CompilerParams(vmem_limit_bytes=VMEM_BYTES),
        name=name,
    )(*arguments)


def exchanged(copies, axis):
    return lax.all_to_all(copies, axis, 0, 0, tiled=True)


def body(cost, src_label, tgt_label, class_mask, g_start, f_bar, g_bar, src_emb, tgt_emb):
    row_count = lax.axis_size("rows")
    col_count = lax.axis_size("cols")
    src_rows, tgt_cols = cost.shape
    width = src_emb.shape[1]
    log_source = -math.log2(src_rows * row_count)
    log_target = -math.log2(tgt_cols * col_count)
    row_shape = (src_rows // LANES, LANES)
    col_shape = (tgt_cols // LANES, LANES)
    src_label, f_bar = src_label.reshape(row_shape), f_bar.reshape(row_shape)
    tgt_label, g_bar = tgt_label.reshape(col_shape), g_bar.reshape(col_shape)
    g_start = (g_start * SCALE).reshape(col_shape)

    def array(shape, dtype=F32):
        return jax.ShapeDtypeStruct(shape, dtype)

    matrix = array(cost.shape)
    row_vector, col_vector = array(row_shape), array(col_shape)
    row_copies = array((col_count,) + row_shape)
    col_copies = array((row_count,) + col_shape)
    row_held, col_held = pltpu.VMEM(row_shape, F32), pltpu.VMEM(col_shape, F32)
    slow = [pltpu.VMEM((LANES, tgt_cols), F32), pltpu.SemaphoreType.DMA]

    score, start_base, start_top, copies = call(
        first_kernel,
        (cost, src_label, tgt_label, class_mask, g_start),
        [matrix, matrix, row_vector, row_copies],
        [pltpu.VMEM((LANES, tgt_cols), F32), row_held],
        name="first_row_logs",
    )

    def col_logs(parts, top, base_dual, base):
        return call(
            functools.partial(col_log_kernel, log_source),
            (parts, top, base_dual, base, score),
            [row_vector, col_copies],
            [row_held, col_held] + slow,
            in_hbm=(4,),
            name="col_logs",
        )

    zero = jnp.zeros(col_shape, F32)
    row1, copies = col_logs(exchanged(copies, "cols"), start_top, zero, start_base)
    base, top, col1, copies = call(
        functools.partial(rebase_kernel, log_target),
        (exchanged(copies, "rows"), score),
        [matrix, row_vector, col_vector, row_copies],
        [row_held],
        name="second_row_logs",
    )
    row2, copies = col_logs(exchanged(copies, "cols"), top, col1, base)
    col2, copies = call(
        functools.partial(row_log_kernel, log_target),
        (exchanged(copies, "rows"), top, col1, base, score),
        [col_vector, row_copies],
        [col_held, row_held] + slow,
        in_hbm=(4,),
        name="third_row_logs",
    )
    row3, copies = col_logs(exchanged(copies, "cols"), top, col1, base)

    def row_plan(first, parts, grad, dual, row):
        return call(
            functools.partial(row_plan_kernel, log_target, first),
            (parts, grad, dual, row, top, col1, base, score),
            [col_vector, row_copies],
            [col_held, col_held, row_held] + slow,
            in_hbm=(7,),
            name="row_plan",
        )

    def col_plan(parts, outer, dual, row, top, base_dual, base):
        return call(
            functools.partial(col_plan_kernel, log_source),
            (parts, outer, dual, row, top, base_dual, base, score),
            [row_vector, col_copies],
            [row_held, col_held, col_held] + slow,
            in_hbm=(7,),
            name="col_plan",
        )

    none = jnp.zeros(row_shape, F32)
    col3, copies = row_plan(True, exchanged(copies, "rows"), g_bar, col2, row3)
    fbar3, copies = col_plan(exchanged(copies, "cols"), f_bar, col2, row3, top, col1, base)
    gbar2, copies = row_plan(False, exchanged(copies, "rows"), g_bar, col2, row2)
    fbar2, copies = col_plan(exchanged(copies, "cols"), none, col1, row2, top, col1, base)
    gbar1, copies = row_plan(False, exchanged(copies, "rows"), g_bar, col1, row1)
    parts = exchanged(copies, "cols")
    (rounded,) = call(
        functools.partial(grad_kernel, log_source, log_target),
        (
            parts, row1, row2, row3, col1, col2, col3, fbar2, fbar3, gbar1, gbar2, g_bar,
            start_top, top, start_base, base, score,
        ),
        [array(cost.shape, jnp.bfloat16)],
        [pltpu.VMEM((6,) + row_shape, F32), pltpu.VMEM((7,) + col_shape, F32)] + slow,
        in_hbm=(16,),
        name="cost_grad",
    )
    x_count, z_count = 4, row_count // 4
    owned = width // row_count
    src_ordered = src_emb.reshape(src_rows, x_count, z_count, owned).transpose(0, 2, 1, 3)
    along_z = [[x * z_count + z for z in range(z_count)] for x in range(x_count)]
    along_x = [[x * z_count + z for x in range(x_count)] for z in range(z_count)]
    y_part = lax.dot_general(
        src_ordered.reshape(src_rows, width),
        rounded,
        (((0,), (0,)), ((), ())),
        preferred_element_type=F32,
    )
    y_part = lax.psum_scatter(
        y_part, "rows", scatter_dimension=0, tiled=True, axis_index_groups=along_z
    )
    x_part = lax.dot_general(
        tgt_emb, rounded, (((0,), (1,)), ((), ())), preferred_element_type=F32
    )
    x_blocks = lax.all_to_all(
        x_part.reshape(col_count, width // col_count, src_rows), "cols", 0, 0, tiled=True
    )
    grad_x = jnp.sum(x_blocks, axis=0)
    fbar1, copies = col_plan(parts, none, zero, row1, start_top, zero, start_base)
    g_start_bar = -jnp.sum(exchanged(copies, "rows"), axis=0).reshape(tgt_cols)
    y_blocks = lax.all_to_all(
        y_part.reshape(x_count, owned, tgt_cols), "rows", 0, 0, tiled=True, axis_index_groups=along_x
    )
    grad_y = jnp.sum(y_blocks, axis=0)
    return (g_start_bar, grad_x, grad_y)


def solution(mesh):
    placed = (
        P("rows", "cols"),
        P("rows"),
        P("cols"),
        P(),
        P("cols"),
        P("rows"),
        P("cols"),
        P("rows", None),
        P("cols", None),
    )
    return jax.shard_map(
        body,
        mesh=mesh,
        in_specs=placed,
        out_specs=(P("cols"), P("cols", "rows"), P("rows", "cols")),
        check_vma=False,
    )
```

```python
import functools
import math

import jax
import jax.numpy as jnp
from jax import lax
from jax.experimental import pallas as pl
from jax.experimental.pallas import tpu as pltpu
from jax.sharding import PartitionSpec as P

K = 3


EPSILON = 0.05
PENALTY = 1.0
SCALE = 1.0 / (EPSILON * math.log(2.0))
LANES = 128
STRIP = 32
REACH = 40.0
VMEM_BYTES = 16 * 2**20
F32 = jnp.float32


def eye():
    return lax.broadcasted_iota(jnp.int32, (LANES, LANES), 0) == lax.broadcasted_iota(
        jnp.int32, (LANES, LANES), 1
    )


def to_column(row):
    return jnp.sum(jnp.where(eye(), row, 0.0), axis=1, keepdims=True)


def to_row(column):
    return jnp.sum(jnp.where(eye(), column, 0.0), axis=0, keepdims=True)


def log_combined(parts):
    top = jnp.max(parts, axis=0)
    return top + jnp.log2(jnp.sum(jnp.exp2(parts - top[None]), axis=0))


def spread(copies_ref, value):
    copies_ref[...] = jnp.broadcast_to(value[None], copies_ref.shape)


def groups_of(ref):
    return ref.shape[0]


def row_sums(base_ref, weight_ref, out_ref):
    for s in range(groups_of(out_ref)):
        held = None
        for c in range(groups_of(weight_ref)):
            tile = base_ref[s * LANES : (s + 1) * LANES, c * LANES : (c + 1) * LANES]
            term = tile * weight_ref[c : c + 1, :]
            held = term if held is None else held + term
        out_ref[s : s + 1, :] = to_row(jnp.sum(held, axis=1, keepdims=True))


def col_sums(base_ref, weight_ref, out_ref):
    held = [None] * groups_of(out_ref)
    for s in range(groups_of(weight_ref)):
        column = jnp.broadcast_to(to_column(weight_ref[s : s + 1, :]), (LANES, LANES))
        for c in range(len(held)):
            tile = base_ref[s * LANES : (s + 1) * LANES, c * LANES : (c + 1) * LANES]
            term = jnp.sum((tile * column).reshape(LANES // 8, 8, LANES), axis=0)
            held[c] = term if held[c] is None else held[c] + term
    for c, term in enumerate(held):
        out_ref[c : c + 1, :] = jnp.sum(term, axis=0, keepdims=True)


def strip_logs(scores):
    highest = jnp.max(scores, axis=1, keepdims=True)
    powers = jnp.exp2(scores - highest)
    return highest, powers, highest + jnp.log2(jnp.sum(powers, axis=1, keepdims=True))


def wide(ref):
    return jnp.concatenate([ref[c : c + 1, :] for c in range(groups_of(ref))], axis=1)


def load_rows(score_hbm, tile_ref, sem, group):
    copy = pltpu.make_async_copy(
        score_hbm.at[pl.ds(pl.multiple_of(group * LANES, LANES), LANES), :], tile_ref, sem
    )
    copy.start()
    copy.wait()


def slow_row_logs(score_hbm, tile_ref, sem, col_ref, out_ref):
    @pl.loop(0, groups_of(out_ref))
    def _(group):
        load_rows(score_hbm, tile_ref, sem, group)
        logs = []
        for q in range(LANES // STRIP):
            logs.append(strip_logs(tile_ref[q * STRIP : (q + 1) * STRIP, :] + wide(col_ref))[2])
        out_ref[pl.ds(group, 1), :] = to_row(jnp.concatenate(logs, axis=0))


def slow_col_logs(score_hbm, tile_ref, sem, row_ref, out_ref):
    count = groups_of(out_ref)
    tops = tuple(jnp.full((1, LANES), -1e30, F32) for _ in range(count))

    def highest(group, tops):
        load_rows(score_hbm, tile_ref, sem, group)
        column = to_column(row_ref[pl.ds(group, 1), :])
        return tuple(
            jnp.maximum(
                tops[c],
                jnp.max(
                    tile_ref[:, c * LANES : (c + 1) * LANES] + column, axis=0, keepdims=True
                ),
            )
            for c in range(count)
        )

    tops = lax.fori_loop(0, groups_of(row_ref), highest, tops)
    sums = tuple(jnp.zeros((1, LANES), F32) for _ in range(count))

    def summed(group, sums):
        load_rows(score_hbm, tile_ref, sem, group)
        column = to_column(row_ref[pl.ds(group, 1), :])
        return tuple(
            sums[c]
            + jnp.sum(
                jnp.exp2(tile_ref[:, c * LANES : (c + 1) * LANES] + column - tops[c]),
                axis=0,
                keepdims=True,
            )
            for c in range(count)
        )

    sums = lax.fori_loop(0, groups_of(row_ref), summed, sums)
    for c in range(count):
        out_ref[c : c + 1, :] = tops[c] + jnp.log2(sums[c])


def slow_row_weighted(score_hbm, tile_ref, sem, row_ref, col_ref, weight_ref, out_ref):
    @pl.loop(0, groups_of(out_ref))
    def _(group):
        load_rows(score_hbm, tile_ref, sem, group)
        column = to_column(row_ref[pl.ds(group, 1), :])
        sums = []
        for q in range(LANES // STRIP):
            part = slice(q * STRIP, (q + 1) * STRIP)
            plan = jnp.exp2(tile_ref[part, :] + column[part] + wide(col_ref))
            sums.append(jnp.sum(plan * wide(weight_ref), axis=1, keepdims=True))
        out_ref[pl.ds(group, 1), :] = to_row(jnp.concatenate(sums, axis=0))


def slow_col_weighted(score_hbm, tile_ref, sem, row_ref, col_ref, weight_ref, out_ref):
    count = groups_of(out_ref)
    sums = tuple(jnp.zeros((1, LANES), F32) for _ in range(count))

    def summed(group, sums):
        load_rows(score_hbm, tile_ref, sem, group)
        column = to_column(row_ref[pl.ds(group, 1), :])
        weight = to_column(weight_ref[pl.ds(group, 1), :])
        return tuple(
            sums[c]
            + jnp.sum(
                weight
                * jnp.exp2(
                    tile_ref[:, c * LANES : (c + 1) * LANES] + column + col_ref[c : c + 1, :]
                ),
                axis=0,
                keepdims=True,
            )
            for c in range(count)
        )

    sums = lax.fori_loop(0, groups_of(row_ref), summed, sums)
    for c in range(count):
        out_ref[c : c + 1, :] = sums[c]


def first_kernel(
    cost_hbm, src_hbm, tgt_hbm, mask_hbm, dual_hbm, score_ref, base_ref, top_ref, copies_ref,
    cost_ref, src_ref, tgt_ref, mask_ref, dual_ref, allowed_ref, log_ref, small_sem, cost_sem,
):
    small = [
        pltpu.make_async_copy(source, target, small_sem.at[at])
        for at, (source, target) in enumerate(
            ((tgt_hbm, tgt_ref), (mask_hbm, mask_ref), (src_hbm, src_ref), (dual_hbm, dual_ref))
        )
    ]
    for copy in small:
        copy.start()
    blocks = []
    for s in range(groups_of(log_ref)):
        rows = pl.ds(s * LANES, LANES)
        blocks.append(
            pltpu.make_async_copy(cost_hbm.at[rows, :], cost_ref.at[rows, :], cost_sem.at[s])
        )
        blocks[-1].start()
    for copy in small:
        copy.wait()
    classes = mask_ref.shape[0]
    mask = mask_ref[...].astype(F32).astype(jnp.bfloat16)
    ids = lax.broadcasted_iota(jnp.int32, (classes, LANES), 0)
    hot = jnp.concatenate(
        [
            jnp.where(tgt_ref[c : c + 1, :] == ids, 1.0, 0.0).astype(jnp.bfloat16)
            for c in range(groups_of(tgt_ref))
        ],
        axis=1,
    )
    allowed_of = jnp.dot(mask, hot, preferred_element_type=F32).astype(jnp.bfloat16)
    lane_ids = lax.broadcasted_iota(jnp.int32, (LANES, classes), 1).astype(F32)
    dual = wide(dual_ref) * SCALE - PENALTY * SCALE
    for s in range(groups_of(log_ref)):
        label = to_column(src_ref[s : s + 1, :].astype(F32))
        src_hot = jnp.where(label == lane_ids, 1.0, 0.0).astype(jnp.bfloat16)
        allowed_ref[...] = jnp.dot(src_hot, allowed_of, preferred_element_type=F32)
        blocks[s].wait()
        tops, logs = [], []
        for q in range(LANES // STRIP):
            rows = slice(s * LANES + q * STRIP, s * LANES + (q + 1) * STRIP)
            shifted = cost_ref[rows, :].astype(F32) - PENALTY * allowed_ref[
                q * STRIP : (q + 1) * STRIP, :
            ]
            scores = dual - shifted * SCALE
            highest, powers, log = strip_logs(scores)
            score_ref[rows, :] = scores
            base_ref[rows, :] = powers
            tops.append(highest)
            logs.append(log)
        top_ref[s : s + 1, :] = to_row(jnp.concatenate(tops, axis=0))
        log_ref[s : s + 1, :] = to_row(jnp.concatenate(logs, axis=0))
    spread(copies_ref, log_ref[...])


def rebase_kernel(
    log_target, parts_ref, score_ref, base_ref, top_ref, dual_ref, copies_ref, log_ref
):
    dual_ref[...] = log_target - log_combined(parts_ref[...])
    dual = wide(dual_ref)
    for s in range(groups_of(log_ref)):
        tops, logs = [], []
        for q in range(LANES // STRIP):
            rows = slice(s * LANES + q * STRIP, s * LANES + (q + 1) * STRIP)
            highest, powers, log = strip_logs(score_ref[rows, :] + dual)
            base_ref[rows, :] = powers
            tops.append(highest)
            logs.append(log)
        top_ref[s : s + 1, :] = to_row(jnp.concatenate(tops, axis=0))
        log_ref[s : s + 1, :] = to_row(jnp.concatenate(logs, axis=0))
    spread(copies_ref, log_ref[...])


def row_log_kernel(
    log_target, parts_ref, top_ref, base_dual_ref, base_ref, score_hbm, dual_ref, copies_ref,
    weight_ref, sum_ref, tile_ref, sem,
):
    dual_ref[...] = log_target - log_combined(parts_ref[...])
    lead = dual_ref[...] - base_dual_ref[...]
    near = jnp.max(jnp.abs(lead)) <= REACH

    @pl.when(near)
    def _():
        weight_ref[...] = jnp.exp2(lead)
        row_sums(base_ref, weight_ref, sum_ref)
        sum_ref[...] = top_ref[...] + jnp.log2(sum_ref[...])

    @pl.when(jnp.logical_not(near))
    def _():
        slow_row_logs(score_hbm, tile_ref, sem, dual_ref, sum_ref)

    spread(copies_ref, sum_ref[...])


def col_log_kernel(
    log_source, parts_ref, top_ref, base_dual_ref, base_ref, score_hbm, dual_ref, copies_ref,
    weight_ref, sum_ref, tile_ref, sem,
):
    dual_ref[...] = log_source - log_combined(parts_ref[...])
    lead = dual_ref[...] + top_ref[...]
    weight_ref[...] = jnp.exp2(jnp.minimum(lead, 100.0))
    col_sums(base_ref, weight_ref, sum_ref)
    most = jnp.max(lead)
    near = jnp.logical_and(
        most <= 60.0,
        jnp.min(jnp.log2(jnp.maximum(sum_ref[...], 1e-37))) >= jnp.maximum(most, -15.0) - 85.0,
    )

    @pl.when(near)
    def _():
        sum_ref[...] = jnp.log2(sum_ref[...]) - base_dual_ref[...]

    @pl.when(jnp.logical_not(near))
    def _():
        slow_col_logs(score_hbm, tile_ref, sem, dual_ref, sum_ref)

    spread(copies_ref, sum_ref[...])


def row_plan_kernel(
    log_target, first, parts_ref, grad_ref, dual_in_ref, row_dual_ref, top_ref, base_dual_ref,
    base_ref, score_hbm, out_ref, copies_ref, weight_ref, col_ref, sum_ref, tile_ref, sem,
):
    if first:
        dual = log_target - log_combined(parts_ref[...])
        grad = grad_ref[...]
        out_ref[...] = dual
    else:
        dual = dual_in_ref[...]
        grad = -jnp.sum(parts_ref[...], axis=0)
        out_ref[...] = grad
    lead = dual - base_dual_ref[...]
    row_lead = row_dual_ref[...] + top_ref[...]
    near = jnp.logical_and(jnp.max(jnp.abs(lead)) <= REACH, jnp.max(row_lead) <= 60.0)

    @pl.when(near)
    def _():
        weight_ref[...] = jnp.exp2(lead - log_target) * grad
        row_sums(base_ref, weight_ref, sum_ref)
        sum_ref[...] = sum_ref[...] * jnp.exp2(row_lead)

    @pl.when(jnp.logical_not(near))
    def _():
        col_ref[...] = dual - log_target
        weight_ref[...] = grad
        slow_row_weighted(score_hbm, tile_ref, sem, row_dual_ref, col_ref, weight_ref, sum_ref)

    spread(copies_ref, sum_ref[...])


def col_plan_kernel(
    log_source, parts_ref, outer_ref, dual_ref, row_dual_ref, top_ref, base_dual_ref, base_ref,
    score_hbm, out_ref, copies_ref, weight_ref, col_ref, sum_ref, tile_ref, sem,
):
    grad = outer_ref[...] - jnp.sum(parts_ref[...], axis=0)
    out_ref[...] = grad
    lead = dual_ref[...] - base_dual_ref[...]
    row_lead = row_dual_ref[...] + top_ref[...]
    near = jnp.logical_and(jnp.max(jnp.abs(lead)) <= REACH, jnp.max(row_lead) <= 60.0)

    @pl.when(near)
    def _():
        weight_ref[...] = jnp.exp2(row_lead) * grad
        col_sums(base_ref, weight_ref, sum_ref)
        sum_ref[...] = sum_ref[...] * jnp.exp2(lead - log_source)

    @pl.when(jnp.logical_not(near))
    def _():
        col_ref[...] = dual_ref[...] - log_source
        weight_ref[...] = grad
        slow_col_weighted(score_hbm, tile_ref, sem, row_dual_ref, col_ref, weight_ref, sum_ref)

    spread(copies_ref, sum_ref[...])


def is_near(dual_refs, row_refs, top_ref, base_dual_ref):
    near = None
    for ref in dual_refs:
        test = jnp.max(jnp.abs(ref[...] - base_dual_ref[...])) <= REACH
        near = test if near is None else jnp.logical_and(near, test)
    for ref in row_refs:
        near = jnp.logical_and(near, jnp.max(ref[...] + top_ref[...]) <= 60.0)
    return near


def most_grad_kernel(
    log_source, log_target,
    row1, row2, row3, col1, col2, col3, fbar2, fbar3, gbar1, gbar2, gbar3, top_ref, base_ref,
    score_hbm, out_ref, rows_ref, cols_ref, tile_ref, sem,
):
    near = is_near((col2, col3), (row1, row2, row3), top_ref, col1)
    count = groups_of(col1)

    @pl.when(near)
    def _():
        for k, row in enumerate((row1, row2, row3)):
            rows_ref[k] = -jnp.exp2(row[...] + top_ref[...])
        rows_ref[3] = rows_ref[1] * fbar2[...]
        rows_ref[4] = rows_ref[2] * fbar3[...]
        leads = [jnp.zeros_like(col1), col2[...] - col1[...], col3[...] - col1[...]]
        for k, grad in enumerate((gbar1, gbar2, gbar3)):
            cols_ref[k] = jnp.exp2(leads[k] - log_target) * grad[...]
        for k in range(2):
            cols_ref[3 + k] = jnp.exp2(leads[k] - log_source)
        for s in range(groups_of(row1)):
            columns = [to_column(rows_ref[k, s : s + 1, :]) for k in range(5)]
            for q in range(LANES // STRIP):
                rows = slice(s * LANES + q * STRIP, s * LANES + (q + 1) * STRIP)
                strips = [
                    jnp.broadcast_to(part[q * STRIP : (q + 1) * STRIP], (STRIP, LANES))
                    for part in columns
                ]
                for c in range(count):
                    lanes = slice(c * LANES, (c + 1) * LANES)
                    weight = strips[0] * cols_ref[0, c : c + 1, :]
                    for k in range(1, 5):
                        weight = weight + strips[k] * cols_ref[k, c : c + 1, :]
                    out_ref[rows, lanes] = base_ref[rows, lanes] * weight

    @pl.when(jnp.logical_not(near))
    def _():
        for k, row in enumerate((row1, row2, row3)):
            rows_ref[k] = row[...]
        rows_ref[3] = fbar2[...]
        rows_ref[4] = fbar3[...]
        for k, col in enumerate((col1, col2, col3)):
            cols_ref[k] = col[...]
        for k, grad in enumerate((gbar1, gbar2, gbar3)):
            cols_ref[3 + k] = grad[...]

        @pl.loop(0, groups_of(row1))
        def _(group):
            load_rows(score_hbm, tile_ref, sem, group)
            columns = [to_column(rows_ref[k, pl.ds(group, 1), :]) for k in range(5)]
            for c in range(count):
                lanes = slice(c * LANES, (c + 1) * LANES)
                value = jnp.zeros((LANES, LANES), F32)
                for k in reversed(range(3)):
                    scores = tile_ref[:, lanes] + columns[k]
                    plan_q = jnp.exp2(scores + (cols_ref[k, c : c + 1, :] - log_target))
                    value = value + plan_q * cols_ref[3 + k, c : c + 1, :]
                    if k:
                        plan_r = jnp.exp2(scores + (cols_ref[k - 1, c : c + 1, :] - log_source))
                        value = value + plan_r * columns[2 + k]
                start = pl.multiple_of(group * LANES, LANES)
                out_ref[pl.ds(start, LANES), lanes] = -value


def grad_kernel(
    log_source, parts_ref, row1, top_ref, base_ref, most_ref, out_ref, first_ref, second_ref, rows_ref
):
    fbar1 = -jnp.sum(parts_ref[...], axis=0)
    rows_ref[...] = -jnp.exp2(row1[...] + top_ref[...] - log_source) * fbar1
    half = first_ref.shape[1]
    for s in range(groups_of(row1)):
        column = jnp.broadcast_to(to_column(rows_ref[s : s + 1, :]), (LANES, LANES))
        rows = slice(s * LANES, (s + 1) * LANES)
        for c in range(out_ref.shape[1] // LANES):
            lanes = slice(c * LANES, (c + 1) * LANES)
            value = (most_ref[rows, lanes] + base_ref[rows, lanes] * column).astype(jnp.bfloat16)
            out_ref[rows, lanes] = value
            part, at = (first_ref, c * LANES) if c * LANES < half else (second_ref, c * LANES - half)
            part[rows, at : at + LANES] = value


def call(kernel, arguments, outs, scratch=(), in_hbm=(), flops=0, name=None):
    specs = [
        pl.BlockSpec(memory_space=pl.ANY if at in in_hbm else pltpu.VMEM)
        for at in range(len(arguments))
    ]
    return pl.pallas_call(
        kernel,
        out_shape=outs,
        in_specs=specs,
        out_specs=[pl.BlockSpec(memory_space=pltpu.VMEM)] * len(outs),
        scratch_shapes=list(scratch),
        compiler_params=pltpu.CompilerParams(vmem_limit_bytes=VMEM_BYTES),
        name=name,
    )(*arguments)


def exchanged(copies, axis):
    return lax.all_to_all(copies, axis, 0, 0, tiled=True)


def ring_sum(values, dim, at, axis, moves):
    count = values.shape[dim]

    def block(offset):
        return lax.dynamic_index_in_dim(values, (at + offset) % count, dim, keepdims=False)

    reach = count // 2
    farthest = block(reach)
    middle = farthest.shape[0] // 2
    up = lax.ppermute(farthest[:middle], axis, moves(1))
    down = lax.ppermute(farthest[middle:], axis, moves(-1))
    for left in range(reach - 1, 0, -1):
        ahead, behind = block(left), block(-left)
        if left == reach - 1:
            ahead = jnp.concatenate([ahead[:middle] + up, ahead[middle:]])
            behind = jnp.concatenate([behind[:middle], behind[middle:] + down])
        else:
            ahead, behind = ahead + up, behind + down
        up = lax.ppermute(ahead, axis, moves(1))
        down = lax.ppermute(behind, axis, moves(-1))
    return block(0) + up + down


def body(cost, src_label, tgt_label, class_mask, g_start, f_bar, g_bar, src_emb, tgt_emb):
    row_count = lax.axis_size("rows")
    col_count = lax.axis_size("cols")
    src_rows, tgt_cols = cost.shape
    width = src_emb.shape[1]
    log_source = -math.log2(src_rows * row_count)
    log_target = -math.log2(tgt_cols * col_count)
    row_shape = (src_rows // LANES, LANES)
    col_shape = (tgt_cols // LANES, LANES)
    src_label, f_bar = src_label.reshape(row_shape), f_bar.reshape(row_shape)
    tgt_label, g_bar = tgt_label.reshape(col_shape), g_bar.reshape(col_shape)
    g_start = g_start.reshape(col_shape)

    def array(shape, dtype=F32):
        return jax.ShapeDtypeStruct(shape, dtype)

    matrix = array(cost.shape)
    row_vector, col_vector = array(row_shape), array(col_shape)
    row_copies = array((col_count,) + row_shape)
    col_copies = array((row_count,) + col_shape)
    row_held, col_held = pltpu.VMEM(row_shape, F32), pltpu.VMEM(col_shape, F32)
    slow = [pltpu.VMEM((LANES, tgt_cols), F32), pltpu.SemaphoreType.DMA]

    score, start_base, start_top, copies = call(
        first_kernel,
        (cost, src_label, tgt_label, class_mask, g_start),
        [matrix, matrix, row_vector, row_copies],
        [
            pltpu.VMEM(cost.shape, cost.dtype),
            pltpu.VMEM(row_shape, jnp.int32),
            pltpu.VMEM(col_shape, jnp.int32),
            pltpu.VMEM(class_mask.shape, jnp.int32),
            col_held,
            pltpu.VMEM((LANES, tgt_cols), F32),
            row_held,
            pltpu.SemaphoreType.DMA((4,)),
            pltpu.SemaphoreType.DMA(row_shape[:1]),
        ],
        in_hbm=range(5),
        name="first_row_logs",
    )

    def col_logs(parts, top, base_dual, base):
        return call(
            functools.partial(col_log_kernel, log_source),
            (parts, top, base_dual, base, score),
            [row_vector, col_copies],
            [row_held, col_held] + slow,
            in_hbm=(4,),
            name="col_logs",
        )

    zero = jnp.zeros(col_shape, F32)
    row1, copies = col_logs(exchanged(copies, "cols"), start_top, zero, start_base)
    base, top, col1, copies = call(
        functools.partial(rebase_kernel, log_target),
        (exchanged(copies, "rows"), score),
        [matrix, row_vector, col_vector, row_copies],
        [row_held],
        name="second_row_logs",
    )
    row2, copies = col_logs(exchanged(copies, "cols"), top, col1, base)
    col2, copies = call(
        functools.partial(row_log_kernel, log_target),
        (exchanged(copies, "rows"), top, col1, base, score),
        [col_vector, row_copies],
        [col_held, row_held] + slow,
        in_hbm=(4,),
        name="third_row_logs",
    )
    row3, copies = col_logs(exchanged(copies, "cols"), top, col1, base)

    def row_plan(first, parts, grad, dual, row):
        return call(
            functools.partial(row_plan_kernel, log_target, first),
            (parts, grad, dual, row, top, col1, base, score),
            [col_vector, row_copies],
            [col_held, col_held, row_held] + slow,
            in_hbm=(7,),
            name="row_plan",
        )

    def col_plan(parts, outer, dual, row, top, base_dual, base):
        return call(
            functools.partial(col_plan_kernel, log_source),
            (parts, outer, dual, row, top, base_dual, base, score),
            [row_vector, col_copies],
            [row_held, col_held, col_held] + slow,
            in_hbm=(7,),
            name="col_plan",
        )

    none = jnp.zeros(row_shape, F32)
    col3, copies = row_plan(True, exchanged(copies, "rows"), g_bar, col2, row3)
    fbar3, copies = col_plan(exchanged(copies, "cols"), f_bar, col2, row3, top, col1, base)
    gbar2, copies = row_plan(False, exchanged(copies, "rows"), g_bar, col2, row2)
    fbar2, copies = col_plan(exchanged(copies, "cols"), none, col1, row2, top, col1, base)
    gbar1, copies = row_plan(False, exchanged(copies, "rows"), g_bar, col1, row1)
    parts = exchanged(copies, "cols")
    (most,) = call(
        functools.partial(most_grad_kernel, log_source, log_target),
        (
            row1, row2, row3, col1, col2, col3, fbar2, fbar3, gbar1, gbar2, g_bar, top, base, score,
        ),
        [matrix],
        [pltpu.VMEM((5,) + row_shape, F32), pltpu.VMEM((6,) + col_shape, F32)] + slow,
        in_hbm=(13,),
        name="most_cost_grad",
    )
    half = array((src_rows, tgt_cols // 2), jnp.bfloat16)
    rounded, rounded1, rounded2 = call(
        functools.partial(grad_kernel, log_source),
        (parts, row1, start_top, start_base, most),
        [array(cost.shape, jnp.bfloat16), half, half],
        [row_held],
        name="cost_grad",
    )
    x_count, z_count, y_count = 4, row_count // 4, col_count // 2
    owned = width // row_count
    row_at, col_at = lax.axis_index("rows"), lax.axis_index("cols")
    x_at, z_at, y_at, core_at = row_at // z_count, row_at % z_count, col_at // 2, col_at % 2

    def along_x(step):
        return [
            (x * z_count + z, (x + step) % x_count * z_count + z)
            for x in range(x_count)
            for z in range(z_count)
        ]

    def along_z(step):
        return [
            (x * z_count + z, x * z_count + (z + step) % z_count)
            for x in range(x_count)
            for z in range(z_count)
        ]

    def along_y(step):
        return [
            (y * 2 + core, (y + step) % y_count * 2 + core)
            for y in range(y_count)
            for core in range(2)
        ]

    def y_dot(grads):
        return lax.dot_general(
            src_emb, grads, (((0,), (0,)), ((), ())), preferred_element_type=F32
        )

    first = y_dot(rounded1).reshape(x_count, z_count * owned, -1)
    first = ring_sum(first, 0, x_at, "rows", along_x)
    second = y_dot(rounded2).reshape(x_count, z_count, owned, -1)
    second = ring_sum(second, 1, z_at, "rows", along_z)
    x_part = lax.dot_general(
        tgt_emb, rounded, (((0,), (1,)), ((), ())), preferred_element_type=F32
    ).reshape(y_count, 2, -1, src_rows)
    sent = lax.dynamic_index_in_dim(x_part, 1 - core_at, 1, keepdims=False)
    kept = lax.dynamic_index_in_dim(x_part, core_at, 1, keepdims=False)
    arrived = lax.ppermute(sent, "cols", [(at, at ^ 1) for at in range(col_count)])
    grad_x = ring_sum(kept + arrived, 0, y_at, "cols", along_y)
    fbar1, copies = col_plan(parts, none, zero, row1, start_top, zero, start_base)
    g_start_bar = -jnp.sum(exchanged(copies, "rows"), axis=0).reshape(tgt_cols)
    first = ring_sum(first.reshape(z_count, owned, -1), 0, z_at, "rows", along_z)
    second = ring_sum(second, 0, x_at, "rows", along_x)
    grad_y = jnp.concatenate([first, second], axis=1)
    return (g_start_bar, grad_x, grad_y)


def solution(mesh):
    placed = (
        P("rows", "cols"),
        P("rows"),
        P("cols"),
        P(),
        P("cols"),
        P("rows"),
        P("cols"),
        P("rows", None),
        P("cols", None),
    )
    return jax.shard_map(
        body,
        mesh=mesh,
        in_specs=placed,
        out_specs=(P("cols"), P("cols", "rows"), P("rows", "cols")),
        check_vma=False,
    )
```

```python
import functools
import math

import jax
import jax.numpy as jnp
from jax import lax
from jax.experimental import pallas as pl
from jax.experimental.pallas import tpu as pltpu
from jax.sharding import PartitionSpec as P

K = 3


EPSILON = 0.05
PENALTY = 1.0
SCALE = 1.0 / (EPSILON * math.log(2.0))
LANES = 128
STRIP = 32
REACH = 40.0
FIRST_REACH = 75.0
VMEM_BYTES = 16 * 2**20
F32 = jnp.float32


def eye():
    return lax.broadcasted_iota(jnp.int32, (LANES, LANES), 0) == lax.broadcasted_iota(
        jnp.int32, (LANES, LANES), 1
    )


def to_column(row):
    return jnp.sum(jnp.where(eye(), row, 0.0), axis=1, keepdims=True)


def to_row(column):
    return jnp.sum(jnp.where(eye(), column, 0.0), axis=0, keepdims=True)


def log_combined(parts):
    top = jnp.max(parts, axis=0)
    return top + jnp.log2(jnp.sum(jnp.exp2(parts - top[None]), axis=0))


def spread(copies_ref, value):
    copies_ref[...] = jnp.broadcast_to(value[None], copies_ref.shape)


def groups_of(ref):
    return ref.shape[0]


def row_sums(base_ref, weight_ref, out_ref):
    for s in range(groups_of(out_ref)):
        held = None
        for c in range(groups_of(weight_ref)):
            tile = base_ref[s * LANES : (s + 1) * LANES, c * LANES : (c + 1) * LANES]
            term = tile * weight_ref[c : c + 1, :]
            held = term if held is None else held + term
        out_ref[s : s + 1, :] = to_row(jnp.sum(held, axis=1, keepdims=True))


def col_sums(base_ref, weight_ref, out_ref):
    held = [None] * groups_of(out_ref)
    for s in range(groups_of(weight_ref)):
        column = jnp.broadcast_to(to_column(weight_ref[s : s + 1, :]), (LANES, LANES))
        for c in range(len(held)):
            tile = base_ref[s * LANES : (s + 1) * LANES, c * LANES : (c + 1) * LANES]
            term = jnp.sum((tile * column).reshape(LANES // 8, 8, LANES), axis=0)
            held[c] = term if held[c] is None else held[c] + term
    for c, term in enumerate(held):
        out_ref[c : c + 1, :] = jnp.sum(term, axis=0, keepdims=True)


def strip_logs(scores):
    highest = jnp.max(scores, axis=1, keepdims=True)
    powers = jnp.exp2(scores - highest)
    return highest, powers, highest + jnp.log2(jnp.sum(powers, axis=1, keepdims=True))


def wide(ref):
    return jnp.concatenate([ref[c : c + 1, :] for c in range(groups_of(ref))], axis=1)


def load_rows(score_hbm, tile_ref, sem, group):
    copy = pltpu.make_async_copy(
        score_hbm.at[pl.ds(pl.multiple_of(group * LANES, LANES), LANES), :], tile_ref, sem
    )
    copy.start()
    copy.wait()


def slow_row_logs(score_hbm, tile_ref, sem, col_ref, out_ref):
    @pl.loop(0, groups_of(out_ref))
    def _(group):
        load_rows(score_hbm, tile_ref, sem, group)
        logs = []
        for q in range(LANES // STRIP):
            logs.append(strip_logs(tile_ref[q * STRIP : (q + 1) * STRIP, :] + wide(col_ref))[2])
        out_ref[pl.ds(group, 1), :] = to_row(jnp.concatenate(logs, axis=0))


def slow_col_logs(score_hbm, tile_ref, sem, row_ref, out_ref):
    count = groups_of(out_ref)
    tops = tuple(jnp.full((1, LANES), -1e30, F32) for _ in range(count))

    def highest(group, tops):
        load_rows(score_hbm, tile_ref, sem, group)
        column = to_column(row_ref[pl.ds(group, 1), :])
        return tuple(
            jnp.maximum(
                tops[c],
                jnp.max(
                    tile_ref[:, c * LANES : (c + 1) * LANES] + column, axis=0, keepdims=True
                ),
            )
            for c in range(count)
        )

    tops = lax.fori_loop(0, groups_of(row_ref), highest, tops)
    sums = tuple(jnp.zeros((1, LANES), F32) for _ in range(count))

    def summed(group, sums):
        load_rows(score_hbm, tile_ref, sem, group)
        column = to_column(row_ref[pl.ds(group, 1), :])
        return tuple(
            sums[c]
            + jnp.sum(
                jnp.exp2(tile_ref[:, c * LANES : (c + 1) * LANES] + column - tops[c]),
                axis=0,
                keepdims=True,
            )
            for c in range(count)
        )

    sums = lax.fori_loop(0, groups_of(row_ref), summed, sums)
    for c in range(count):
        out_ref[c : c + 1, :] = tops[c] + jnp.log2(sums[c])


def slow_row_weighted(score_hbm, tile_ref, sem, row_ref, col_ref, weight_ref, out_ref):
    @pl.loop(0, groups_of(out_ref))
    def _(group):
        load_rows(score_hbm, tile_ref, sem, group)
        column = to_column(row_ref[pl.ds(group, 1), :])
        sums = []
        for q in range(LANES // STRIP):
            part = slice(q * STRIP, (q + 1) * STRIP)
            plan = jnp.exp2(tile_ref[part, :] + column[part] + wide(col_ref))
            sums.append(jnp.sum(plan * wide(weight_ref), axis=1, keepdims=True))
        out_ref[pl.ds(group, 1), :] = to_row(jnp.concatenate(sums, axis=0))


def slow_col_weighted(score_hbm, tile_ref, sem, row_ref, col_ref, weight_ref, out_ref):
    count = groups_of(out_ref)
    sums = tuple(jnp.zeros((1, LANES), F32) for _ in range(count))

    def summed(group, sums):
        load_rows(score_hbm, tile_ref, sem, group)
        column = to_column(row_ref[pl.ds(group, 1), :])
        weight = to_column(weight_ref[pl.ds(group, 1), :])
        return tuple(
            sums[c]
            + jnp.sum(
                weight
                * jnp.exp2(
                    tile_ref[:, c * LANES : (c + 1) * LANES] + column + col_ref[c : c + 1, :]
                ),
                axis=0,
                keepdims=True,
            )
            for c in range(count)
        )

    sums = lax.fori_loop(0, groups_of(row_ref), summed, sums)
    for c in range(count):
        out_ref[c : c + 1, :] = sums[c]


def first_kernel(
    cost_hbm, src_hbm, tgt_hbm, mask_hbm, dual_hbm, score_hbm, base_ref, top_ref, copies_ref,
    cost_ref, src_ref, tgt_ref, mask_ref, dual_ref, allowed_ref, log_ref, score_ref,
    small_sem, cost_sem, score_sem,
):
    small = [
        pltpu.make_async_copy(source, target, small_sem.at[at])
        for at, (source, target) in enumerate(
            ((tgt_hbm, tgt_ref), (mask_hbm, mask_ref), (src_hbm, src_ref), (dual_hbm, dual_ref))
        )
    ]
    for copy in small:
        copy.start()
    blocks = []
    for s in range(groups_of(log_ref)):
        rows = pl.ds(s * LANES, LANES)
        blocks.append(
            pltpu.make_async_copy(cost_hbm.at[rows, :], cost_ref.at[rows, :], cost_sem.at[s])
        )
        blocks[-1].start()
    for copy in small:
        copy.wait()
    classes = mask_ref.shape[0]
    mask = mask_ref[...].astype(F32).astype(jnp.bfloat16)
    ids = lax.broadcasted_iota(jnp.int32, (classes, LANES), 0)
    hot = jnp.concatenate(
        [
            jnp.where(tgt_ref[c : c + 1, :] == ids, 1.0, 0.0).astype(jnp.bfloat16)
            for c in range(groups_of(tgt_ref))
        ],
        axis=1,
    )
    allowed_of = jnp.dot(mask, hot, preferred_element_type=F32).astype(jnp.bfloat16)
    lane_ids = lax.broadcasted_iota(jnp.int32, (LANES, classes), 1).astype(F32)
    dual = wide(dual_ref) * SCALE - PENALTY * SCALE
    for s in range(groups_of(log_ref)):
        label = to_column(src_ref[s : s + 1, :].astype(F32))
        src_hot = jnp.where(label == lane_ids, 1.0, 0.0).astype(jnp.bfloat16)
        allowed_ref[...] = jnp.dot(src_hot, allowed_of, preferred_element_type=F32)
        blocks[s].wait()
        tops, logs = [], []
        for q in range(LANES // STRIP):
            rows = slice(s * LANES + q * STRIP, s * LANES + (q + 1) * STRIP)
            shifted = cost_ref[rows, :].astype(F32) - PENALTY * allowed_ref[
                q * STRIP : (q + 1) * STRIP, :
            ]
            scores = dual - shifted * SCALE
            highest, powers, log = strip_logs(scores)
            score_ref[rows, :] = scores
            base_ref[rows, :] = powers
            tops.append(highest)
            logs.append(log)
        top_ref[s : s + 1, :] = to_row(jnp.concatenate(tops, axis=0))
        log_ref[s : s + 1, :] = to_row(jnp.concatenate(logs, axis=0))
        rows = pl.ds(s * LANES, LANES)
        blocks[s] = pltpu.make_async_copy(
            score_ref.at[rows, :], score_hbm.at[rows, :], score_sem.at[s]
        )
        blocks[s].start()
    spread(copies_ref, log_ref[...])
    for copy in blocks:
        copy.wait()


def rebase_kernel(
    log_target, parts_ref, score_hbm, base_ref, top_ref, dual_ref, copies_ref, log_ref, score_ref,
    score_sem,
):
    blocks = []
    for s in range(groups_of(log_ref)):
        rows = pl.ds(s * LANES, LANES)
        blocks.append(
            pltpu.make_async_copy(score_hbm.at[rows, :], score_ref.at[rows, :], score_sem.at[s])
        )
        blocks[-1].start()
    dual_ref[...] = log_target - log_combined(parts_ref[...])
    dual = wide(dual_ref)
    for s in range(groups_of(log_ref)):
        blocks[s].wait()
        tops, logs = [], []
        for q in range(LANES // STRIP):
            rows = slice(s * LANES + q * STRIP, s * LANES + (q + 1) * STRIP)
            highest, powers, log = strip_logs(score_ref[rows, :] + dual)
            base_ref[rows, :] = powers
            tops.append(highest)
            logs.append(log)
        top_ref[s : s + 1, :] = to_row(jnp.concatenate(tops, axis=0))
        log_ref[s : s + 1, :] = to_row(jnp.concatenate(logs, axis=0))
    spread(copies_ref, log_ref[...])


def row_log_kernel(
    log_target, parts_ref, top_ref, base_dual_ref, base_ref, score_hbm, dual_ref, copies_ref,
    weight_ref, sum_ref, tile_ref, sem,
):
    dual_ref[...] = log_target - log_combined(parts_ref[...])
    lead = dual_ref[...] - base_dual_ref[...]
    near = jnp.max(jnp.abs(lead)) <= REACH

    @pl.when(near)
    def _():
        weight_ref[...] = jnp.exp2(lead)
        row_sums(base_ref, weight_ref, sum_ref)
        sum_ref[...] = top_ref[...] + jnp.log2(sum_ref[...])

    @pl.when(jnp.logical_not(near))
    def _():
        slow_row_logs(score_hbm, tile_ref, sem, dual_ref, sum_ref)

    spread(copies_ref, sum_ref[...])


def col_log_kernel(
    log_source, parts_ref, top_ref, base_dual_ref, base_ref, score_hbm, dual_ref, copies_ref,
    weight_ref, sum_ref, tile_ref, sem,
):
    dual_ref[...] = log_source - log_combined(parts_ref[...])
    lead = dual_ref[...] + top_ref[...]
    weight_ref[...] = jnp.exp2(jnp.minimum(lead, 100.0))
    col_sums(base_ref, weight_ref, sum_ref)
    most = jnp.max(lead)
    near = jnp.logical_and(
        most <= 60.0,
        jnp.min(jnp.log2(jnp.maximum(sum_ref[...], 1e-37))) >= jnp.maximum(most, -15.0) - 85.0,
    )

    @pl.when(near)
    def _():
        sum_ref[...] = jnp.log2(sum_ref[...]) - base_dual_ref[...]

    @pl.when(jnp.logical_not(near))
    def _():
        slow_col_logs(score_hbm, tile_ref, sem, dual_ref, sum_ref)

    spread(copies_ref, sum_ref[...])


def row_plan_kernel(
    log_target, first, parts_ref, grad_ref, dual_in_ref, row_dual_ref, top_ref, base_dual_ref,
    base_ref, score_hbm, out_ref, copies_ref, weight_ref, col_ref, sum_ref, tile_ref, sem,
):
    if first:
        dual = log_target - log_combined(parts_ref[...])
        grad = grad_ref[...]
        out_ref[...] = dual
    else:
        dual = dual_in_ref[...]
        grad = -jnp.sum(parts_ref[...], axis=0)
        out_ref[...] = grad
    lead = dual - base_dual_ref[...]
    row_lead = row_dual_ref[...] + top_ref[...]
    near = jnp.logical_and(jnp.max(jnp.abs(lead)) <= REACH, jnp.max(row_lead) <= 60.0)

    @pl.when(near)
    def _():
        weight_ref[...] = jnp.exp2(lead - log_target) * grad
        row_sums(base_ref, weight_ref, sum_ref)
        sum_ref[...] = sum_ref[...] * jnp.exp2(row_lead)

    @pl.when(jnp.logical_not(near))
    def _():
        col_ref[...] = dual - log_target
        weight_ref[...] = grad
        slow_row_weighted(score_hbm, tile_ref, sem, row_dual_ref, col_ref, weight_ref, sum_ref)

    spread(copies_ref, sum_ref[...])


def col_plan_kernel(
    log_source, reach, parts_ref, outer_ref, dual_ref, row_dual_ref, top_ref, base_dual_ref, base_ref,
    score_hbm, out_ref, copies_ref, weight_ref, col_ref, sum_ref, tile_ref, sem,
):
    grad = outer_ref[...] - jnp.sum(parts_ref[...], axis=0)
    out_ref[...] = grad
    lead = dual_ref[...] - base_dual_ref[...]
    row_lead = row_dual_ref[...] + top_ref[...]
    near = jnp.logical_and(jnp.max(jnp.abs(lead)) <= reach, jnp.max(row_lead) <= 60.0)

    @pl.when(near)
    def _():
        weight_ref[...] = jnp.exp2(row_lead) * grad
        col_sums(base_ref, weight_ref, sum_ref)
        sum_ref[...] = sum_ref[...] * jnp.exp2(lead - log_source)

    @pl.when(jnp.logical_not(near))
    def _():
        col_ref[...] = dual_ref[...] - log_source
        weight_ref[...] = grad
        slow_col_weighted(score_hbm, tile_ref, sem, row_dual_ref, col_ref, weight_ref, sum_ref)

    spread(copies_ref, sum_ref[...])


def is_near(dual_refs, row_refs, top_ref, base_dual_ref):
    near = None
    for ref in dual_refs:
        test = jnp.max(jnp.abs(ref[...] - base_dual_ref[...])) <= REACH
        near = test if near is None else jnp.logical_and(near, test)
    for ref in row_refs:
        near = jnp.logical_and(near, jnp.max(ref[...] + top_ref[...]) <= 60.0)
    return near


def most_grad_kernel(
    log_source, log_target,
    row1, row2, row3, col1, col2, col3, fbar2, fbar3, gbar1, gbar2, gbar3, top_ref, base_ref,
    score_hbm, out_ref, rows_ref, cols_ref, tile_ref, sem,
):
    near = is_near((col2, col3), (row1, row2, row3), top_ref, col1)
    count = groups_of(col1)

    @pl.when(near)
    def _():
        for k, row in enumerate((row1, row2, row3)):
            rows_ref[k] = -jnp.exp2(row[...] + top_ref[...])
        rows_ref[3] = rows_ref[1] * fbar2[...]
        rows_ref[4] = rows_ref[2] * fbar3[...]
        leads = [jnp.zeros_like(col1), col2[...] - col1[...], col3[...] - col1[...]]
        for k, grad in enumerate((gbar1, gbar2, gbar3)):
            cols_ref[k] = jnp.exp2(leads[k] - log_target) * grad[...]
        for k in range(2):
            cols_ref[3 + k] = jnp.exp2(leads[k] - log_source)
        for s in range(groups_of(row1)):
            columns = [to_column(rows_ref[k, s : s + 1, :]) for k in range(5)]
            for q in range(LANES // STRIP):
                rows = slice(s * LANES + q * STRIP, s * LANES + (q + 1) * STRIP)
                strips = [
                    jnp.broadcast_to(part[q * STRIP : (q + 1) * STRIP], (STRIP, LANES))
                    for part in columns
                ]
                for c in range(count):
                    lanes = slice(c * LANES, (c + 1) * LANES)
                    weight = strips[0] * cols_ref[0, c : c + 1, :]
                    for k in range(1, 5):
                        weight = weight + strips[k] * cols_ref[k, c : c + 1, :]
                    out_ref[rows, lanes] = base_ref[rows, lanes] * weight

    @pl.when(jnp.logical_not(near))
    def _():
        for k, row in enumerate((row1, row2, row3)):
            rows_ref[k] = row[...]
        rows_ref[3] = fbar2[...]
        rows_ref[4] = fbar3[...]
        for k, col in enumerate((col1, col2, col3)):
            cols_ref[k] = col[...]
        for k, grad in enumerate((gbar1, gbar2, gbar3)):
            cols_ref[3 + k] = grad[...]

        @pl.loop(0, groups_of(row1))
        def _(group):
            load_rows(score_hbm, tile_ref, sem, group)
            columns = [to_column(rows_ref[k, pl.ds(group, 1), :]) for k in range(5)]
            for c in range(count):
                lanes = slice(c * LANES, (c + 1) * LANES)
                value = jnp.zeros((LANES, LANES), F32)
                for k in reversed(range(3)):
                    scores = tile_ref[:, lanes] + columns[k]
                    plan_q = jnp.exp2(scores + (cols_ref[k, c : c + 1, :] - log_target))
                    value = value + plan_q * cols_ref[3 + k, c : c + 1, :]
                    if k:
                        plan_r = jnp.exp2(scores + (cols_ref[k - 1, c : c + 1, :] - log_source))
                        value = value + plan_r * columns[2 + k]
                start = pl.multiple_of(group * LANES, LANES)
                out_ref[pl.ds(start, LANES), lanes] = -value


def direction(place_ref):
    return 1 - 2 * place_ref[3]


def ring_place(place_ref, axis, offset, count):
    return lax.rem(place_ref[axis] + direction(place_ref) * offset + count, count)


def z_block(place_ref, src_ref, grad_ref, offset, counts):
    x_count, z_count = counts
    width, half = src_ref.shape[0], grad_ref.shape[1] // 2
    owned = width // (x_count * z_count)
    at = ring_place(place_ref, 2, offset, z_count)
    rows = [
        src_ref[pl.ds(pl.multiple_of((x * z_count + at) * owned, owned), owned), :]
        for x in range(x_count)
    ]
    return jnp.dot(
        jnp.concatenate(rows, axis=0), grad_ref[:, half:], preferred_element_type=F32
    )


def x_block(place_ref, src_ref, grad_ref, offset, counts):
    x_count = counts[0]
    width, half = src_ref.shape[0], grad_ref.shape[1] // 2
    owned = width // x_count
    at = ring_place(place_ref, 0, offset, x_count)
    rows = src_ref[pl.ds(pl.multiple_of(at * owned, owned), owned), :]
    return jnp.dot(rows, grad_ref[:, :half], preferred_element_type=F32)


def grad_kernel(
    log_source, counts, place_ref, parts_ref, row1, col1, top_ref, base_ref, most_ref, src_ref,
    score_hbm, out_ref, z_far_ref, x_far_ref, rows_ref, cols_ref, tile_ref, sem,
):
    fbar1 = -jnp.sum(parts_ref[...], axis=0)
    row_lead = row1[...] + top_ref[...]
    near = jnp.logical_and(jnp.max(jnp.abs(col1[...])) <= FIRST_REACH, jnp.max(row_lead) <= 60.0)

    @pl.when(near)
    def _():
        rows_ref[...] = -jnp.exp2(row_lead) * fbar1
        cols_ref[...] = jnp.exp2(-col1[...] - log_source)
        for s in range(groups_of(row1)):
            column = jnp.broadcast_to(to_column(rows_ref[s : s + 1, :]), (LANES, LANES))
            rows = slice(s * LANES, (s + 1) * LANES)
            for c in range(groups_of(col1)):
                lanes = slice(c * LANES, (c + 1) * LANES)
                term = base_ref[rows, lanes] * (column * cols_ref[c : c + 1, :])
                out_ref[rows, lanes] = (most_ref[rows, lanes] + term).astype(jnp.bfloat16)

    @pl.when(jnp.logical_not(near))
    def _():
        rows_ref[...] = -fbar1

        @pl.loop(0, groups_of(row1))
        def _(group):
            load_rows(score_hbm, tile_ref, sem, group)
            column = to_column(row1[pl.ds(group, 1), :]) - log_source
            weight = to_column(rows_ref[pl.ds(group, 1), :])
            rows = pl.ds(pl.multiple_of(group * LANES, LANES), LANES)
            term = jnp.exp2(tile_ref[...] + column) * weight
            out_ref[rows, :] = (most_ref[rows, :] + term).astype(jnp.bfloat16)

    z_far_ref[...] = z_block(place_ref, src_ref, out_ref, counts[1] // 2, counts)
    x_far_ref[...] = x_block(place_ref, src_ref, out_ref, counts[0] // 2, counts)


def x_part_kernel(y_count, place_ref, grad_ref, tgt_ref, sent_ref, kept_ref, order_ref):
    block = tgt_ref.shape[0] // (2 * y_count)
    core, turn = place_ref[3], direction(place_ref)
    for side, out_ref in ((0, sent_ref), (1, kept_ref)):
        for k, offset in enumerate((2, 1, -1, 0)):
            step = offset * (2 * side - 1)
            at = lax.rem(place_ref[1] + turn * step + y_count, y_count)
            owner = at * 2 + (core if side else 1 - core)
            order_ref[k * block : (k + 1) * block, :] = tgt_ref[
                pl.ds(pl.multiple_of(owner * block, block), block), :
            ]
        product = lax.dot_general(
            order_ref[...], grad_ref[...], (((1,), (1,)), ((), ())), preferred_element_type=F32
        )
        out_ref[...] = product.reshape(out_ref.shape)


def y_parts_kernel(counts, place_ref, grad_ref, src_ref, after_ref, *outs):
    reach = counts[1] // 2
    offsets = [*range(reach - 1, 0, -1), *range(1 - reach, 1)]
    for out_ref, offset in zip(outs, offsets):
        out_ref[...] = z_block(place_ref, src_ref, grad_ref, offset, counts)
    for out_ref, offset in zip(outs[len(offsets) :], (1, -1, 0)):
        out_ref[...] = x_block(place_ref, src_ref, grad_ref, offset, counts)


def add_kernel(count, *refs):
    value = refs[0][...]
    for ref in refs[1:count]:
        value = value + ref[...]
    refs[-1][...] = value


def split_kernel(x_count, place_ref, own_ref, up_ref, down_ref, *outs):
    block = own_ref.shape[0] // x_count
    for out_ref, offset in zip(outs, (2, 1, -1, 0)):
        at = ring_place(place_ref, 0, offset, x_count)
        rows = pl.ds(pl.multiple_of(at * block, block), block)
        out_ref[...] = own_ref[rows, :] + up_ref[rows, :] + down_ref[rows, :]


def join_kernel(parts_ref, own_ref, up_ref, down_ref, out_ref):
    half = own_ref.shape[1]
    out_ref[:, :half] = jnp.sum(parts_ref[...], axis=0)
    out_ref[:, half:] = own_ref[...] + up_ref[...] + down_ref[...]


def call(
    kernel, arguments, outs, scratch=(), in_hbm=(), loose=(), in_smem=(), out_hbm=(), name=None
):
    specs = [
        pl.BlockSpec(
            memory_space=pltpu.HBM
            if at in in_hbm
            else pl.ANY
            if at in loose
            else pltpu.SMEM
            if at in in_smem
            else pltpu.VMEM
        )
        for at in range(len(arguments))
    ]
    arguments = [
        pltpu.with_memory_space_constraint(value, pltpu.HBM) if at in in_hbm else value
        for at, value in enumerate(arguments)
    ]
    outs = [
        pltpu.HBM(out.shape, out.dtype) if at in out_hbm else out for at, out in enumerate(outs)
    ]
    return pl.pallas_call(
        kernel,
        out_shape=outs,
        in_specs=specs,
        out_specs=[
            pl.BlockSpec(memory_space=pltpu.HBM if at in out_hbm else pltpu.VMEM)
            for at in range(len(outs))
        ],
        scratch_shapes=list(scratch),
        compiler_params=pltpu.CompilerParams(vmem_limit_bytes=VMEM_BYTES),
        name=name,
    )(*arguments)


def exchanged(copies, axis):
    return lax.all_to_all(copies, axis, 0, 0, tiled=True)


def added(values, after=()):
    return call(
        functools.partial(add_kernel, len(values)),
        (*values, *after),
        [jax.ShapeDtypeStruct(values[0].shape, F32)],
        loose=range(len(values), len(values) + len(after)),
        name="added",
    )[0]


def body(cost, src_label, tgt_label, class_mask, g_start, f_bar, g_bar, src_emb, tgt_emb):
    row_count = lax.axis_size("rows")
    col_count = lax.axis_size("cols")
    src_rows, tgt_cols = cost.shape
    width = src_emb.shape[1]
    log_source = -math.log2(src_rows * row_count)
    log_target = -math.log2(tgt_cols * col_count)
    row_shape = (src_rows // LANES, LANES)
    col_shape = (tgt_cols // LANES, LANES)
    src_label, f_bar = src_label.reshape(row_shape), f_bar.reshape(row_shape)
    tgt_label, g_bar = tgt_label.reshape(col_shape), g_bar.reshape(col_shape)
    g_start = g_start.reshape(col_shape)

    def array(shape, dtype=F32):
        return jax.ShapeDtypeStruct(shape, dtype)

    matrix = array(cost.shape)
    row_vector, col_vector = array(row_shape), array(col_shape)
    row_copies = array((col_count,) + row_shape)
    col_copies = array((row_count,) + col_shape)
    row_held, col_held = pltpu.VMEM(row_shape, F32), pltpu.VMEM(col_shape, F32)
    slow = [pltpu.VMEM((LANES, tgt_cols), F32), pltpu.SemaphoreType.DMA]

    score, start_base, start_top, copies = call(
        first_kernel,
        (cost, src_label, tgt_label, class_mask, g_start),
        [matrix, matrix, row_vector, row_copies],
        [
            pltpu.VMEM(cost.shape, cost.dtype),
            pltpu.VMEM(row_shape, jnp.int32),
            pltpu.VMEM(col_shape, jnp.int32),
            pltpu.VMEM(class_mask.shape, jnp.int32),
            col_held,
            pltpu.VMEM((LANES, tgt_cols), F32),
            row_held,
            pltpu.VMEM(cost.shape, F32),
            pltpu.SemaphoreType.DMA((4,)),
            pltpu.SemaphoreType.DMA(row_shape[:1]),
            pltpu.SemaphoreType.DMA(row_shape[:1]),
        ],
        in_hbm=range(5),
        out_hbm=(0,),
        name="first_row_logs",
    )

    def col_logs(parts, top, base_dual, base):
        return call(
            functools.partial(col_log_kernel, log_source),
            (parts, top, base_dual, base, score),
            [row_vector, col_copies],
            [row_held, col_held] + slow,
            in_hbm=(4,),
            name="col_logs",
        )

    zero = jnp.zeros(col_shape, F32)
    row1, copies = col_logs(exchanged(copies, "cols"), start_top, zero, start_base)
    base, top, col1, copies = call(
        functools.partial(rebase_kernel, log_target),
        (exchanged(copies, "rows"), score),
        [matrix, row_vector, col_vector, row_copies],
        [row_held, pltpu.VMEM(cost.shape, F32), pltpu.SemaphoreType.DMA(row_shape[:1])],
        in_hbm=(1,),
        name="second_row_logs",
    )
    row2, copies = col_logs(exchanged(copies, "cols"), top, col1, base)
    col2, copies = call(
        functools.partial(row_log_kernel, log_target),
        (exchanged(copies, "rows"), top, col1, base, score),
        [col_vector, row_copies],
        [col_held, row_held] + slow,
        in_hbm=(4,),
        name="third_row_logs",
    )
    row3, copies = col_logs(exchanged(copies, "cols"), top, col1, base)

    def row_plan(first, parts, grad, dual, row):
        return call(
            functools.partial(row_plan_kernel, log_target, first),
            (parts, grad, dual, row, top, col1, base, score),
            [col_vector, row_copies],
            [col_held, col_held, row_held] + slow,
            in_hbm=(7,),
            name="row_plan",
        )

    def col_plan(parts, outer, dual, row, top, base_dual, base, reach=REACH):
        return call(
            functools.partial(col_plan_kernel, log_source, reach),
            (parts, outer, dual, row, top, base_dual, base, score),
            [row_vector, col_copies],
            [row_held, col_held, col_held] + slow,
            in_hbm=(7,),
            name="col_plan",
        )

    none = jnp.zeros(row_shape, F32)
    src_turned, tgt_turned = src_emb.T, tgt_emb.T
    col3, copies = row_plan(True, exchanged(copies, "rows"), g_bar, col2, row3)
    fbar3, copies = col_plan(exchanged(copies, "cols"), f_bar, col2, row3, top, col1, base)
    gbar2, copies = row_plan(False, exchanged(copies, "rows"), g_bar, col2, row2)
    fbar2, copies = col_plan(exchanged(copies, "cols"), none, col1, row2, top, col1, base)
    gbar1, copies = row_plan(False, exchanged(copies, "rows"), g_bar, col1, row1)
    parts = exchanged(copies, "cols")
    (most,) = call(
        functools.partial(most_grad_kernel, log_source, log_target),
        (
            row1, row2, row3, col1, col2, col3, fbar2, fbar3, gbar1, gbar2, g_bar, top, base, score,
        ),
        [matrix],
        [pltpu.VMEM((5,) + row_shape, F32), pltpu.VMEM((6,) + col_shape, F32)] + slow,
        in_hbm=(13,),
        name="most_cost_grad",
    )
    x_count, z_count, y_count = 4, row_count // 4, col_count // 2
    counts = (x_count, z_count)
    owned = width // row_count
    row_at, col_at = lax.axis_index("rows"), lax.axis_index("cols")
    place = jnp.stack(
        [row_at // z_count, col_at // 2, row_at % z_count, col_at % 2]
    ).astype(jnp.int32)
    devices = [
        (x, y, z, core)
        for x in range(x_count)
        for y in range(y_count)
        for z in range(z_count)
        for core in range(2)
    ]

    def number(x, y, z, core):
        spot = (x % x_count * z_count + z % z_count) * y_count + y % y_count
        return spot * 2 + core

    def turn(value, axis, step):
        moves = []
        for device in devices:
            ahead = list(device)
            ahead[axis] += step * (1 - 2 * device[3])
            moves.append((number(*device), number(*ahead)))
        return lax.ppermute(value, ("rows", "cols"), moves)

    half = tgt_cols // 2
    z_shape = array((x_count * owned, half))
    x_shape = array((z_count * owned, half))
    rounded, z_far, x_far = call(
        functools.partial(grad_kernel, log_source, counts),
        (place, parts, row1, col1, top, base, most, src_turned, score),
        [array(cost.shape, jnp.bfloat16), z_shape, x_shape],
        [row_held, col_held] + slow,
        in_smem=(0,),
        in_hbm=(8,),
        name="cost_grad",
    )
    z_long = turn(z_far, 2, 1)
    x_long = turn(x_far, 0, 1)
    chip_part = array((y_count, width // col_count, src_rows))
    sent, kept = call(
        functools.partial(x_part_kernel, y_count),
        (place, rounded, tgt_turned),
        [chip_part, chip_part],
        [pltpu.VMEM((width // 2, tgt_cols), jnp.bfloat16)],
        in_smem=(0,),
        name="grad_x_parts",
    )
    arrived = lax.ppermute(sent, "cols", [(at, at ^ 1) for at in range(col_count)])
    outs = call(
        functools.partial(y_parts_kernel, counts),
        (place, rounded, src_turned, kept),
        [z_shape] * (z_count - 1) + [x_shape] * 3,
        in_smem=(0,),
        loose=(3,),
        name="grad_y_parts",
    )
    z_longs, z_shorts, z_own = outs[:3], outs[3:6], outs[6]
    x_one, x_back, x_own = outs[7:]
    x_short = turn(x_back, 0, -1)
    z_short = turn(z_shorts[0], 2, -1)
    fbar1, copies = col_plan(
        parts, none, zero, row1, top, col1, base, FIRST_REACH
    )
    start_parts = exchanged(copies, "rows")
    z_long = turn(added((z_longs[0], z_long)), 2, 1)
    chip = added((kept, arrived), (z_long,))
    y_long = turn(chip[0], 1, 1)
    x_long = turn(added((x_one, x_long)), 0, 1)
    y_short = turn(chip[2], 1, -1)
    z_short = turn(added((z_shorts[1], z_short)), 2, -1)
    z_long = turn(added((z_longs[1], z_long)), 2, 1)
    y_long = turn(added((chip[1], y_long)), 1, 1)
    z_short = turn(added((z_shorts[2], z_short)), 2, -1)
    z_long = turn(added((z_longs[2], z_long)), 2, 1)
    first = added((x_own, x_long, x_short))
    along_z = [[x * z_count + z for z in range(z_count)] for x in range(x_count)]
    first = lax.all_to_all(
        first.reshape(z_count, owned, half), "rows", 0, 0, tiled=True, axis_index_groups=along_z
    )
    last = array((owned, half))
    far, one, back, own = call(
        functools.partial(split_kernel, x_count),
        (place, z_own, z_long, z_short),
        [last] * 4,
        in_smem=(0,),
        name="second_half",
    )
    x_long = turn(far, 0, 1)
    x_short = turn(back, 0, -1)
    x_long = turn(added((one, x_long)), 0, 1)
    grad_x = added((chip[3], y_long, y_short))
    (grad_y,) = call(
        join_kernel, (first, own, x_long, x_short), [array((owned, tgt_cols))], name="grad_y"
    )
    g_start_bar = -jnp.sum(start_parts, axis=0).reshape(tgt_cols)
    return (g_start_bar, grad_x, grad_y)


def solution(mesh):
    placed = (
        P("rows", "cols"),
        P("rows"),
        P("cols"),
        P(),
        P("cols"),
        P("rows"),
        P("cols"),
        P("rows", None),
        P("cols", None),
    )
    return jax.shard_map(
        body,
        mesh=mesh,
        in_specs=placed,
        out_specs=(P("cols"), P("cols", "rows"), P("rows", "cols")),
        check_vma=False,
    )
```

```python
import functools
import math

import jax
import jax.numpy as jnp
from jax import lax
from jax.experimental import pallas as pl
from jax.experimental.pallas import tpu as pltpu
from jax.sharding import PartitionSpec as P

K = 3


EPSILON = 0.05
PENALTY = 1.0
SCALE = 1.0 / (EPSILON * math.log(2.0))
LANES = 128
STRIP = 32
REACH = 40.0
FIRST_REACH = 75.0
VMEM_BYTES = 16 * 2**20
PINNED = 2**16
F32 = jnp.float32


def eye():
    return lax.broadcasted_iota(jnp.int32, (LANES, LANES), 0) == lax.broadcasted_iota(
        jnp.int32, (LANES, LANES), 1
    )


def to_column(row):
    return jnp.sum(jnp.where(eye(), row, 0.0), axis=1, keepdims=True)


def to_row(column):
    return jnp.sum(jnp.where(eye(), column, 0.0), axis=0, keepdims=True)


def log_combined(parts):
    top = jnp.max(parts, axis=0)
    return top + jnp.log2(jnp.sum(jnp.exp2(parts - top[None]), axis=0))


def spread(copies_ref, value):
    copies_ref[...] = jnp.broadcast_to(value[None], copies_ref.shape)


def groups_of(ref):
    return ref.shape[0]


def row_sums(base_ref, weight_ref, out_ref):
    for s in range(groups_of(out_ref)):
        held = None
        for c in range(groups_of(weight_ref)):
            tile = base_ref[s * LANES : (s + 1) * LANES, c * LANES : (c + 1) * LANES]
            term = tile * weight_ref[c : c + 1, :]
            held = term if held is None else held + term
        out_ref[s : s + 1, :] = to_row(jnp.sum(held, axis=1, keepdims=True))


def col_sums(base_ref, weight_ref, out_ref):
    held = [None] * groups_of(out_ref)
    for s in range(groups_of(weight_ref)):
        column = jnp.broadcast_to(to_column(weight_ref[s : s + 1, :]), (LANES, LANES))
        for c in range(len(held)):
            tile = base_ref[s * LANES : (s + 1) * LANES, c * LANES : (c + 1) * LANES]
            term = jnp.sum((tile * column).reshape(LANES // 8, 8, LANES), axis=0)
            held[c] = term if held[c] is None else held[c] + term
    for c, term in enumerate(held):
        out_ref[c : c + 1, :] = jnp.sum(term, axis=0, keepdims=True)


def strip_logs(scores):
    highest = jnp.max(scores, axis=1, keepdims=True)
    powers = jnp.exp2(scores - highest)
    return highest, powers, highest + jnp.log2(jnp.sum(powers, axis=1, keepdims=True))


def wide(ref):
    return jnp.concatenate([ref[c : c + 1, :] for c in range(groups_of(ref))], axis=1)


def load_rows(score_ref, tile_ref, group):
    tile_ref[...] = score_ref[pl.ds(pl.multiple_of(group * LANES, LANES), LANES), :]


def slow_row_logs(score_ref, tile_ref, col_ref, out_ref):
    @pl.loop(0, groups_of(out_ref))
    def _(group):
        load_rows(score_ref, tile_ref, group)
        logs = []
        for q in range(LANES // STRIP):
            logs.append(strip_logs(tile_ref[q * STRIP : (q + 1) * STRIP, :] + wide(col_ref))[2])
        out_ref[pl.ds(group, 1), :] = to_row(jnp.concatenate(logs, axis=0))


def slow_col_logs(score_ref, tile_ref, row_ref, out_ref):
    count = groups_of(out_ref)
    tops = tuple(jnp.full((1, LANES), -1e30, F32) for _ in range(count))

    def highest(group, tops):
        load_rows(score_ref, tile_ref, group)
        column = to_column(row_ref[pl.ds(group, 1), :])
        return tuple(
            jnp.maximum(
                tops[c],
                jnp.max(
                    tile_ref[:, c * LANES : (c + 1) * LANES] + column, axis=0, keepdims=True
                ),
            )
            for c in range(count)
        )

    tops = lax.fori_loop(0, groups_of(row_ref), highest, tops)
    sums = tuple(jnp.zeros((1, LANES), F32) for _ in range(count))

    def summed(group, sums):
        load_rows(score_ref, tile_ref, group)
        column = to_column(row_ref[pl.ds(group, 1), :])
        return tuple(
            sums[c]
            + jnp.sum(
                jnp.exp2(tile_ref[:, c * LANES : (c + 1) * LANES] + column - tops[c]),
                axis=0,
                keepdims=True,
            )
            for c in range(count)
        )

    sums = lax.fori_loop(0, groups_of(row_ref), summed, sums)
    for c in range(count):
        out_ref[c : c + 1, :] = tops[c] + jnp.log2(sums[c])


def slow_row_weighted(score_ref, tile_ref, row_ref, col_ref, weight_ref, out_ref):
    @pl.loop(0, groups_of(out_ref))
    def _(group):
        load_rows(score_ref, tile_ref, group)
        column = to_column(row_ref[pl.ds(group, 1), :])
        sums = []
        for q in range(LANES // STRIP):
            part = slice(q * STRIP, (q + 1) * STRIP)
            plan = jnp.exp2(tile_ref[part, :] + column[part] + wide(col_ref))
            sums.append(jnp.sum(plan * wide(weight_ref), axis=1, keepdims=True))
        out_ref[pl.ds(group, 1), :] = to_row(jnp.concatenate(sums, axis=0))


def slow_col_weighted(score_ref, tile_ref, row_ref, col_ref, weight_ref, out_ref):
    count = groups_of(out_ref)
    sums = tuple(jnp.zeros((1, LANES), F32) for _ in range(count))

    def summed(group, sums):
        load_rows(score_ref, tile_ref, group)
        column = to_column(row_ref[pl.ds(group, 1), :])
        weight = to_column(weight_ref[pl.ds(group, 1), :])
        return tuple(
            sums[c]
            + jnp.sum(
                weight
                * jnp.exp2(
                    tile_ref[:, c * LANES : (c + 1) * LANES] + column + col_ref[c : c + 1, :]
                ),
                axis=0,
                keepdims=True,
            )
            for c in range(count)
        )

    sums = lax.fori_loop(0, groups_of(row_ref), summed, sums)
    for c in range(count):
        out_ref[c : c + 1, :] = sums[c]


def first_kernel(
    cost_hbm, src_hbm, tgt_hbm, mask_hbm, dual_hbm, score_ref, base_ref, top_ref, copies_ref,
    cost_ref, src_ref, tgt_ref, mask_ref, dual_ref, allowed_ref, log_ref, small_sem, cost_sem,
):
    small = [
        pltpu.make_async_copy(source, target, small_sem.at[at])
        for at, (source, target) in enumerate(
            ((tgt_hbm, tgt_ref), (mask_hbm, mask_ref), (src_hbm, src_ref), (dual_hbm, dual_ref))
        )
    ]
    for copy in small:
        copy.start()
    blocks = []
    for s in range(groups_of(log_ref)):
        rows = pl.ds(s * LANES, LANES)
        blocks.append(
            pltpu.make_async_copy(cost_hbm.at[rows, :], cost_ref.at[rows, :], cost_sem.at[s])
        )
        blocks[-1].start()
    for copy in small:
        copy.wait()
    classes = mask_ref.shape[0]
    mask = mask_ref[...].astype(F32).astype(jnp.bfloat16)
    ids = lax.broadcasted_iota(jnp.int32, (classes, LANES), 0)
    hot = jnp.concatenate(
        [
            jnp.where(tgt_ref[c : c + 1, :] == ids, 1.0, 0.0).astype(jnp.bfloat16)
            for c in range(groups_of(tgt_ref))
        ],
        axis=1,
    )
    allowed_of = jnp.dot(mask, hot, preferred_element_type=F32).astype(jnp.bfloat16)
    lane_ids = lax.broadcasted_iota(jnp.int32, (LANES, classes), 1).astype(F32)
    dual = wide(dual_ref) * SCALE - PENALTY * SCALE
    for s in range(groups_of(log_ref)):
        label = to_column(src_ref[s : s + 1, :].astype(F32))
        src_hot = jnp.where(label == lane_ids, 1.0, 0.0).astype(jnp.bfloat16)
        allowed_ref[...] = jnp.dot(src_hot, allowed_of, preferred_element_type=F32)
        blocks[s].wait()
        tops, logs = [], []
        for q in range(LANES // STRIP):
            rows = slice(s * LANES + q * STRIP, s * LANES + (q + 1) * STRIP)
            shifted = cost_ref[rows, :].astype(F32) - PENALTY * allowed_ref[
                q * STRIP : (q + 1) * STRIP, :
            ]
            scores = dual - shifted * SCALE
            highest, powers, log = strip_logs(scores)
            score_ref[rows, :] = scores
            base_ref[rows, :] = powers
            tops.append(highest)
            logs.append(log)
        top_ref[s : s + 1, :] = to_row(jnp.concatenate(tops, axis=0))
        log_ref[s : s + 1, :] = to_row(jnp.concatenate(logs, axis=0))
    spread(copies_ref, log_ref[...])


def rebase_kernel(
    log_target, parts_ref, score_ref, base_ref, top_ref, dual_ref, copies_ref, log_ref
):
    dual_ref[...] = log_target - log_combined(parts_ref[...])
    dual = wide(dual_ref)
    for s in range(groups_of(log_ref)):
        tops, logs = [], []
        for q in range(LANES // STRIP):
            rows = slice(s * LANES + q * STRIP, s * LANES + (q + 1) * STRIP)
            highest, powers, log = strip_logs(score_ref[rows, :] + dual)
            base_ref[rows, :] = powers
            tops.append(highest)
            logs.append(log)
        top_ref[s : s + 1, :] = to_row(jnp.concatenate(tops, axis=0))
        log_ref[s : s + 1, :] = to_row(jnp.concatenate(logs, axis=0))
    spread(copies_ref, log_ref[...])


def row_log_kernel(
    log_target, parts_ref, top_ref, base_dual_ref, base_ref, score_ref, dual_ref, copies_ref,
    weight_ref, sum_ref, tile_ref,
):
    dual_ref[...] = log_target - log_combined(parts_ref[...])
    lead = dual_ref[...] - base_dual_ref[...]
    near = jnp.max(jnp.abs(lead)) <= REACH

    @pl.when(near)
    def _():
        weight_ref[...] = jnp.exp2(lead)
        row_sums(base_ref, weight_ref, sum_ref)
        sum_ref[...] = top_ref[...] + jnp.log2(sum_ref[...])

    @pl.when(jnp.logical_not(near))
    def _():
        slow_row_logs(score_ref, tile_ref, dual_ref, sum_ref)

    spread(copies_ref, sum_ref[...])


def col_log_kernel(
    log_source, parts_ref, top_ref, base_dual_ref, base_ref, score_ref, dual_ref, copies_ref,
    weight_ref, sum_ref, tile_ref,
):
    dual_ref[...] = log_source - log_combined(parts_ref[...])
    lead = dual_ref[...] + top_ref[...]
    weight_ref[...] = jnp.exp2(jnp.minimum(lead, 100.0))
    col_sums(base_ref, weight_ref, sum_ref)
    most = jnp.max(lead)
    near = jnp.logical_and(
        most <= 60.0,
        jnp.min(jnp.log2(jnp.maximum(sum_ref[...], 1e-37))) >= jnp.maximum(most, -15.0) - 85.0,
    )

    @pl.when(near)
    def _():
        sum_ref[...] = jnp.log2(sum_ref[...]) - base_dual_ref[...]

    @pl.when(jnp.logical_not(near))
    def _():
        slow_col_logs(score_ref, tile_ref, dual_ref, sum_ref)

    spread(copies_ref, sum_ref[...])


def row_plan_kernel(
    log_target, first, parts_ref, grad_ref, dual_in_ref, row_dual_ref, top_ref, base_dual_ref,
    base_ref, score_ref, after_ref, out_ref, copies_ref, weight_ref, col_ref, sum_ref, tile_ref,
):
    if first:
        dual = log_target - log_combined(parts_ref[...])
        grad = grad_ref[...]
        out_ref[...] = dual
    else:
        dual = dual_in_ref[...]
        grad = -jnp.sum(parts_ref[...], axis=0)
        out_ref[...] = grad
    lead = dual - base_dual_ref[...]
    row_lead = row_dual_ref[...] + top_ref[...]
    near = jnp.logical_and(jnp.max(jnp.abs(lead)) <= REACH, jnp.max(row_lead) <= 60.0)

    @pl.when(near)
    def _():
        weight_ref[...] = jnp.exp2(lead - log_target) * grad
        row_sums(base_ref, weight_ref, sum_ref)
        sum_ref[...] = sum_ref[...] * jnp.exp2(row_lead)

    @pl.when(jnp.logical_not(near))
    def _():
        col_ref[...] = dual - log_target
        weight_ref[...] = grad
        slow_row_weighted(score_ref, tile_ref, row_dual_ref, col_ref, weight_ref, sum_ref)

    spread(copies_ref, sum_ref[...])


def col_plan_kernel(
    log_source, parts_ref, outer_ref, dual_ref, row_dual_ref, top_ref, base_dual_ref, base_ref,
    score_ref, out_ref, copies_ref, weight_ref, col_ref, sum_ref, tile_ref,
):
    grad = outer_ref[...] - jnp.sum(parts_ref[...], axis=0)
    out_ref[...] = grad
    lead = dual_ref[...] - base_dual_ref[...]
    row_lead = row_dual_ref[...] + top_ref[...]
    near = jnp.logical_and(jnp.max(jnp.abs(lead)) <= REACH, jnp.max(row_lead) <= 60.0)

    @pl.when(near)
    def _():
        weight_ref[...] = jnp.exp2(row_lead) * grad
        col_sums(base_ref, weight_ref, sum_ref)
        sum_ref[...] = sum_ref[...] * jnp.exp2(lead - log_source)

    @pl.when(jnp.logical_not(near))
    def _():
        col_ref[...] = dual_ref[...] - log_source
        weight_ref[...] = grad
        slow_col_weighted(score_ref, tile_ref, row_dual_ref, col_ref, weight_ref, sum_ref)

    spread(copies_ref, sum_ref[...])


def turn_kernel(emb_hbm, after_ref, out_ref, emb_ref, sem):
    strips = [slice(at, at + LANES) for at in range(0, emb_ref.shape[0], LANES)]
    copies = [
        pltpu.make_async_copy(
            emb_hbm.at[pl.ds(at * LANES, LANES), :], emb_ref.at[pl.ds(at * LANES, LANES), :], sem.at[at]
        )
        for at in range(len(strips))
    ]
    for copy in copies:
        copy.start()
    for copy, strip in zip(copies, strips):
        copy.wait()
        out_ref[:, strip] = emb_ref[strip, :].T


def is_near(dual_refs, row_refs, top_ref, base_dual_ref):
    near = None
    for ref in dual_refs:
        test = jnp.max(jnp.abs(ref[...] - base_dual_ref[...])) <= REACH
        near = test if near is None else jnp.logical_and(near, test)
    for ref in row_refs:
        near = jnp.logical_and(near, jnp.max(ref[...] + top_ref[...]) <= 60.0)
    return near


def most_grad_kernel(
    log_source, log_target,
    row1, row2, row3, col1, col2, col3, fbar2, fbar3, gbar1, gbar2, gbar3, top_ref, base_ref,
    score_ref, out_ref, rows_ref, cols_ref, tile_ref,
):
    near = is_near((col2, col3), (row1, row2, row3), top_ref, col1)
    count = groups_of(col1)

    @pl.when(near)
    def _():
        for k, row in enumerate((row1, row2, row3)):
            rows_ref[k] = -jnp.exp2(row[...] + top_ref[...])
        rows_ref[3] = rows_ref[1] * fbar2[...]
        rows_ref[4] = rows_ref[2] * fbar3[...]
        leads = [jnp.zeros_like(col1), col2[...] - col1[...], col3[...] - col1[...]]
        for k, grad in enumerate((gbar1, gbar2, gbar3)):
            cols_ref[k] = jnp.exp2(leads[k] - log_target) * grad[...]
        for k in range(2):
            cols_ref[3 + k] = jnp.exp2(leads[k] - log_source)
        for s in range(groups_of(row1)):
            columns = [to_column(rows_ref[k, s : s + 1, :]) for k in range(5)]
            for q in range(LANES // STRIP):
                rows = slice(s * LANES + q * STRIP, s * LANES + (q + 1) * STRIP)
                strips = [
                    jnp.broadcast_to(part[q * STRIP : (q + 1) * STRIP], (STRIP, LANES))
                    for part in columns
                ]
                for c in range(count):
                    lanes = slice(c * LANES, (c + 1) * LANES)
                    weight = strips[0] * cols_ref[0, c : c + 1, :]
                    for k in range(1, 5):
                        weight = weight + strips[k] * cols_ref[k, c : c + 1, :]
                    out_ref[rows, lanes] = base_ref[rows, lanes] * weight

    @pl.when(jnp.logical_not(near))
    def _():
        for k, row in enumerate((row1, row2, row3)):
            rows_ref[k] = row[...]
        rows_ref[3] = fbar2[...]
        rows_ref[4] = fbar3[...]
        for k, col in enumerate((col1, col2, col3)):
            cols_ref[k] = col[...]
        for k, grad in enumerate((gbar1, gbar2, gbar3)):
            cols_ref[3 + k] = grad[...]

        @pl.loop(0, groups_of(row1))
        def _(group):
            load_rows(score_ref, tile_ref, group)
            columns = [to_column(rows_ref[k, pl.ds(group, 1), :]) for k in range(5)]
            for c in range(count):
                lanes = slice(c * LANES, (c + 1) * LANES)
                value = jnp.zeros((LANES, LANES), F32)
                for k in reversed(range(3)):
                    scores = tile_ref[:, lanes] + columns[k]
                    plan_q = jnp.exp2(scores + (cols_ref[k, c : c + 1, :] - log_target))
                    value = value + plan_q * cols_ref[3 + k, c : c + 1, :]
                    if k:
                        plan_r = jnp.exp2(scores + (cols_ref[k - 1, c : c + 1, :] - log_source))
                        value = value + plan_r * columns[2 + k]
                start = pl.multiple_of(group * LANES, LANES)
                out_ref[pl.ds(start, LANES), lanes] = -value


def direction(place_ref):
    return 1 - 2 * place_ref[3]


def ring_place(place_ref, axis, offset, count):
    return lax.rem(place_ref[axis] + direction(place_ref) * offset + count, count)


def z_block(place_ref, src_ref, grad_ref, offset, counts):
    x_count, z_count = counts
    width, half = src_ref.shape[0], grad_ref.shape[1] // 2
    owned = width // (x_count * z_count)
    at = ring_place(place_ref, 2, offset, z_count)
    rows = [
        src_ref[pl.ds(pl.multiple_of((x * z_count + at) * owned, owned), owned), :]
        for x in range(x_count)
    ]
    return jnp.dot(
        jnp.concatenate(rows, axis=0), grad_ref[:, half:], preferred_element_type=F32
    )


def x_block(place_ref, src_ref, grad_ref, offset, counts):
    x_count = counts[0]
    width, half = src_ref.shape[0], grad_ref.shape[1] // 2
    owned = width // x_count
    at = ring_place(place_ref, 0, offset, x_count)
    rows = src_ref[pl.ds(pl.multiple_of(at * owned, owned), owned), :]
    return jnp.dot(rows, grad_ref[:, :half], preferred_element_type=F32)


def grad_kernel(
    log_source, counts, place_ref, parts_ref, row1, col1, top_ref, base_ref, most_ref, src_ref,
    score_ref, out_ref, start_ref, z_far_ref, x_far_ref, rows_ref, cols_ref, tile_ref,
):
    fbar1 = -jnp.sum(parts_ref[...], axis=0)
    row_lead = row1[...] + top_ref[...]
    near = jnp.logical_and(jnp.max(jnp.abs(col1[...])) <= FIRST_REACH, jnp.max(row_lead) <= 60.0)
    count = groups_of(col1)

    @pl.when(near)
    def _():
        rows_ref[...] = -jnp.exp2(row_lead) * fbar1
        cols_ref[...] = jnp.exp2(-col1[...] - log_source)
        held = [None] * count
        for s in range(groups_of(row1)):
            column = jnp.broadcast_to(to_column(rows_ref[s : s + 1, :]), (LANES, LANES))
            rows = slice(s * LANES, (s + 1) * LANES)
            for c in range(count):
                lanes = slice(c * LANES, (c + 1) * LANES)
                term = base_ref[rows, lanes] * column * cols_ref[c : c + 1, :]
                out_ref[rows, lanes] = (most_ref[rows, lanes] + term).astype(jnp.bfloat16)
                term = jnp.sum(term.reshape(LANES // 8, 8, LANES), axis=0)
                held[c] = term if held[c] is None else held[c] + term
        for c, term in enumerate(held):
            start_ref[c : c + 1, :] = jnp.sum(term, axis=0, keepdims=True)

    @pl.when(jnp.logical_not(near))
    def _():
        rows_ref[...] = -fbar1
        start_ref[...] = jnp.zeros_like(start_ref)

        @pl.loop(0, groups_of(row1))
        def _(group):
            load_rows(score_ref, tile_ref, group)
            column = to_column(row1[pl.ds(group, 1), :]) - log_source
            weight = to_column(rows_ref[pl.ds(group, 1), :])
            rows = pl.ds(pl.multiple_of(group * LANES, LANES), LANES)
            for c in range(count):
                lanes = slice(c * LANES, (c + 1) * LANES)
                term = jnp.exp2(tile_ref[:, lanes] + column) * weight
                out_ref[rows, lanes] = (most_ref[rows, lanes] + term).astype(jnp.bfloat16)
                start_ref[c : c + 1, :] += jnp.sum(term, axis=0, keepdims=True)

    x_far_ref[...] = x_block(place_ref, src_ref, out_ref, counts[0] // 2, counts)
    put(z_far_ref, z_block(place_ref, src_ref, out_ref, counts[1] // 2, counts), start_ref[...])


def put(out_ref, block, rider):
    rows = block.shape[0]
    out_ref[:rows, :] = block
    out_ref[rows:, :] = jnp.zeros_like(out_ref[rows:, :])
    out_ref[rows:, :LANES] = rider


def rider(ref):
    return ref[ref.shape[0] - 8 :, :LANES]


def x_part_kernel(y_count, place_ref, grad_ref, tgt_ref, sent_ref, kept_ref, order_ref):
    block = tgt_ref.shape[0] // (2 * y_count)
    core, turn = place_ref[3], direction(place_ref)
    for side, out_ref in ((0, sent_ref), (1, kept_ref)):
        for k, offset in enumerate((2, 1, -1, 0)):
            step = offset * (2 * side - 1)
            at = lax.rem(place_ref[1] + turn * step + y_count, y_count)
            owner = at * 2 + (core if side else 1 - core)
            order_ref[k * block : (k + 1) * block, :] = tgt_ref[
                pl.ds(pl.multiple_of(owner * block, block), block), :
            ]
        product = lax.dot_general(
            order_ref[...], grad_ref[...], (((1,), (1,)), ((), ())), preferred_element_type=F32
        )
        out_ref[...] = product.reshape(out_ref.shape)


def y_parts_kernel(counts, place_ref, grad_ref, src_ref, start_ref, after_ref, *outs):
    x_outs, z_outs = outs[:3], outs[3:]
    for out_ref, offset in zip(x_outs, (-1, 1, 0)):
        out_ref[...] = x_block(place_ref, src_ref, grad_ref, offset, counts)
    reach = counts[1] // 2
    offsets = [1 - reach, *range(reach - 1, 0, -1), *range(2 - reach, 1)]
    for out_ref, offset in zip(z_outs, offsets):
        block = z_block(place_ref, src_ref, grad_ref, offset, counts)
        if offset == 1 - reach:
            put(out_ref, block, start_ref[...])
        else:
            out_ref[...] = block


def add_kernel(count, *refs):
    value = refs[0][...]
    for ref in refs[1:count]:
        value = value + ref[...]
    out_ref, token_ref = refs[-2:]
    out_ref[...] = value
    token_ref[...] = jnp.zeros_like(token_ref)


def pair_kernel(one_ref, up_ref, own_ref, down_ref, after_ref, pay_ref, sum_ref, token_ref):
    pay_ref[...] = one_ref[...] + up_ref[...]
    sum_ref[...] = own_ref[...] + down_ref[...]
    token_ref[...] = jnp.zeros_like(token_ref)


def pass_kernel(block_ref, arrived_ref, held_ref, after_ref, out_ref, sum_ref):
    rows = block_ref.shape[0]
    out_ref[:rows, :] = block_ref[...] + arrived_ref[:rows, :]
    out_ref[rows:, :] = arrived_ref[rows:, :]
    sum_ref[...] = held_ref[...] + rider(arrived_ref)


def chip_kernel(kept_ref, arrived_ref, after_ref, *outs):
    for k, out_ref in enumerate(outs[:-1]):
        out_ref[...] = kept_ref[k] + arrived_ref[k]
    outs[-1][...] = jnp.zeros_like(outs[-1])


def split_kernel(
    x_count, place_ref, own_ref, up_ref, down_ref, held_up_ref, held_down_ref, after_ref, far_ref,
    back_ref, one_ref, last_ref, start_ref,
):
    start_ref[...] = (
        held_up_ref[...] + held_down_ref[...] + rider(up_ref) + rider(down_ref)
    )
    block = own_ref.shape[0] // x_count
    for out_ref, offset in ((far_ref, 2), (back_ref, -1), (one_ref, 1), (last_ref, 0)):
        at = ring_place(place_ref, 0, offset, x_count)
        rows = pl.ds(pl.multiple_of(at * block, block), block)
        value = own_ref[rows, :] + up_ref[rows, :] + down_ref[rows, :]
        if offset in (2, -1):
            put(out_ref, value, start_ref[...])
        else:
            out_ref[...] = value


def join_kernel(parts_ref, own_ref, up_ref, down_ref, held_ref, out_ref, start_ref):
    rows, half = own_ref.shape
    out_ref[:, :half] = jnp.sum(parts_ref[...], axis=0)
    out_ref[:, half:] = own_ref[...] + up_ref[:rows, :] + down_ref[:rows, :]
    start_ref[...] = held_ref[...] + rider(up_ref) + rider(down_ref)


def call(
    kernel, arguments, outs, scratch=(), in_hbm=(), loose=(), in_smem=(), last=False, name=None
):
    spaces, values = [], []
    for at, value in enumerate(arguments):
        space = pltpu.VMEM
        if at in in_hbm:
            space = pltpu.HBM
        elif at in loose:
            space = pl.ANY
        elif at in in_smem:
            space = pltpu.SMEM
        if at in in_hbm or (space is pltpu.VMEM and value.size >= PINNED):
            value = pltpu.with_memory_space_constraint(value, space)
        spaces.append(space)
        values.append(value)
    return pl.pallas_call(
        kernel,
        out_shape=[
            pltpu.VMEM(out.shape, out.dtype) if math.prod(out.shape) >= PINNED and not last else out
            for out in outs
        ],
        in_specs=[pl.BlockSpec(memory_space=space) for space in spaces],
        out_specs=[pl.BlockSpec(memory_space=pltpu.VMEM)] * len(outs),
        scratch_shapes=list(scratch),
        compiler_params=pltpu.CompilerParams(vmem_limit_bytes=VMEM_BYTES),
        name=name,
    )(*values)


def exchanged(copies, axis):
    return lax.all_to_all(copies, axis, 0, 0, tiled=True)


def token():
    return jax.ShapeDtypeStruct((8, LANES), F32)


def added(values, after, last=False):
    return call(
        functools.partial(add_kernel, len(values)),
        (*values, after),
        [jax.ShapeDtypeStruct(values[0].shape, F32), token()],
        loose=(len(values),),
        last=last,
        name="added",
    )


def paired(one, up, own, down, after):
    shape = jax.ShapeDtypeStruct(one.shape, F32)
    return call(
        pair_kernel, (one, up, own, down, after), [shape, shape, token()], loose=(4,), name="paired"
    )


def passed(block, arrived, held, after):
    return call(
        pass_kernel,
        (block, arrived, held, after),
        [jax.ShapeDtypeStruct(arrived.shape, F32), token()],
        loose=(3,),
        name="passed",
    )


def body(cost, src_label, tgt_label, class_mask, g_start, f_bar, g_bar, src_emb, tgt_emb):
    row_count = lax.axis_size("rows")
    col_count = lax.axis_size("cols")
    src_rows, tgt_cols = cost.shape
    width = src_emb.shape[1]
    log_source = -math.log2(src_rows * row_count)
    log_target = -math.log2(tgt_cols * col_count)
    row_shape = (src_rows // LANES, LANES)
    col_shape = (tgt_cols // LANES, LANES)
    src_label, f_bar = src_label.reshape(row_shape), f_bar.reshape(row_shape)
    tgt_label, g_bar = tgt_label.reshape(col_shape), g_bar.reshape(col_shape)
    g_start = g_start.reshape(col_shape)

    def array(shape, dtype=F32):
        return jax.ShapeDtypeStruct(shape, dtype)

    matrix = array(cost.shape)
    row_vector, col_vector = array(row_shape), array(col_shape)
    row_copies = array((col_count,) + row_shape)
    col_copies = array((row_count,) + col_shape)
    row_held, col_held = pltpu.VMEM(row_shape, F32), pltpu.VMEM(col_shape, F32)
    slow = [pltpu.VMEM((LANES, tgt_cols), F32)]

    score, start_base, start_top, copies = call(
        first_kernel,
        (cost, src_label, tgt_label, class_mask, g_start),
        [matrix, matrix, row_vector, row_copies],
        [
            pltpu.VMEM(cost.shape, cost.dtype),
            pltpu.VMEM(row_shape, jnp.int32),
            pltpu.VMEM(col_shape, jnp.int32),
            pltpu.VMEM(class_mask.shape, jnp.int32),
            col_held,
            pltpu.VMEM((LANES, tgt_cols), F32),
            row_held,
            pltpu.SemaphoreType.DMA((4,)),
            pltpu.SemaphoreType.DMA(row_shape[:1]),
        ],
        in_hbm=range(5),
        name="first_row_logs",
    )

    def col_logs(parts, top, base_dual, base):
        return call(
            functools.partial(col_log_kernel, log_source),
            (parts, top, base_dual, base, score),
            [row_vector, col_copies],
            [row_held, col_held] + slow,
                name="col_logs",
        )

    zero = jnp.zeros(col_shape, F32)
    row1, copies = col_logs(exchanged(copies, "cols"), start_top, zero, start_base)
    base, top, col1, copies = call(
        functools.partial(rebase_kernel, log_target),
        (exchanged(copies, "rows"), score),
        [matrix, row_vector, col_vector, row_copies],
        [row_held],
        name="second_row_logs",
    )
    row2, copies = col_logs(exchanged(copies, "cols"), top, col1, base)
    col2, copies = call(
        functools.partial(row_log_kernel, log_target),
        (exchanged(copies, "rows"), top, col1, base, score),
        [col_vector, row_copies],
        [col_held, row_held] + slow,
        name="third_row_logs",
    )
    row3, copies = col_logs(exchanged(copies, "cols"), top, col1, base)

    def row_plan(first, parts, grad, dual, row, after):
        return call(
            functools.partial(row_plan_kernel, log_target, first),
            (parts, grad, dual, row, top, col1, base, score, after),
            [col_vector, row_copies],
            [col_held, col_held, row_held] + slow,
            loose=(8,),
                name="row_plan",
        )

    def col_plan(parts, outer, dual, row):
        return call(
            functools.partial(col_plan_kernel, log_source),
            (parts, outer, dual, row, top, col1, base, score),
            [row_vector, col_copies],
            [row_held, col_held, col_held] + slow,
                name="col_plan",
        )

    none = jnp.zeros(row_shape, F32)

    def turned(emb, after):
        return call(
            turn_kernel,
            (emb, after),
            [array(emb.shape[::-1], emb.dtype)],
            [pltpu.VMEM(emb.shape, emb.dtype), pltpu.SemaphoreType.DMA((emb.shape[0] // LANES,))],
            in_hbm=(0,),
            loose=(1,),
            name="turned",
        )[0]

    col3, copies = row_plan(True, exchanged(copies, "rows"), g_bar, col2, row3, g_bar)
    fbar3, copies = col_plan(exchanged(copies, "cols"), f_bar, col2, row3)
    src_turned = turned(src_emb, copies)
    gbar2, copies = row_plan(False, exchanged(copies, "rows"), g_bar, col2, row2, src_turned)
    fbar2, copies = col_plan(exchanged(copies, "cols"), none, col1, row2)
    tgt_turned = turned(tgt_emb, copies)
    gbar1, copies = row_plan(False, exchanged(copies, "rows"), g_bar, col1, row1, tgt_turned)
    parts = exchanged(copies, "cols")
    (most,) = call(
        functools.partial(most_grad_kernel, log_source, log_target),
        (
            row1, row2, row3, col1, col2, col3, fbar2, fbar3, gbar1, gbar2, g_bar, top, base, score,
        ),
        [matrix],
        [pltpu.VMEM((5,) + row_shape, F32), pltpu.VMEM((6,) + col_shape, F32)] + slow,
        name="most_cost_grad",
    )
    x_count, z_count, y_count = 4, row_count // 4, col_count // 2
    counts = (x_count, z_count)
    owned = width // row_count
    row_at, col_at = lax.axis_index("rows"), lax.axis_index("cols")
    place = jnp.stack(
        [row_at // z_count, col_at // 2, row_at % z_count, col_at % 2]
    ).astype(jnp.int32)
    devices = [
        (x, y, z, core)
        for x in range(x_count)
        for y in range(y_count)
        for z in range(z_count)
        for core in range(2)
    ]

    def number(x, y, z, core):
        spot = (x % x_count * z_count + z % z_count) * y_count + y % y_count
        return spot * 2 + core

    def turn(value, axis, step):
        moves = []
        for device in devices:
            ahead = list(device)
            ahead[axis] += step * (1 - 2 * device[3])
            moves.append((number(*device), number(*ahead)))
        return lax.ppermute(value, ("rows", "cols"), moves)

    half = tgt_cols // 2
    z_rows, x_rows = x_count * owned, z_count * owned
    z_shape, z_riding = array((z_rows, half)), array((z_rows + 8, half))
    x_shape = array((x_rows, half))
    rounded, start, z_far, x_far = call(
        functools.partial(grad_kernel, log_source, counts),
        (place, parts, row1, col1, top, base, most, src_turned, score),
        [array(cost.shape, jnp.bfloat16), col_vector, z_riding, x_shape],
        [row_held, col_held] + slow,
        in_smem=(0,),
        name="cost_grad",
    )
    z_up = turn(z_far, 2, 1)
    x_up = turn(x_far, 0, 1)
    chip_part = array((y_count, width // col_count, src_rows))
    sent, kept = call(
        functools.partial(x_part_kernel, y_count),
        (place, rounded, tgt_turned),
        [chip_part, chip_part],
        [pltpu.VMEM((width // 2, tgt_cols), jnp.bfloat16)],
        in_smem=(0,),
        name="grad_x_parts",
    )
    arrived = lax.ppermute(sent, "cols", [(at, at ^ 1) for at in range(col_count)])
    outs = call(
        functools.partial(y_parts_kernel, counts),
        (place, rounded, src_turned, start, kept),
        [x_shape] * 3 + [z_riding] + [z_shape] * (z_count - 2),
        in_smem=(0,),
        loose=(4,),
        name="grad_y_parts",
    )
    x_back, x_one, x_own, z_back, z_3, z_2, z_1, z_back2, z_back1, z_own = outs
    x_down = turn(x_back, 0, -1)
    z_down = turn(z_back, 2, -1)
    z_pay, up_held = passed(z_3, z_up, start, start)
    z_up = turn(z_pay, 2, 1)
    far, one, back, own = (array((width // col_count, src_rows)) for _ in range(4))
    far, one, back, own, mark = call(
        chip_kernel,
        (kept, arrived, up_held),
        [far, one, back, own, token()],
        loose=(2,),
        name="chip_sums",
    )
    y_up, y_down = turn(far, 1, 1), turn(back, 1, -1)
    z_pay, down_held = passed(z_back2, z_down, jnp.zeros_like(start), mark)
    z_down = turn(z_pay, 2, -1)
    x_pay, x_sum, mark = paired(x_one, x_up, x_own, x_down, down_held)
    x_up = turn(x_pay, 0, 1)
    z_pay, up_held = passed(z_2, z_up, up_held, mark)
    z_up = turn(z_pay, 2, 1)
    z_pay, down_held = passed(z_back1, z_down, down_held, up_held)
    z_down = turn(z_pay, 2, -1)
    y_pay, y_sum, mark = paired(one, y_up, own, y_down, down_held)
    y_up = turn(y_pay, 1, 1)
    first, mark = added((x_sum, x_up), mark)
    along_z = [[x * z_count + z for z in range(z_count)] for x in range(x_count)]
    first = lax.all_to_all(
        first.reshape(z_count, owned, half), "rows", 0, 0, tiled=True, axis_index_groups=along_z
    )
    z_pay, up_held = passed(z_1, z_up, up_held, mark)
    z_up = turn(z_pay, 2, 1)
    grad_x, mark = added((y_sum, y_up), up_held, last=True)
    last, riding = array((owned, half)), array((owned + 8, half))
    x_far, x_back, x_one, x_own, start = call(
        functools.partial(split_kernel, x_count),
        (place, z_own, z_up, z_down, up_held, down_held, mark),
        [riding, riding, last, last, col_vector],
        in_smem=(0,),
        loose=(6,),
        name="second_half",
    )
    x_up, x_down = turn(x_far, 0, 1), turn(x_back, 0, -1)
    x_pay, start = passed(x_one, x_up, start, start)
    x_up = turn(x_pay, 0, 1)
    grad_y, start = call(
        join_kernel,
        (first, x_own, x_up, x_down, start),
        [array((owned, tgt_cols)), col_vector],
        name="grad_y",
    )
    g_start_bar = start.reshape(tgt_cols)
    return (g_start_bar, grad_x, grad_y)


def solution(mesh):
    placed = (
        P("rows", "cols"),
        P("rows"),
        P("cols"),
        P(),
        P("cols"),
        P("rows"),
        P("cols"),
        P("rows", None),
        P("cols", None),
    )
    return jax.shard_map(
        body,
        mesh=mesh,
        in_specs=placed,
        out_specs=(P("cols"), P("cols", "rows"), P("rows", "cols")),
        check_vma=False,
    )
```

```python
import functools
import math

import jax
import jax.numpy as jnp
from jax import lax
from jax.experimental import pallas as pl
from jax.experimental.pallas import tpu as pltpu
from jax.sharding import PartitionSpec as P

K = 3


EPSILON = 0.05
PENALTY = 1.0
SCALE = 1.0 / (EPSILON * math.log(2.0))
LANES = 128
STRIP = 32
REACH = 40.0
FIRST_REACH = 75.0
VMEM_BYTES = 16 * 2**20
PINNED = 2**16
BIG = 2**32
F32 = jnp.float32


def eye():
    return lax.broadcasted_iota(jnp.int32, (LANES, LANES), 0) == lax.broadcasted_iota(
        jnp.int32, (LANES, LANES), 1
    )


def to_column(row):
    return jnp.sum(jnp.where(eye(), row, 0.0), axis=1, keepdims=True)


def to_row(column):
    return jnp.sum(jnp.where(eye(), column, 0.0), axis=0, keepdims=True)


def log_combined(parts):
    top = jnp.max(parts, axis=0)
    return top + jnp.log2(jnp.sum(jnp.exp2(parts - top[None]), axis=0))


def spread(copies_ref, value):
    copies_ref[...] = jnp.broadcast_to(value[None], copies_ref.shape)


def groups_of(ref):
    return ref.shape[0]


def row_sums(base_ref, weight_ref, out_ref):
    for s in range(groups_of(out_ref)):
        held = None
        for c in range(groups_of(weight_ref)):
            tile = base_ref[s * LANES : (s + 1) * LANES, c * LANES : (c + 1) * LANES]
            term = tile * weight_ref[c : c + 1, :]
            held = term if held is None else held + term
        out_ref[s : s + 1, :] = to_row(jnp.sum(held, axis=1, keepdims=True))


def col_sums(base_ref, weight_ref, out_ref):
    held = [None] * groups_of(out_ref)
    for s in range(groups_of(weight_ref)):
        column = jnp.broadcast_to(to_column(weight_ref[s : s + 1, :]), (LANES, LANES))
        for c in range(len(held)):
            tile = base_ref[s * LANES : (s + 1) * LANES, c * LANES : (c + 1) * LANES]
            term = jnp.sum((tile * column).reshape(LANES // 8, 8, LANES), axis=0)
            held[c] = term if held[c] is None else held[c] + term
    for c, term in enumerate(held):
        out_ref[c : c + 1, :] = jnp.sum(term, axis=0, keepdims=True)


def strip_logs(scores):
    highest = jnp.max(scores, axis=1, keepdims=True)
    powers = jnp.exp2(scores - highest)
    return highest, powers, highest + jnp.log2(jnp.sum(powers, axis=1, keepdims=True))


def wide(ref):
    return jnp.concatenate([ref[c : c + 1, :] for c in range(groups_of(ref))], axis=1)


def load_rows(score_ref, tile_ref, group):
    tile_ref[...] = score_ref[pl.ds(pl.multiple_of(group * LANES, LANES), LANES), :]


def slow_row_logs(score_ref, tile_ref, col_ref, out_ref):
    @pl.loop(0, groups_of(out_ref))
    def _(group):
        load_rows(score_ref, tile_ref, group)
        logs = []
        for q in range(LANES // STRIP):
            logs.append(strip_logs(tile_ref[q * STRIP : (q + 1) * STRIP, :] + wide(col_ref))[2])
        out_ref[pl.ds(group, 1), :] = to_row(jnp.concatenate(logs, axis=0))


def slow_col_logs(score_ref, tile_ref, row_ref, out_ref):
    count = groups_of(out_ref)
    tops = tuple(jnp.full((1, LANES), -1e30, F32) for _ in range(count))

    def highest(group, tops):
        load_rows(score_ref, tile_ref, group)
        column = to_column(row_ref[pl.ds(group, 1), :])
        return tuple(
            jnp.maximum(
                tops[c],
                jnp.max(
                    tile_ref[:, c * LANES : (c + 1) * LANES] + column, axis=0, keepdims=True
                ),
            )
            for c in range(count)
        )

    tops = lax.fori_loop(0, groups_of(row_ref), highest, tops)
    sums = tuple(jnp.zeros((1, LANES), F32) for _ in range(count))

    def summed(group, sums):
        load_rows(score_ref, tile_ref, group)
        column = to_column(row_ref[pl.ds(group, 1), :])
        return tuple(
            sums[c]
            + jnp.sum(
                jnp.exp2(tile_ref[:, c * LANES : (c + 1) * LANES] + column - tops[c]),
                axis=0,
                keepdims=True,
            )
            for c in range(count)
        )

    sums = lax.fori_loop(0, groups_of(row_ref), summed, sums)
    for c in range(count):
        out_ref[c : c + 1, :] = tops[c] + jnp.log2(sums[c])


def slow_row_weighted(score_ref, tile_ref, row_ref, col_ref, weight_ref, out_ref):
    @pl.loop(0, groups_of(out_ref))
    def _(group):
        load_rows(score_ref, tile_ref, group)
        column = to_column(row_ref[pl.ds(group, 1), :])
        sums = []
        for q in range(LANES // STRIP):
            part = slice(q * STRIP, (q + 1) * STRIP)
            plan = jnp.exp2(tile_ref[part, :] + column[part] + wide(col_ref))
            sums.append(jnp.sum(plan * wide(weight_ref), axis=1, keepdims=True))
        out_ref[pl.ds(group, 1), :] = to_row(jnp.concatenate(sums, axis=0))


def slow_col_weighted(score_ref, tile_ref, row_ref, col_ref, weight_ref, out_ref):
    count = groups_of(out_ref)
    sums = tuple(jnp.zeros((1, LANES), F32) for _ in range(count))

    def summed(group, sums):
        load_rows(score_ref, tile_ref, group)
        column = to_column(row_ref[pl.ds(group, 1), :])
        weight = to_column(weight_ref[pl.ds(group, 1), :])
        return tuple(
            sums[c]
            + jnp.sum(
                weight
                * jnp.exp2(
                    tile_ref[:, c * LANES : (c + 1) * LANES] + column + col_ref[c : c + 1, :]
                ),
                axis=0,
                keepdims=True,
            )
            for c in range(count)
        )

    sums = lax.fori_loop(0, groups_of(row_ref), summed, sums)
    for c in range(count):
        out_ref[c : c + 1, :] = sums[c]


def first_kernel(
    cost_hbm, src_hbm, tgt_hbm, mask_hbm, dual_hbm, emb_hbm, place_ref, score_ref, base_ref, top_ref,
    copies_ref, turned_ref, cost_ref, src_ref, tgt_ref, mask_ref, dual_ref, emb_ref, allowed_ref,
    log_ref, small_sem, cost_sem, emb_sem,
):
    small = [
        pltpu.make_async_copy(source, target, small_sem.at[at])
        for at, (source, target) in enumerate(
            ((tgt_hbm, tgt_ref), (mask_hbm, mask_ref), (src_hbm, src_ref), (dual_hbm, dual_ref))
        )
    ]
    for copy in small:
        copy.start()
    blocks = []
    for s in range(groups_of(log_ref)):
        rows = pl.ds(s * LANES, LANES)
        blocks.append(
            pltpu.make_async_copy(cost_hbm.at[rows, :], cost_ref.at[rows, :], cost_sem.at[s])
        )
        blocks[-1].start()
    embs = []
    for s in range(emb_ref.shape[0] // LANES):
        rows = pl.ds(s * LANES, LANES)
        embs.append(pltpu.make_async_copy(emb_hbm.at[rows, :], emb_ref.at[rows, :], emb_sem.at[s]))
        embs[-1].start()
    for copy in small:
        copy.wait()
    classes = mask_ref.shape[0]
    mask = mask_ref[...].astype(F32).astype(jnp.bfloat16)
    ids = lax.broadcasted_iota(jnp.int32, (classes, LANES), 0)
    hot = jnp.concatenate(
        [
            jnp.where(tgt_ref[c : c + 1, :] == ids, 1.0, 0.0).astype(jnp.bfloat16)
            for c in range(groups_of(tgt_ref))
        ],
        axis=1,
    )
    allowed_of = jnp.dot(mask, hot, preferred_element_type=F32).astype(jnp.bfloat16)
    lane_ids = lax.broadcasted_iota(jnp.int32, (LANES, classes), 1).astype(F32)
    dual = wide(dual_ref) * SCALE - PENALTY * SCALE
    for s in range(groups_of(log_ref)):
        label = to_column(src_ref[s : s + 1, :].astype(F32))
        src_hot = jnp.where(label == lane_ids, 1.0, 0.0).astype(jnp.bfloat16)
        allowed_ref[...] = jnp.dot(src_hot, allowed_of, preferred_element_type=F32)
        blocks[s].wait()
        tops, logs = [], []
        for q in range(LANES // STRIP):
            rows = slice(s * LANES + q * STRIP, s * LANES + (q + 1) * STRIP)
            shifted = cost_ref[rows, :].astype(F32) - PENALTY * allowed_ref[
                q * STRIP : (q + 1) * STRIP, :
            ]
            scores = dual - shifted * SCALE
            highest, powers, log = strip_logs(scores)
            score_ref[rows, :] = scores
            base_ref[rows, :] = powers
            tops.append(highest)
            logs.append(log)
        top_ref[s : s + 1, :] = to_row(jnp.concatenate(tops, axis=0))
        log_ref[s : s + 1, :] = to_row(jnp.concatenate(logs, axis=0))
    spread(copies_ref, log_ref[...])
    for s, copy in enumerate(embs):
        copy.wait()
        rows = slice(s * LANES, (s + 1) * LANES)
        turned_ref[:, rows] = emb_ref[rows, :].T


def rebase_kernel(
    log_target, parts_ref, score_ref, base_ref, top_ref, dual_ref, copies_ref, log_ref
):
    dual_ref[...] = log_target - log_combined(parts_ref[...])
    dual = wide(dual_ref)
    for s in range(groups_of(log_ref)):
        tops, logs = [], []
        for q in range(LANES // STRIP):
            rows = slice(s * LANES + q * STRIP, s * LANES + (q + 1) * STRIP)
            highest, powers, log = strip_logs(score_ref[rows, :] + dual)
            base_ref[rows, :] = powers
            tops.append(highest)
            logs.append(log)
        top_ref[s : s + 1, :] = to_row(jnp.concatenate(tops, axis=0))
        log_ref[s : s + 1, :] = to_row(jnp.concatenate(logs, axis=0))
    spread(copies_ref, log_ref[...])


def row_log_kernel(
    log_target, parts_ref, top_ref, base_dual_ref, base_ref, score_ref, dual_ref, copies_ref,
    weight_ref, sum_ref, tile_ref,
):
    dual_ref[...] = log_target - log_combined(parts_ref[...])
    lead = dual_ref[...] - base_dual_ref[...]
    near = jnp.max(jnp.abs(lead)) <= REACH

    @pl.when(near)
    def _():
        weight_ref[...] = jnp.exp2(lead)
        row_sums(base_ref, weight_ref, sum_ref)
        sum_ref[...] = top_ref[...] + jnp.log2(sum_ref[...])

    @pl.when(jnp.logical_not(near))
    def _():
        slow_row_logs(score_ref, tile_ref, dual_ref, sum_ref)

    spread(copies_ref, sum_ref[...])


def col_log_kernel(
    log_source, parts_ref, top_ref, base_dual_ref, base_ref, score_ref, dual_ref, copies_ref,
    weight_ref, sum_ref, tile_ref,
):
    dual_ref[...] = log_source - log_combined(parts_ref[...])
    lead = dual_ref[...] + top_ref[...]
    weight_ref[...] = jnp.exp2(jnp.minimum(lead, 100.0))
    col_sums(base_ref, weight_ref, sum_ref)
    most = jnp.max(lead)
    near = jnp.logical_and(
        most <= 60.0,
        jnp.min(jnp.log2(jnp.maximum(sum_ref[...], 1e-37))) >= jnp.maximum(most, -15.0) - 85.0,
    )

    @pl.when(near)
    def _():
        sum_ref[...] = jnp.log2(sum_ref[...]) - base_dual_ref[...]

    @pl.when(jnp.logical_not(near))
    def _():
        slow_col_logs(score_ref, tile_ref, dual_ref, sum_ref)

    spread(copies_ref, sum_ref[...])


def row_plan_kernel(
    log_target, first, parts_ref, grad_ref, dual_in_ref, row_dual_ref, top_ref, base_dual_ref,
    base_ref, score_ref, out_ref, copies_ref, weight_ref, col_ref, sum_ref, tile_ref,
):
    if first:
        dual = log_target - log_combined(parts_ref[...])
        grad = grad_ref[...]
        out_ref[...] = dual
    else:
        dual = dual_in_ref[...]
        grad = -jnp.sum(parts_ref[...], axis=0)
        out_ref[...] = grad
    lead = dual - base_dual_ref[...]
    row_lead = row_dual_ref[...] + top_ref[...]
    near = jnp.logical_and(jnp.max(jnp.abs(lead)) <= REACH, jnp.max(row_lead) <= 60.0)

    @pl.when(near)
    def _():
        weight_ref[...] = jnp.exp2(lead - log_target) * grad
        row_sums(base_ref, weight_ref, sum_ref)
        sum_ref[...] = sum_ref[...] * jnp.exp2(row_lead)

    @pl.when(jnp.logical_not(near))
    def _():
        col_ref[...] = dual - log_target
        weight_ref[...] = grad
        slow_row_weighted(score_ref, tile_ref, row_dual_ref, col_ref, weight_ref, sum_ref)

    spread(copies_ref, sum_ref[...])


def col_plan_kernel(
    log_source, parts_ref, outer_ref, dual_ref, row_dual_ref, top_ref, base_dual_ref, base_ref,
    score_ref, out_ref, copies_ref, weight_ref, col_ref, sum_ref, tile_ref,
):
    grad = outer_ref[...] - jnp.sum(parts_ref[...], axis=0)
    out_ref[...] = grad
    lead = dual_ref[...] - base_dual_ref[...]
    row_lead = row_dual_ref[...] + top_ref[...]
    near = jnp.logical_and(jnp.max(jnp.abs(lead)) <= REACH, jnp.max(row_lead) <= 60.0)

    @pl.when(near)
    def _():
        weight_ref[...] = jnp.exp2(row_lead) * grad
        col_sums(base_ref, weight_ref, sum_ref)
        sum_ref[...] = sum_ref[...] * jnp.exp2(lead - log_source)

    @pl.when(jnp.logical_not(near))
    def _():
        col_ref[...] = dual_ref[...] - log_source
        weight_ref[...] = grad
        slow_col_weighted(score_ref, tile_ref, row_dual_ref, col_ref, weight_ref, sum_ref)

    spread(copies_ref, sum_ref[...])


def direction(place_ref):
    return 1 - 2 * place_ref[3]


def ring_place(place_ref, axis, offset, count):
    return lax.rem(place_ref[axis] + direction(place_ref) * offset + count, count)


def z_block(place_ref, src_ref, grad_ref, offset, counts):
    x_count, z_count = counts
    width, half = src_ref.shape[0], grad_ref.shape[1] // 2
    owned = width // (x_count * z_count)
    at = ring_place(place_ref, 2, offset, z_count)
    rows = [
        src_ref[pl.ds(pl.multiple_of((x * z_count + at) * owned, owned), owned), :]
        for x in range(x_count)
    ]
    return jnp.dot(
        jnp.concatenate(rows, axis=0), grad_ref[:, half:], preferred_element_type=F32
    )


def x_block(place_ref, src_ref, grad_ref, offset, counts):
    x_count = counts[0]
    width, half = src_ref.shape[0], grad_ref.shape[1] // 2
    owned = width // x_count
    at = ring_place(place_ref, 0, offset, x_count)
    rows = src_ref[pl.ds(pl.multiple_of(at * owned, owned), owned), :]
    return jnp.dot(rows, grad_ref[:, :half], preferred_element_type=F32)


def pieces(value):
    first = value.astype(jnp.bfloat16).astype(F32)
    second = (value - first).astype(jnp.bfloat16).astype(F32)
    return first, second, value - first - second


def grad_kernel(
    log_source, log_target, counts, place_ref, parts_ref, row1, row2, row3, col1, col2, col3,
    fbar2, fbar3, gbar1, gbar2, gbar3, top_ref, base_ref, src_ref, score_ref,
    out_ref, start_ref, z_far_ref, x_far_ref, z_back_ref, x_back_ref, rows_ref, cols_ref, tile_ref,
):
    fbar1 = -jnp.sum(parts_ref[...], axis=0)
    leads = [ref[...] - col1[...] for ref in (col2, col3)]
    row_leads = [ref[...] + top_ref[...] for ref in (row1, row2, row3)]
    near = jnp.logical_and(
        jnp.maximum(jnp.max(jnp.abs(leads[0])), jnp.max(jnp.abs(leads[1]))) <= REACH,
        jnp.logical_and(
            jnp.max(jnp.abs(col1[...])) <= FIRST_REACH,
            jnp.max(jnp.maximum(jnp.maximum(row_leads[0], row_leads[1]), row_leads[2])) <= 60.0,
        ),
    )
    count, groups = groups_of(col1), groups_of(row1)

    @pl.when(near)
    def _():
        powers = [-jnp.exp2(lead) for lead in row_leads]
        factors = [*powers, powers[1] * fbar2[...], powers[2] * fbar3[...], powers[0] * fbar1]
        for k in range(8):
            rows_ref[:, k, :] = factors[k] if k < 6 else jnp.zeros_like(fbar1)
        column_factors = [
            jnp.exp2(jnp.full_like(leads[0], -log_target)) * gbar1[...],
            jnp.exp2(leads[0] - log_target) * gbar2[...],
            jnp.exp2(leads[1] - log_target) * gbar3[...],
            jnp.exp2(jnp.full_like(leads[0], -log_source)),
            jnp.exp2(leads[0] - log_source),
            jnp.exp2(-col1[...] - log_source),
        ]
        cols_ref[...] = jnp.zeros_like(cols_ref)
        for k, factor in enumerate(column_factors):
            for c in range(count):
                cols_ref[k : k + 1, c * LANES : (c + 1) * LANES] = factor[c : c + 1, :]
        b1, b2, b3 = pieces(cols_ref[...])
        right = jnp.concatenate([b1, b2, b1, b2, b3, b1], axis=0).astype(jnp.bfloat16)
        held = [None] * count
        for s in range(groups):
            a1, a2, a3 = pieces(rows_ref[s])
            left = jnp.concatenate([a1, a1, a2, a2, a1, a3], axis=0).astype(jnp.bfloat16)
            tile_ref[...] = lax.dot_general(
                left, right, (((0,), (0,)), ((), ())), preferred_element_type=F32
            )
            column = jnp.broadcast_to(to_column(rows_ref[s, 5:6, :]), (LANES, LANES))
            rows = slice(s * LANES, (s + 1) * LANES)
            for c in range(count):
                lanes = slice(c * LANES, (c + 1) * LANES)
                base = base_ref[rows, lanes]
                out_ref[rows, lanes] = (base * tile_ref[:, lanes]).astype(jnp.bfloat16)
                term = jnp.sum((base * column).reshape(LANES // 8, 8, LANES), axis=0)
                held[c] = term if held[c] is None else held[c] + term
        for c, term in enumerate(held):
            start_ref[c : c + 1, :] = (
                jnp.sum(term, axis=0, keepdims=True) * column_factors[5][c : c + 1, :]
            )

    @pl.when(jnp.logical_not(near))
    def _():
        zero = jnp.zeros_like(fbar1)
        for k, value in enumerate(
            (row1[...], row2[...], row3[...], fbar1, fbar2[...], fbar3[...], zero, zero)
        ):
            rows_ref[:, k, :] = value
        start_ref[...] = jnp.zeros_like(start_ref)
        columns_of = (None, col1, col2, col3)
        grads_of = (None, gbar1, gbar2, gbar3)

        @pl.loop(0, groups)
        def _(group):
            load_rows(score_ref, tile_ref, group)
            taken = rows_ref[group]
            columns = [to_column(taken[k : k + 1, :]) for k in range(6)]
            rows = pl.ds(pl.multiple_of(group * LANES, LANES), LANES)
            for c in range(count):
                lanes = slice(c * LANES, (c + 1) * LANES)
                value = jnp.zeros((LANES, LANES), F32)
                for k in reversed(range(3)):
                    scores = tile_ref[:, lanes] + columns[k]
                    plan_q = jnp.exp2(scores + (columns_of[k + 1][c : c + 1, :] - log_target))
                    value = value + plan_q * grads_of[k + 1][c : c + 1, :]
                    before = columns_of[k][c : c + 1, :] if k else jnp.zeros((1, LANES), F32)
                    term = jnp.exp2(scores + (before - log_source)) * columns[3 + k]
                    value = value + term
                    if not k:
                        start_ref[c : c + 1, :] -= jnp.sum(term, axis=0, keepdims=True)
                out_ref[rows, lanes] = (-value).astype(jnp.bfloat16)

    reach = counts[1] // 2
    put(z_far_ref, z_block(place_ref, src_ref, out_ref, reach, counts), start_ref[...])
    put(z_back_ref, z_block(place_ref, src_ref, out_ref, 1 - reach, counts), start_ref[...])
    x_far_ref[...] = x_block(place_ref, src_ref, out_ref, counts[0] // 2, counts)
    x_back_ref[...] = x_block(place_ref, src_ref, out_ref, -1, counts)


def put(out_ref, block, rider):
    rows = block.shape[0]
    out_ref[:rows, :] = block
    out_ref[rows:, :] = jnp.zeros_like(out_ref[rows:, :])
    out_ref[rows:, :LANES] = rider


def rider(ref):
    return ref[ref.shape[0] - 8 :, :LANES]


def x_part_kernel(y_count, place_ref, grad_ref, tgt_ref, after_ref, sent_ref, kept_ref, order_ref):
    block = tgt_ref.shape[1] // (2 * y_count)
    core, turn = place_ref[3], direction(place_ref)
    for side, out_ref in ((0, sent_ref), (1, kept_ref)):
        for k, offset in enumerate((2, 1, -1, 0)):
            step = offset * (2 * side - 1)
            at = lax.rem(place_ref[1] + turn * step + y_count, y_count)
            owner = at * 2 + (core if side else 1 - core)
            order_ref[:, k * block : (k + 1) * block] = tgt_ref[
                :, pl.ds(pl.multiple_of(owner * block, block), block)
            ]
        out_ref[...] = jnp.dot(grad_ref[...], order_ref[...], preferred_element_type=F32)


def y_parts_kernel(counts, place_ref, grad_ref, src_ref, *outs):
    reach = counts[1] // 2
    offsets = [*range(reach - 1, 0, -1), *range(2 - reach, 1)]
    for out_ref, offset in zip(outs, offsets):
        out_ref[...] = z_block(place_ref, src_ref, grad_ref, offset, counts)
    for out_ref, offset in zip(outs[len(offsets) :], (1, 0)):
        out_ref[...] = x_block(place_ref, src_ref, grad_ref, offset, counts)


def add_kernel(count, *refs):
    value = refs[0][...]
    for ref in refs[1:count]:
        value = value + ref[...]
    out_ref, token_ref = refs[-2:]
    out_ref[...] = value
    token_ref[...] = jnp.zeros_like(token_ref)


def turn_kernel(sum_ref, up_ref, after_ref, out_ref, token_ref):
    for s in range(sum_ref.shape[0] // LANES):
        rows = slice(s * LANES, (s + 1) * LANES)
        out_ref[:, rows] = (sum_ref[rows, :] + up_ref[rows, :]).T
    token_ref[...] = jnp.zeros_like(token_ref)


def pair_kernel(one_ref, up_ref, own_ref, down_ref, after_ref, pay_ref, sum_ref, token_ref):
    pay_ref[...] = one_ref[...] + up_ref[...]
    sum_ref[...] = own_ref[...] + down_ref[...]
    token_ref[...] = jnp.zeros_like(token_ref)


def pass_kernel(block_ref, arrived_ref, held_ref, after_ref, out_ref, sum_ref):
    rows = block_ref.shape[0]
    out_ref[:rows, :] = block_ref[...] + arrived_ref[:rows, :]
    out_ref[rows:, :] = arrived_ref[rows:, :]
    sum_ref[...] = held_ref[...] + rider(arrived_ref)


def chip_kernel(kept_ref, arrived_ref, after_ref, *outs):
    block = outs[0].shape[1]
    for k, out_ref in enumerate(outs[:-1]):
        lanes = slice(k * block, (k + 1) * block)
        out_ref[...] = kept_ref[:, lanes] + arrived_ref[:, lanes]
    outs[-1][...] = jnp.zeros_like(outs[-1])


def split_kernel(
    x_count, place_ref, own_ref, up_ref, down_ref, held_up_ref, held_down_ref, after_ref, far_ref,
    back_ref, one_ref, last_ref, start_ref,
):
    start_ref[...] = (
        held_up_ref[...] + held_down_ref[...] + rider(up_ref) + rider(down_ref)
    )
    block = own_ref.shape[0] // x_count
    for out_ref, offset in ((far_ref, 2), (back_ref, -1), (one_ref, 1), (last_ref, 0)):
        at = ring_place(place_ref, 0, offset, x_count)
        rows = pl.ds(pl.multiple_of(at * block, block), block)
        value = own_ref[rows, :] + up_ref[rows, :] + down_ref[rows, :]
        if offset in (2, -1):
            put(out_ref, value, start_ref[...])
        else:
            out_ref[...] = value


def join_kernel(parts_ref, own_ref, up_ref, down_ref, held_ref, out_ref, start_ref):
    rows, half = own_ref.shape
    out_ref[:, :half] = jnp.sum(parts_ref[...], axis=0)
    out_ref[:, half:] = own_ref[...] + up_ref[:rows, :] + down_ref[:rows, :]
    start_ref[...] = held_ref[...] + rider(up_ref) + rider(down_ref)


def call(
    kernel, arguments, outs, scratch=(), in_hbm=(), loose=(), in_smem=(), free=(), last=False, flops=1024, name=None
):
    spaces, values = [], []
    for at, value in enumerate(arguments):
        space = pltpu.VMEM
        if at in in_hbm:
            space = pltpu.HBM
        elif at in loose:
            space = pl.ANY
        elif at in in_smem:
            space = pltpu.SMEM
        if at in in_hbm or (space is pltpu.VMEM and value.size >= PINNED and at not in free):
            value = pltpu.with_memory_space_constraint(value, space)
        spaces.append(space)
        values.append(value)
    return pl.pallas_call(
        kernel,
        out_shape=[
            pltpu.VMEM(out.shape, out.dtype) if math.prod(out.shape) >= PINNED and not last else out
            for out in outs
        ],
        in_specs=[pl.BlockSpec(memory_space=space) for space in spaces],
        out_specs=[pl.BlockSpec(memory_space=pltpu.VMEM)] * len(outs),
        scratch_shapes=list(scratch),
        compiler_params=pltpu.CompilerParams(vmem_limit_bytes=VMEM_BYTES),
        cost_estimate=pl.CostEstimate(flops=flops, bytes_accessed=1024, transcendentals=0),
        name=name,
    )(*values)


def exchanged(copies, axis):
    return lax.all_to_all(copies, axis, 0, 0, tiled=True)


def token():
    return jax.ShapeDtypeStruct((8, LANES), F32)


def added(values, after):
    return call(
        functools.partial(add_kernel, len(values)),
        (*values, after),
        [jax.ShapeDtypeStruct(values[0].shape, F32), token()],
        loose=(len(values),),
        name="added",
    )


def paired(one, up, own, down, after):
    shape = jax.ShapeDtypeStruct(one.shape, F32)
    return call(
        pair_kernel, (one, up, own, down, after), [shape, shape, token()], loose=(4,), name="paired"
    )


def passed(block, arrived, held, after):
    return call(
        pass_kernel,
        (block, arrived, held, after),
        [jax.ShapeDtypeStruct(arrived.shape, F32), token()],
        loose=(3,),
        name="passed",
    )


def body(cost, src_label, tgt_label, class_mask, g_start, f_bar, g_bar, src_emb, tgt_emb):
    row_count = lax.axis_size("rows")
    col_count = lax.axis_size("cols")
    src_rows, tgt_cols = cost.shape
    width = src_emb.shape[1]
    log_source = -math.log2(src_rows * row_count)
    log_target = -math.log2(tgt_cols * col_count)
    row_shape = (src_rows // LANES, LANES)
    col_shape = (tgt_cols // LANES, LANES)
    src_label, f_bar = src_label.reshape(row_shape), f_bar.reshape(row_shape)
    tgt_label, g_bar = tgt_label.reshape(col_shape), g_bar.reshape(col_shape)
    g_start = g_start.reshape(col_shape)

    def array(shape, dtype=F32):
        return jax.ShapeDtypeStruct(shape, dtype)

    matrix = array(cost.shape)
    row_vector, col_vector = array(row_shape), array(col_shape)
    row_copies = array((col_count,) + row_shape)
    col_copies = array((row_count,) + col_shape)
    row_held, col_held = pltpu.VMEM(row_shape, F32), pltpu.VMEM(col_shape, F32)
    slow = [pltpu.VMEM((LANES, tgt_cols), F32)]

    x_count, z_count, y_count = 4, row_count // 4, col_count // 2
    counts = (x_count, z_count)
    owned = width // row_count
    row_at, col_at = lax.axis_index("rows"), lax.axis_index("cols")
    place = jnp.stack(
        [row_at // z_count, col_at // 2, row_at % z_count, col_at % 2]
    ).astype(jnp.int32)
    score, start_base, start_top, copies, src_turned = call(
        first_kernel,
        (cost, src_label, tgt_label, class_mask, g_start, src_emb, place),
        [matrix, matrix, row_vector, row_copies, array(src_emb.shape[::-1], src_emb.dtype)],
        [
            pltpu.VMEM(cost.shape, cost.dtype),
            pltpu.VMEM(row_shape, jnp.int32),
            pltpu.VMEM(col_shape, jnp.int32),
            pltpu.VMEM(class_mask.shape, jnp.int32),
            col_held,
            pltpu.VMEM(src_emb.shape, src_emb.dtype),
            pltpu.VMEM((LANES, tgt_cols), F32),
            row_held,
            pltpu.SemaphoreType.DMA((4,)),
            pltpu.SemaphoreType.DMA(row_shape[:1]),
            pltpu.SemaphoreType.DMA(row_shape[:1]),
        ],
        in_hbm=range(6),
        in_smem=(6,),
        name="first_row_logs",
    )

    def col_logs(parts, top, base_dual, base):
        return call(
            functools.partial(col_log_kernel, log_source),
            (parts, top, base_dual, base, score),
            [row_vector, col_copies],
            [row_held, col_held] + slow,
                name="col_logs",
        )

    zero = jnp.zeros(col_shape, F32)
    row1, copies = col_logs(exchanged(copies, "cols"), start_top, zero, start_base)
    base, top, col1, copies = call(
        functools.partial(rebase_kernel, log_target),
        (exchanged(copies, "rows"), score),
        [matrix, row_vector, col_vector, row_copies],
        [row_held],
        name="second_row_logs",
    )
    row2, copies = col_logs(exchanged(copies, "cols"), top, col1, base)
    col2, copies = call(
        functools.partial(row_log_kernel, log_target),
        (exchanged(copies, "rows"), top, col1, base, score),
        [col_vector, row_copies],
        [col_held, row_held] + slow,
        name="third_row_logs",
    )
    row3, copies = col_logs(exchanged(copies, "cols"), top, col1, base)

    def row_plan(first, parts, grad, dual, row):
        return call(
            functools.partial(row_plan_kernel, log_target, first),
            (parts, grad, dual, row, top, col1, base, score),
            [col_vector, row_copies],
            [col_held, col_held, row_held] + slow,
                name="row_plan",
        )

    def col_plan(parts, outer, dual, row):
        return call(
            functools.partial(col_plan_kernel, log_source),
            (parts, outer, dual, row, top, col1, base, score),
            [row_vector, col_copies],
            [row_held, col_held, col_held] + slow,
                name="col_plan",
        )

    none = jnp.zeros(row_shape, F32)
    col3, copies = row_plan(True, exchanged(copies, "rows"), g_bar, col2, row3)
    fbar3, copies = col_plan(exchanged(copies, "cols"), f_bar, col2, row3)
    gbar2, copies = row_plan(False, exchanged(copies, "rows"), g_bar, col2, row2)
    fbar2, copies = col_plan(exchanged(copies, "cols"), none, col1, row2)
    gbar1, copies = row_plan(False, exchanged(copies, "rows"), g_bar, col1, row1)
    parts = exchanged(copies, "cols")
    devices = [
        (x, y, z, core)
        for x in range(x_count)
        for y in range(y_count)
        for z in range(z_count)
        for core in range(2)
    ]

    def number(x, y, z, core):
        spot = (x % x_count * z_count + z % z_count) * y_count + y % y_count
        return spot * 2 + core

    def turn(value, axis, step):
        moves = []
        for device in devices:
            ahead = list(device)
            ahead[axis] += step * (1 - 2 * device[3])
            moves.append((number(*device), number(*ahead)))
        return lax.ppermute(value, ("rows", "cols"), moves)

    half = tgt_cols // 2
    z_rows, x_rows = x_count * owned, z_count * owned
    z_shape, z_riding = array((z_rows, half)), array((z_rows + 8, half))
    x_shape = array((x_rows, half))
    rounded, start, z_far, x_far, z_back, x_back = call(
        functools.partial(grad_kernel, log_source, log_target, counts),
        (
            place, parts, row1, row2, row3, col1, col2, col3, fbar2, fbar3, gbar1, gbar2, g_bar,
            top, base, src_turned, score,
        ),
        [array(cost.shape, jnp.bfloat16), col_vector, z_riding, x_shape, z_riding, x_shape],
        [pltpu.VMEM((row_shape[0], 8, LANES), F32), pltpu.VMEM((8, tgt_cols), F32)] + slow,
        in_smem=(0,),
        name="cost_grad",
    )
    z_up, z_down = turn(z_far, 2, 1), turn(z_back, 2, -1)
    x_up, x_down = turn(x_far, 0, 1), turn(x_back, 0, -1)
    outs = call(
        functools.partial(y_parts_kernel, counts),
        (place, rounded, src_turned),
        [z_shape] * (z_count - 2) + [x_shape] * 2,
        in_smem=(0,),
        flops=BIG,
        name="grad_y_parts",
    )
    z_3, z_2, z_1, z_back2, z_back1, z_own, x_one, x_own = outs
    z_pay, up_held = passed(z_3, z_up, start, start)
    z_up = turn(z_pay, 2, 1)
    chip_part = array((src_rows, width // 2))
    sent, kept = call(
        functools.partial(x_part_kernel, y_count),
        (place, rounded, tgt_emb, up_held),
        [chip_part, chip_part],
        [pltpu.VMEM((tgt_cols, width // 2), jnp.bfloat16)],
        in_smem=(0,),
        loose=(3,),
        free=(2,),
        flops=BIG,
        name="grad_x_parts",
    )
    arrived = lax.ppermute(sent, "cols", [(at, at ^ 1) for at in range(col_count)])
    z_pay, down_held = passed(z_back2, z_down, jnp.zeros_like(start), kept)
    z_down = turn(z_pay, 2, -1)
    x_pay, x_sum, mark = paired(x_one, x_up, x_own, x_down, down_held)
    x_up = turn(x_pay, 0, 1)
    far, one, back, own, mark = call(
        chip_kernel,
        (kept, arrived, mark),
        [array((src_rows, width // col_count))] * 4 + [token()],
        loose=(2,),
        name="chip_sums",
    )
    y_up, y_down = turn(far, 1, 1), turn(back, 1, -1)
    z_pay, up_held = passed(z_2, z_up, up_held, mark)
    z_up = turn(z_pay, 2, 1)
    z_pay, down_held = passed(z_back1, z_down, down_held, up_held)
    z_down = turn(z_pay, 2, -1)
    y_pay, y_sum, mark = paired(one, y_up, own, y_down, down_held)
    y_up = turn(y_pay, 1, 1)
    first, mark = added((x_sum, x_up), mark)
    along_z = [[x * z_count + z for z in range(z_count)] for x in range(x_count)]
    first = lax.all_to_all(
        first.reshape(z_count, owned, half), "rows", 0, 0, tiled=True, axis_index_groups=along_z
    )
    z_pay, up_held = passed(z_1, z_up, up_held, mark)
    z_up = turn(z_pay, 2, 1)
    grad_x, mark = call(
        turn_kernel,
        (y_sum, y_up, up_held),
        [array((width // col_count, src_rows)), token()],
        loose=(2,),
        last=True,
        name="grad_x",
    )
    last, riding = array((owned, half)), array((owned + 8, half))
    x_far, x_back, x_one, x_own, start = call(
        functools.partial(split_kernel, x_count),
        (place, z_own, z_up, z_down, up_held, down_held, mark),
        [riding, riding, last, last, col_vector],
        in_smem=(0,),
        loose=(6,),
        name="second_half",
    )
    x_up, x_down = turn(x_far, 0, 1), turn(x_back, 0, -1)
    x_pay, start = passed(x_one, x_up, start, start)
    x_up = turn(x_pay, 0, 1)
    grad_y, start = call(
        join_kernel,
        (first, x_own, x_up, x_down, start),
        [array((owned, tgt_cols)), col_vector],
        name="grad_y",
    )
    g_start_bar = start.reshape(tgt_cols)
    return (g_start_bar, grad_x, grad_y)


def solution(mesh):
    placed = (
        P("rows", "cols"),
        P("rows"),
        P("cols"),
        P(),
        P("cols"),
        P("rows"),
        P("cols"),
        P("rows", None),
        P("cols", None),
    )
    return jax.shard_map(
        body,
        mesh=mesh,
        in_specs=placed,
        out_specs=(P("cols"), P("cols", "rows"), P("rows", "cols")),
        check_vma=False,
    )
```

```python
import functools
import math

import jax
import jax.numpy as jnp
from jax import lax
from jax.experimental import pallas as pl
from jax.experimental.pallas import tpu as pltpu
from jax.sharding import PartitionSpec as P

K = 3


EPSILON = 0.05
PENALTY = 1.0
SCALE = 1.0 / (EPSILON * math.log(2.0))
LANES = 128
STRIP = 32
REACH = 40.0
FIRST_REACH = 75.0
VMEM_BYTES = 16 * 2**20
PINNED = 2**16
BIG = 2**32
F32 = jnp.float32


def eye():
    return lax.broadcasted_iota(jnp.int32, (LANES, LANES), 0) == lax.broadcasted_iota(
        jnp.int32, (LANES, LANES), 1
    )


def to_column(row):
    return jnp.sum(jnp.where(eye(), row, 0.0), axis=1, keepdims=True)


def to_row(column):
    return jnp.sum(jnp.where(eye(), column, 0.0), axis=0, keepdims=True)


def log_combined(parts):
    top = jnp.max(parts, axis=0)
    return top + jnp.log2(jnp.sum(jnp.exp2(parts - top[None]), axis=0))


def spread(copies_ref, value):
    copies_ref[...] = jnp.broadcast_to(value[None], copies_ref.shape)


def groups_of(ref):
    return ref.shape[0]


def row_sums(base_ref, weight_ref, out_ref):
    for s in range(groups_of(out_ref)):
        held = None
        for c in range(groups_of(weight_ref)):
            tile = base_ref[s * LANES : (s + 1) * LANES, c * LANES : (c + 1) * LANES]
            term = tile * weight_ref[c : c + 1, :]
            held = term if held is None else held + term
        out_ref[s : s + 1, :] = to_row(jnp.sum(held, axis=1, keepdims=True))


def col_sums(base_ref, weight_ref, out_ref):
    held = [None] * groups_of(out_ref)
    for s in range(groups_of(weight_ref)):
        column = jnp.broadcast_to(to_column(weight_ref[s : s + 1, :]), (LANES, LANES))
        for c in range(len(held)):
            tile = base_ref[s * LANES : (s + 1) * LANES, c * LANES : (c + 1) * LANES]
            term = jnp.sum((tile * column).reshape(LANES // 8, 8, LANES), axis=0)
            held[c] = term if held[c] is None else held[c] + term
    for c, term in enumerate(held):
        out_ref[c : c + 1, :] = jnp.sum(term, axis=0, keepdims=True)


def strip_logs(scores):
    highest = jnp.max(scores, axis=1, keepdims=True)
    powers = jnp.exp2(scores - highest)
    return highest, powers, highest + jnp.log2(jnp.sum(powers, axis=1, keepdims=True))


def wide(ref):
    return jnp.concatenate([ref[c : c + 1, :] for c in range(groups_of(ref))], axis=1)


def load_rows(score_ref, tile_ref, group):
    tile_ref[...] = score_ref[pl.ds(pl.multiple_of(group * LANES, LANES), LANES), :]


def slow_row_logs(score_ref, tile_ref, col_ref, out_ref):
    @pl.loop(0, groups_of(out_ref))
    def _(group):
        load_rows(score_ref, tile_ref, group)
        logs = []
        for q in range(LANES // STRIP):
            logs.append(strip_logs(tile_ref[q * STRIP : (q + 1) * STRIP, :] + wide(col_ref))[2])
        out_ref[pl.ds(group, 1), :] = to_row(jnp.concatenate(logs, axis=0))


def slow_col_logs(score_ref, tile_ref, row_ref, out_ref):
    count = groups_of(out_ref)
    tops = tuple(jnp.full((1, LANES), -1e30, F32) for _ in range(count))

    def highest(group, tops):
        load_rows(score_ref, tile_ref, group)
        column = to_column(row_ref[pl.ds(group, 1), :])
        return tuple(
            jnp.maximum(
                tops[c],
                jnp.max(
                    tile_ref[:, c * LANES : (c + 1) * LANES] + column, axis=0, keepdims=True
                ),
            )
            for c in range(count)
        )

    tops = lax.fori_loop(0, groups_of(row_ref), highest, tops)
    sums = tuple(jnp.zeros((1, LANES), F32) for _ in range(count))

    def summed(group, sums):
        load_rows(score_ref, tile_ref, group)
        column = to_column(row_ref[pl.ds(group, 1), :])
        return tuple(
            sums[c]
            + jnp.sum(
                jnp.exp2(tile_ref[:, c * LANES : (c + 1) * LANES] + column - tops[c]),
                axis=0,
                keepdims=True,
            )
            for c in range(count)
        )

    sums = lax.fori_loop(0, groups_of(row_ref), summed, sums)
    for c in range(count):
        out_ref[c : c + 1, :] = tops[c] + jnp.log2(sums[c])


def slow_row_weighted(score_ref, tile_ref, row_ref, col_ref, weight_ref, out_ref):
    @pl.loop(0, groups_of(out_ref))
    def _(group):
        load_rows(score_ref, tile_ref, group)
        column = to_column(row_ref[pl.ds(group, 1), :])
        sums = []
        for q in range(LANES // STRIP):
            part = slice(q * STRIP, (q + 1) * STRIP)
            plan = jnp.exp2(tile_ref[part, :] + column[part] + wide(col_ref))
            sums.append(jnp.sum(plan * wide(weight_ref), axis=1, keepdims=True))
        out_ref[pl.ds(group, 1), :] = to_row(jnp.concatenate(sums, axis=0))


def slow_col_weighted(score_ref, tile_ref, row_ref, col_ref, weight_ref, out_ref):
    count = groups_of(out_ref)
    sums = tuple(jnp.zeros((1, LANES), F32) for _ in range(count))

    def summed(group, sums):
        load_rows(score_ref, tile_ref, group)
        column = to_column(row_ref[pl.ds(group, 1), :])
        weight = to_column(weight_ref[pl.ds(group, 1), :])
        return tuple(
            sums[c]
            + jnp.sum(
                weight
                * jnp.exp2(
                    tile_ref[:, c * LANES : (c + 1) * LANES] + column + col_ref[c : c + 1, :]
                ),
                axis=0,
                keepdims=True,
            )
            for c in range(count)
        )

    sums = lax.fori_loop(0, groups_of(row_ref), summed, sums)
    for c in range(count):
        out_ref[c : c + 1, :] = sums[c]


def first_kernel(
    cost_hbm, src_hbm, tgt_hbm, mask_hbm, dual_hbm, emb_hbm, place_ref, score_ref, base_ref, top_ref,
    copies_ref, turned_ref, cost_ref, src_ref, tgt_ref, mask_ref, dual_ref, emb_ref, allowed_ref,
    log_ref, small_sem, cost_sem, emb_sem,
):
    small = [
        pltpu.make_async_copy(source, target, small_sem.at[at])
        for at, (source, target) in enumerate(
            ((tgt_hbm, tgt_ref), (mask_hbm, mask_ref), (src_hbm, src_ref), (dual_hbm, dual_ref))
        )
    ]
    for copy in small:
        copy.start()
    blocks = []
    for s in range(groups_of(log_ref)):
        rows = pl.ds(s * LANES, LANES)
        blocks.append(
            pltpu.make_async_copy(cost_hbm.at[rows, :], cost_ref.at[rows, :], cost_sem.at[s])
        )
        blocks[-1].start()
    embs = []
    for s in range(emb_ref.shape[0] // LANES):
        rows = pl.ds(s * LANES, LANES)
        embs.append(pltpu.make_async_copy(emb_hbm.at[rows, :], emb_ref.at[rows, :], emb_sem.at[s]))
        embs[-1].start()
    for copy in small:
        copy.wait()
    classes = mask_ref.shape[0]
    mask = mask_ref[...].astype(F32).astype(jnp.bfloat16)
    ids = lax.broadcasted_iota(jnp.int32, (classes, LANES), 0)
    hot = jnp.concatenate(
        [
            jnp.where(tgt_ref[c : c + 1, :] == ids, 1.0, 0.0).astype(jnp.bfloat16)
            for c in range(groups_of(tgt_ref))
        ],
        axis=1,
    )
    allowed_of = jnp.dot(mask, hot, preferred_element_type=F32).astype(jnp.bfloat16)
    lane_ids = lax.broadcasted_iota(jnp.int32, (LANES, classes), 1).astype(F32)
    dual = wide(dual_ref) * SCALE - PENALTY * SCALE
    for s in range(groups_of(log_ref)):
        label = to_column(src_ref[s : s + 1, :].astype(F32))
        src_hot = jnp.where(label == lane_ids, 1.0, 0.0).astype(jnp.bfloat16)
        allowed_ref[...] = jnp.dot(src_hot, allowed_of, preferred_element_type=F32)
        blocks[s].wait()
        embs[s].wait()
        strip = slice(s * LANES, (s + 1) * LANES)
        turned_ref[:, strip] = emb_ref[strip, :].T
        tops, logs = [], []
        for q in range(LANES // STRIP):
            rows = slice(s * LANES + q * STRIP, s * LANES + (q + 1) * STRIP)
            shifted = cost_ref[rows, :].astype(F32) - PENALTY * allowed_ref[
                q * STRIP : (q + 1) * STRIP, :
            ]
            scores = dual - shifted * SCALE
            highest, powers, log = strip_logs(scores)
            score_ref[rows, :] = scores
            base_ref[rows, :] = powers
            tops.append(highest)
            logs.append(log)
        top_ref[s : s + 1, :] = to_row(jnp.concatenate(tops, axis=0))
        log_ref[s : s + 1, :] = to_row(jnp.concatenate(logs, axis=0))
    spread(copies_ref, log_ref[...])


def rebase_kernel(
    log_target, parts_ref, score_ref, base_ref, top_ref, dual_ref, copies_ref, log_ref
):
    dual_ref[...] = log_target - log_combined(parts_ref[...])
    dual = wide(dual_ref)
    for s in range(groups_of(log_ref)):
        tops, logs = [], []
        for q in range(LANES // STRIP):
            rows = slice(s * LANES + q * STRIP, s * LANES + (q + 1) * STRIP)
            highest, powers, log = strip_logs(score_ref[rows, :] + dual)
            base_ref[rows, :] = powers
            tops.append(highest)
            logs.append(log)
        top_ref[s : s + 1, :] = to_row(jnp.concatenate(tops, axis=0))
        log_ref[s : s + 1, :] = to_row(jnp.concatenate(logs, axis=0))
    spread(copies_ref, log_ref[...])


def row_log_kernel(
    log_target, parts_ref, top_ref, base_dual_ref, base_ref, score_ref, dual_ref, copies_ref,
    weight_ref, sum_ref, tile_ref,
):
    dual_ref[...] = log_target - log_combined(parts_ref[...])
    lead = dual_ref[...] - base_dual_ref[...]
    near = jnp.max(jnp.abs(lead)) <= REACH

    @pl.when(near)
    def _():
        weight_ref[...] = jnp.exp2(lead)
        row_sums(base_ref, weight_ref, sum_ref)
        sum_ref[...] = top_ref[...] + jnp.log2(sum_ref[...])

    @pl.when(jnp.logical_not(near))
    def _():
        slow_row_logs(score_ref, tile_ref, dual_ref, sum_ref)

    spread(copies_ref, sum_ref[...])


def col_log_kernel(
    log_source, parts_ref, top_ref, base_dual_ref, base_ref, score_ref, dual_ref, copies_ref,
    weight_ref, sum_ref, tile_ref,
):
    dual_ref[...] = log_source - log_combined(parts_ref[...])
    lead = dual_ref[...] + top_ref[...]
    weight_ref[...] = jnp.exp2(jnp.minimum(lead, 100.0))
    col_sums(base_ref, weight_ref, sum_ref)
    most = jnp.max(lead)
    near = jnp.logical_and(
        most <= 60.0,
        jnp.min(jnp.log2(jnp.maximum(sum_ref[...], 1e-37))) >= jnp.maximum(most, -15.0) - 85.0,
    )

    @pl.when(near)
    def _():
        sum_ref[...] = jnp.log2(sum_ref[...]) - base_dual_ref[...]

    @pl.when(jnp.logical_not(near))
    def _():
        slow_col_logs(score_ref, tile_ref, dual_ref, sum_ref)

    spread(copies_ref, sum_ref[...])


def row_plan_kernel(
    log_target, first, parts_ref, grad_ref, dual_in_ref, row_dual_ref, top_ref, base_dual_ref,
    base_ref, score_ref, out_ref, copies_ref, weight_ref, col_ref, sum_ref, tile_ref,
):
    if first:
        dual = log_target - log_combined(parts_ref[...])
        grad = grad_ref[...]
        out_ref[...] = dual
    else:
        dual = dual_in_ref[...]
        grad = -jnp.sum(parts_ref[...], axis=0)
        out_ref[...] = grad
    lead = dual - base_dual_ref[...]
    row_lead = row_dual_ref[...] + top_ref[...]
    near = jnp.logical_and(jnp.max(jnp.abs(lead)) <= REACH, jnp.max(row_lead) <= 60.0)

    @pl.when(near)
    def _():
        weight_ref[...] = jnp.exp2(lead - log_target) * grad
        row_sums(base_ref, weight_ref, sum_ref)
        sum_ref[...] = sum_ref[...] * jnp.exp2(row_lead)

    @pl.when(jnp.logical_not(near))
    def _():
        col_ref[...] = dual - log_target
        weight_ref[...] = grad
        slow_row_weighted(score_ref, tile_ref, row_dual_ref, col_ref, weight_ref, sum_ref)

    spread(copies_ref, sum_ref[...])


def col_plan_kernel(
    log_source, parts_ref, outer_ref, dual_ref, row_dual_ref, top_ref, base_dual_ref, base_ref,
    score_ref, out_ref, copies_ref, weight_ref, col_ref, sum_ref, tile_ref,
):
    grad = outer_ref[...] - jnp.sum(parts_ref[...], axis=0)
    out_ref[...] = grad
    lead = dual_ref[...] - base_dual_ref[...]
    row_lead = row_dual_ref[...] + top_ref[...]
    near = jnp.logical_and(jnp.max(jnp.abs(lead)) <= REACH, jnp.max(row_lead) <= 60.0)

    @pl.when(near)
    def _():
        weight_ref[...] = jnp.exp2(row_lead) * grad
        col_sums(base_ref, weight_ref, sum_ref)
        sum_ref[...] = sum_ref[...] * jnp.exp2(lead - log_source)

    @pl.when(jnp.logical_not(near))
    def _():
        col_ref[...] = dual_ref[...] - log_source
        weight_ref[...] = grad
        slow_col_weighted(score_ref, tile_ref, row_dual_ref, col_ref, weight_ref, sum_ref)

    spread(copies_ref, sum_ref[...])


def direction(place_ref):
    return 1 - 2 * place_ref[3]


def ring_place(place_ref, axis, offset, count):
    return lax.rem(place_ref[axis] + direction(place_ref) * offset + count, count)


def z_block(place_ref, src_ref, grad_ref, offset, counts):
    x_count, z_count = counts
    width, half = src_ref.shape[0], grad_ref.shape[1] // 2
    owned = width // (x_count * z_count)
    at = ring_place(place_ref, 2, offset, z_count)
    rows = [
        src_ref[pl.ds(pl.multiple_of((x * z_count + at) * owned, owned), owned), :]
        for x in range(x_count)
    ]
    return jnp.dot(
        jnp.concatenate(rows, axis=0), grad_ref[:, half:], preferred_element_type=F32
    )


def x_block(place_ref, src_ref, grad_ref, offset, counts):
    x_count = counts[0]
    width, half = src_ref.shape[0], grad_ref.shape[1] // 2
    owned = width // x_count
    at = ring_place(place_ref, 0, offset, x_count)
    rows = src_ref[pl.ds(pl.multiple_of(at * owned, owned), owned), :]
    return jnp.dot(rows, grad_ref[:, :half], preferred_element_type=F32)


def pieces(value):
    first = value.astype(jnp.bfloat16).astype(F32)
    second = (value - first).astype(jnp.bfloat16).astype(F32)
    return first, second, value - first - second


def grad_kernel(
    log_source, log_target, counts, place_ref, parts_ref, row1, row2, row3, col1, col2, col3,
    fbar2, fbar3, gbar1, gbar2, gbar3, top_ref, base_ref, src_ref, score_ref,
    out_ref, start_ref, z_far_ref, x_far_ref, z_back_ref, x_back_ref, rows_ref, cols_ref, tile_ref,
):
    fbar1 = -jnp.sum(parts_ref[...], axis=0)
    leads = [ref[...] - col1[...] for ref in (col2, col3)]
    row_leads = [ref[...] + top_ref[...] for ref in (row1, row2, row3)]
    near = jnp.logical_and(
        jnp.maximum(jnp.max(jnp.abs(leads[0])), jnp.max(jnp.abs(leads[1]))) <= REACH,
        jnp.logical_and(
            jnp.max(jnp.abs(col1[...])) <= FIRST_REACH,
            jnp.max(jnp.maximum(jnp.maximum(row_leads[0], row_leads[1]), row_leads[2])) <= 60.0,
        ),
    )
    count, groups = groups_of(col1), groups_of(row1)

    @pl.when(near)
    def _():
        powers = [-jnp.exp2(lead) for lead in row_leads]
        factors = [*powers, powers[1] * fbar2[...], powers[2] * fbar3[...], powers[0] * fbar1]
        for k in range(8):
            rows_ref[:, k, :] = factors[k] if k < 6 else jnp.zeros_like(fbar1)
        column_factors = [
            jnp.exp2(jnp.full_like(leads[0], -log_target)) * gbar1[...],
            jnp.exp2(leads[0] - log_target) * gbar2[...],
            jnp.exp2(leads[1] - log_target) * gbar3[...],
            jnp.exp2(jnp.full_like(leads[0], -log_source)),
            jnp.exp2(leads[0] - log_source),
            jnp.exp2(-col1[...] - log_source),
        ]
        cols_ref[...] = jnp.zeros_like(cols_ref)
        for k, factor in enumerate(column_factors):
            for c in range(count):
                cols_ref[k : k + 1, c * LANES : (c + 1) * LANES] = factor[c : c + 1, :]
        b1, b2, b3 = pieces(cols_ref[...])
        right = jnp.concatenate([b1, b2, b1, b2, b3, b1], axis=0).astype(jnp.bfloat16)
        held = [None] * count
        for s in range(groups):
            a1, a2, a3 = pieces(rows_ref[s])
            left = jnp.concatenate([a1, a1, a2, a2, a1, a3], axis=0).astype(jnp.bfloat16)
            tile_ref[...] = lax.dot_general(
                left, right, (((0,), (0,)), ((), ())), preferred_element_type=F32
            )
            column = jnp.broadcast_to(to_column(rows_ref[s, 5:6, :]), (LANES, LANES))
            rows = slice(s * LANES, (s + 1) * LANES)
            for c in range(count):
                lanes = slice(c * LANES, (c + 1) * LANES)
                base = base_ref[rows, lanes]
                out_ref[rows, lanes] = (base * tile_ref[:, lanes]).astype(jnp.bfloat16)
                term = jnp.sum((base * column).reshape(LANES // 8, 8, LANES), axis=0)
                held[c] = term if held[c] is None else held[c] + term
        for c, term in enumerate(held):
            start_ref[c : c + 1, :] = (
                jnp.sum(term, axis=0, keepdims=True) * column_factors[5][c : c + 1, :]
            )

    @pl.when(jnp.logical_not(near))
    def _():
        zero = jnp.zeros_like(fbar1)
        for k, value in enumerate(
            (row1[...], row2[...], row3[...], fbar1, fbar2[...], fbar3[...], zero, zero)
        ):
            rows_ref[:, k, :] = value
        start_ref[...] = jnp.zeros_like(start_ref)
        columns_of = (None, col1, col2, col3)
        grads_of = (None, gbar1, gbar2, gbar3)

        @pl.loop(0, groups)
        def _(group):
            load_rows(score_ref, tile_ref, group)
            taken = rows_ref[group]
            columns = [to_column(taken[k : k + 1, :]) for k in range(6)]
            rows = pl.ds(pl.multiple_of(group * LANES, LANES), LANES)
            for c in range(count):
                lanes = slice(c * LANES, (c + 1) * LANES)
                value = jnp.zeros((LANES, LANES), F32)
                for k in reversed(range(3)):
                    scores = tile_ref[:, lanes] + columns[k]
                    plan_q = jnp.exp2(scores + (columns_of[k + 1][c : c + 1, :] - log_target))
                    value = value + plan_q * grads_of[k + 1][c : c + 1, :]
                    before = columns_of[k][c : c + 1, :] if k else jnp.zeros((1, LANES), F32)
                    term = jnp.exp2(scores + (before - log_source)) * columns[3 + k]
                    value = value + term
                    if not k:
                        start_ref[c : c + 1, :] -= jnp.sum(term, axis=0, keepdims=True)
                out_ref[rows, lanes] = (-value).astype(jnp.bfloat16)

    reach = counts[1] // 2
    put(z_far_ref, z_block(place_ref, src_ref, out_ref, reach, counts), start_ref[...])
    put(z_back_ref, z_block(place_ref, src_ref, out_ref, 1 - reach, counts), start_ref[...])
    x_far_ref[...] = x_block(place_ref, src_ref, out_ref, counts[0] // 2, counts)
    x_back_ref[...] = x_block(place_ref, src_ref, out_ref, -1, counts)


def put(out_ref, block, rider):
    rows = block.shape[0]
    out_ref[:rows, :] = block
    out_ref[rows:, :] = jnp.zeros_like(out_ref[rows:, :])
    out_ref[rows:, :LANES] = rider


def rider(ref):
    return ref[ref.shape[0] - 8 :, :LANES]


def x_part(y_count, place_ref, grad_ref, tgt_ref, sent_ref, kept_ref, order_ref):
    block = tgt_ref.shape[1] // (2 * y_count)
    core, turn = place_ref[3], direction(place_ref)
    for side, out_ref in ((0, sent_ref), (1, kept_ref)):
        for k, offset in enumerate((2, 1, -1, 0)):
            step = offset * (2 * side - 1)
            at = lax.rem(place_ref[1] + turn * step + y_count, y_count)
            owner = at * 2 + (core if side else 1 - core)
            order_ref[:, k * block : (k + 1) * block] = tgt_ref[
                :, pl.ds(pl.multiple_of(owner * block, block), block)
            ]
        out_ref[...] = jnp.dot(grad_ref[...], order_ref[...], preferred_element_type=F32)


def parts_kernel(
    counts, y_count, place_ref, grad_ref, src_ref, tgt_ref, sent_ref, kept_ref, *outs
):
    *outs, order_ref = outs
    x_part(y_count, place_ref, grad_ref, tgt_ref, sent_ref, kept_ref, order_ref)
    reach = counts[1] // 2
    offsets = [*range(reach - 1, 0, -1), *range(2 - reach, 1)]
    for out_ref, offset in zip(outs, offsets):
        out_ref[...] = z_block(place_ref, src_ref, grad_ref, offset, counts)
    for out_ref, offset in zip(outs[len(offsets) :], (1, 0)):
        out_ref[...] = x_block(place_ref, src_ref, grad_ref, offset, counts)


def forward(out_ref, block_ref, arrived_ref):
    rows = block_ref.shape[0]
    out_ref[:rows, :] = block_ref[...] + arrived_ref[:rows, :]
    out_ref[rows:, :] = arrived_ref[rows:, :]


def second_kernel(
    z_up_ref, z_down_ref, x_up_ref, z_3_ref, z_back2_ref, x_one_ref, start_ref, part_ref,
    z_ref, z_back_ref, x_ref, held_ref, sent_ref,
):
    sent_ref[...] = part_ref[...]
    forward(z_ref, z_3_ref, z_up_ref)
    forward(z_back_ref, z_back2_ref, z_down_ref)
    x_ref[...] = x_one_ref[...] + x_up_ref[...]
    held_ref[...] = start_ref[...] + rider(z_up_ref) + rider(z_down_ref)


def third_kernel(
    z_up_ref, z_down_ref, x_up_ref, arrived_ref, z_2_ref, z_back1_ref, x_own_ref, kept_ref,
    start_ref, z_ref, z_back_ref, x_ref, far_ref, one_ref, back_ref, own_ref, held_ref,
):
    forward(z_ref, z_2_ref, z_up_ref)
    forward(z_back_ref, z_back1_ref, z_down_ref)
    x_ref[...] = x_own_ref[...] + x_up_ref[...]
    block = far_ref.shape[1]
    for k, out_ref in enumerate((far_ref, one_ref, back_ref, own_ref)):
        lanes = slice(k * block, (k + 1) * block)
        out_ref[...] = kept_ref[:, lanes] + arrived_ref[:, lanes]
    held_ref[...] = start_ref[...] + rider(z_up_ref) + rider(z_down_ref)


def fourth_kernel(
    z_up_ref, z_down_ref, x_down_ref, y_up_ref, z_1_ref, z_own_ref, x_sum_ref, one_ref, start_ref,
    z_ref, z_sum_ref, x_ref, y_ref, held_ref,
):
    forward(z_ref, z_1_ref, z_up_ref)
    z_sum_ref[...] = z_own_ref[...] + z_down_ref[: z_own_ref.shape[0], :]
    x_ref[...] = x_sum_ref[...] + x_down_ref[...]
    y_ref[...] = one_ref[...] + y_up_ref[...]
    held_ref[...] = start_ref[...] + rider(z_up_ref) + rider(z_down_ref)


def fifth_kernel(
    x_count, place_ref, z_up_ref, y_up_ref, z_sum_ref, own_ref, start_ref,
    far_ref, back_ref, one_ref, last_ref, y_ref, held_ref,
):
    held_ref[...] = start_ref[...] + rider(z_up_ref)
    block = z_sum_ref.shape[0] // x_count
    for out_ref, offset in ((far_ref, 2), (back_ref, -1), (one_ref, 1), (last_ref, 0)):
        at = ring_place(place_ref, 0, offset, x_count)
        rows = pl.ds(pl.multiple_of(at * block, block), block)
        value = z_sum_ref[rows, :] + z_up_ref[rows, :]
        if offset in (2, -1):
            put(out_ref, value, held_ref[...])
        else:
            out_ref[...] = value
    y_ref[...] = own_ref[...] + y_up_ref[...]


def sixth_kernel(
    x_up_ref, x_down_ref, y_down_ref, x_one_ref, x_own_ref, y_sum_ref, start_ref,
    x_ref, x_sum_ref, grad_x_ref, held_ref,
):
    forward(x_ref, x_one_ref, x_up_ref)
    x_sum_ref[...] = x_own_ref[...] + x_down_ref[: x_own_ref.shape[0], :]
    for s in range(y_sum_ref.shape[0] // LANES):
        rows = slice(s * LANES, (s + 1) * LANES)
        grad_x_ref[:, rows] = (y_sum_ref[rows, :] + y_down_ref[rows, :]).T
    held_ref[...] = start_ref[...] + rider(x_up_ref) + rider(x_down_ref)


def last_kernel(parts_ref, x_up_ref, x_sum_ref, start_ref, out_ref, held_ref):
    rows, half = x_sum_ref.shape
    out_ref[:, :half] = jnp.sum(parts_ref[...], axis=0)
    out_ref[:, half:] = x_sum_ref[...] + x_up_ref[:rows, :]
    held_ref[...] = start_ref[...] + rider(x_up_ref)


def call(
    kernel, arguments, outs, scratch=(), in_hbm=(), loose=(), in_smem=(), free=(), last=False, flops=1024, name=None
):
    spaces, values = [], []
    for at, value in enumerate(arguments):
        space = pltpu.VMEM
        if at in in_hbm:
            space = pltpu.HBM
        elif at in loose:
            space = pl.ANY
        elif at in in_smem:
            space = pltpu.SMEM
        if at in in_hbm or (space is pltpu.VMEM and value.size >= PINNED and at not in free):
            value = pltpu.with_memory_space_constraint(value, space)
        spaces.append(space)
        values.append(value)
    return pl.pallas_call(
        kernel,
        out_shape=[
            pltpu.VMEM(out.shape, out.dtype) if math.prod(out.shape) >= PINNED and not last else out
            for out in outs
        ],
        in_specs=[pl.BlockSpec(memory_space=space) for space in spaces],
        out_specs=[pl.BlockSpec(memory_space=pltpu.VMEM)] * len(outs),
        scratch_shapes=list(scratch),
        compiler_params=pltpu.CompilerParams(vmem_limit_bytes=VMEM_BYTES),
        cost_estimate=pl.CostEstimate(flops=flops, bytes_accessed=1024, transcendentals=0),
        name=name,
    )(*values)


def exchanged(copies, axis):
    return lax.all_to_all(copies, axis, 0, 0, tiled=True)


def body(cost, src_label, tgt_label, class_mask, g_start, f_bar, g_bar, src_emb, tgt_emb):
    row_count = lax.axis_size("rows")
    col_count = lax.axis_size("cols")
    src_rows, tgt_cols = cost.shape
    width = src_emb.shape[1]
    log_source = -math.log2(src_rows * row_count)
    log_target = -math.log2(tgt_cols * col_count)
    row_shape = (src_rows // LANES, LANES)
    col_shape = (tgt_cols // LANES, LANES)
    src_label, f_bar = src_label.reshape(row_shape), f_bar.reshape(row_shape)
    tgt_label, g_bar = tgt_label.reshape(col_shape), g_bar.reshape(col_shape)
    g_start = g_start.reshape(col_shape)

    def array(shape, dtype=F32):
        return jax.ShapeDtypeStruct(shape, dtype)

    matrix = array(cost.shape)
    row_vector, col_vector = array(row_shape), array(col_shape)
    row_copies = array((col_count,) + row_shape)
    col_copies = array((row_count,) + col_shape)
    row_held, col_held = pltpu.VMEM(row_shape, F32), pltpu.VMEM(col_shape, F32)
    slow = [pltpu.VMEM((LANES, tgt_cols), F32)]

    x_count, z_count, y_count = 4, row_count // 4, col_count // 2
    counts = (x_count, z_count)
    owned = width // row_count
    row_at, col_at = lax.axis_index("rows"), lax.axis_index("cols")
    place = jnp.stack(
        [row_at // z_count, col_at // 2, row_at % z_count, col_at % 2]
    ).astype(jnp.int32)
    score, start_base, start_top, copies, src_turned = call(
        first_kernel,
        (cost, src_label, tgt_label, class_mask, g_start, src_emb, place),
        [matrix, matrix, row_vector, row_copies, array(src_emb.shape[::-1], src_emb.dtype)],
        [
            pltpu.VMEM(cost.shape, cost.dtype),
            pltpu.VMEM(row_shape, jnp.int32),
            pltpu.VMEM(col_shape, jnp.int32),
            pltpu.VMEM(class_mask.shape, jnp.int32),
            col_held,
            pltpu.VMEM(src_emb.shape, src_emb.dtype),
            pltpu.VMEM((LANES, tgt_cols), F32),
            row_held,
            pltpu.SemaphoreType.DMA((4,)),
            pltpu.SemaphoreType.DMA(row_shape[:1]),
            pltpu.SemaphoreType.DMA(row_shape[:1]),
        ],
        in_hbm=range(6),
        in_smem=(6,),
        name="first_row_logs",
    )

    def col_logs(parts, top, base_dual, base):
        return call(
            functools.partial(col_log_kernel, log_source),
            (parts, top, base_dual, base, score),
            [row_vector, col_copies],
            [row_held, col_held] + slow,
                name="col_logs",
        )

    zero = jnp.zeros(col_shape, F32)
    row1, copies = col_logs(exchanged(copies, "cols"), start_top, zero, start_base)
    base, top, col1, copies = call(
        functools.partial(rebase_kernel, log_target),
        (exchanged(copies, "rows"), score),
        [matrix, row_vector, col_vector, row_copies],
        [row_held],
        name="second_row_logs",
    )
    row2, copies = col_logs(exchanged(copies, "cols"), top, col1, base)
    col2, copies = call(
        functools.partial(row_log_kernel, log_target),
        (exchanged(copies, "rows"), top, col1, base, score),
        [col_vector, row_copies],
        [col_held, row_held] + slow,
        name="third_row_logs",
    )
    row3, copies = col_logs(exchanged(copies, "cols"), top, col1, base)

    def row_plan(first, parts, grad, dual, row):
        return call(
            functools.partial(row_plan_kernel, log_target, first),
            (parts, grad, dual, row, top, col1, base, score),
            [col_vector, row_copies],
            [col_held, col_held, row_held] + slow,
                name="row_plan",
        )

    def col_plan(parts, outer, dual, row):
        return call(
            functools.partial(col_plan_kernel, log_source),
            (parts, outer, dual, row, top, col1, base, score),
            [row_vector, col_copies],
            [row_held, col_held, col_held] + slow,
                name="col_plan",
        )

    none = jnp.zeros(row_shape, F32)
    col3, copies = row_plan(True, exchanged(copies, "rows"), g_bar, col2, row3)
    fbar3, copies = col_plan(exchanged(copies, "cols"), f_bar, col2, row3)
    gbar2, copies = row_plan(False, exchanged(copies, "rows"), g_bar, col2, row2)
    fbar2, copies = col_plan(exchanged(copies, "cols"), none, col1, row2)
    gbar1, copies = row_plan(False, exchanged(copies, "rows"), g_bar, col1, row1)
    parts = exchanged(copies, "cols")
    devices = [
        (x, y, z, core)
        for x in range(x_count)
        for y in range(y_count)
        for z in range(z_count)
        for core in range(2)
    ]

    def number(x, y, z, core):
        spot = (x % x_count * z_count + z % z_count) * y_count + y % y_count
        return spot * 2 + core

    def turn(value, axis, step):
        moves = []
        for device in devices:
            ahead = list(device)
            ahead[axis] += step * (1 - 2 * device[3])
            moves.append((number(*device), number(*ahead)))
        return lax.ppermute(value, ("rows", "cols"), moves)

    half = tgt_cols // 2
    z_rows, x_rows = x_count * owned, z_count * owned
    z_shape, z_riding = array((z_rows, half)), array((z_rows + 8, half))
    x_shape = array((x_rows, half))
    rounded, start, z_far, x_far, z_back, x_back = call(
        functools.partial(grad_kernel, log_source, log_target, counts),
        (
            place, parts, row1, row2, row3, col1, col2, col3, fbar2, fbar3, gbar1, gbar2, g_bar,
            top, base, src_turned, score,
        ),
        [array(cost.shape, jnp.bfloat16), col_vector, z_riding, x_shape, z_riding, x_shape],
        [pltpu.VMEM((row_shape[0], 8, LANES), F32), pltpu.VMEM((8, tgt_cols), F32)] + slow,
        in_smem=(0,),
        name="cost_grad",
    )
    z_up, z_down, x_up = turn(z_far, 2, 1), turn(z_back, 2, -1), turn(x_far, 0, 1)
    chip_part = array((src_rows, width // 2))
    outs = call(
        functools.partial(parts_kernel, counts, y_count),
        (place, rounded, src_turned, tgt_emb),
        [chip_part] * 2 + [z_shape] * (z_count - 2) + [x_shape] * 2,
        [pltpu.VMEM((tgt_cols, width // 2), jnp.bfloat16)],
        in_smem=(0,),
        free=(3,),
        flops=BIG,
        name="grad_parts",
    )
    sent, kept, z_3, z_2, z_1, z_back2, z_back1, z_own, x_one, x_own = outs
    z_pay, z_back, x_pay, start, sent = call(
        second_kernel,
        (z_up, z_down, x_up, z_3, z_back2, x_one, start, sent),
        [z_riding, z_riding, x_shape, col_vector, chip_part],
        name="second_step",
    )
    z_up, z_down, x_up = turn(z_pay, 2, 1), turn(z_back, 2, -1), turn(x_pay, 0, 1)
    arrived = lax.ppermute(sent, "cols", [(at, at ^ 1) for at in range(col_count)])
    y_shape = array((src_rows, width // col_count))
    z_pay, z_back, x_sum, far, one, back, own, start = call(
        third_kernel,
        (z_up, z_down, x_up, arrived, z_2, z_back1, x_own, kept, start),
        [z_riding, z_riding, x_shape] + [y_shape] * 4 + [col_vector],
        name="third_step",
    )
    z_up, z_down = turn(z_pay, 2, 1), turn(z_back, 2, -1)
    x_down, y_up = turn(x_back, 0, -1), turn(far, 1, 1)
    z_pay, z_sum, first, y_pay, start = call(
        fourth_kernel,
        (z_up, z_down, x_down, y_up, z_1, z_own, x_sum, one, start),
        [z_riding, z_shape, x_shape, y_shape, col_vector],
        name="fourth_step",
    )
    z_up, y_up = turn(z_pay, 2, 1), turn(y_pay, 1, 1)
    along_z = [[x * z_count + z for z in range(z_count)] for x in range(x_count)]
    first = lax.all_to_all(
        first.reshape(z_count, owned, half), "rows", 0, 0, tiled=True, axis_index_groups=along_z
    )
    last, riding = array((owned, half)), array((owned + 8, half))
    x_far, x_back, x_one, x_own, y_sum, start = call(
        functools.partial(fifth_kernel, x_count),
        (place, z_up, y_up, z_sum, own, start),
        [riding, riding, last, last, y_shape, col_vector],
        in_smem=(0,),
        name="fifth_step",
    )
    x_up, x_down, y_down = turn(x_far, 0, 1), turn(x_back, 0, -1), turn(back, 1, -1)
    x_pay, x_sum, grad_x, start = call(
        sixth_kernel,
        (x_up, x_down, y_down, x_one, x_own, y_sum, start),
        [riding, last, array((width // col_count, src_rows)), col_vector],
        last=True,
        name="sixth_step",
    )
    grad_y, start = call(
        last_kernel,
        (first, turn(x_pay, 0, 1), x_sum, start),
        [array((owned, tgt_cols)), col_vector],
        name="last_step",
    )
    g_start_bar = start.reshape(tgt_cols)
    return (g_start_bar, grad_x, grad_y)


def solution(mesh):
    placed = (
        P("rows", "cols"),
        P("rows"),
        P("cols"),
        P(),
        P("cols"),
        P("rows"),
        P("cols"),
        P("rows", None),
        P("cols", None),
    )
    return jax.shard_map(
        body,
        mesh=mesh,
        in_specs=placed,
        out_specs=(P("cols"), P("cols", "rows"), P("rows", "cols")),
        check_vma=False,
    )
```

```python
import functools
import math

import jax
import jax.numpy as jnp
from jax import lax
from jax.experimental import pallas as pl
from jax.experimental.pallas import tpu as pltpu
from jax.sharding import PartitionSpec as P

K = 3


EPSILON = 0.05
PENALTY = 1.0
SCALE = 1.0 / (EPSILON * math.log(2.0))
LANES = 128
STRIP = 32
REACH = 40.0
FIRST_REACH = 75.0
VMEM_BYTES = 16 * 2**20
PINNED = 2**16
BIG = 2**32
STEP = 2**33
F32 = jnp.float32


def eye():
    return lax.broadcasted_iota(jnp.int32, (LANES, LANES), 0) == lax.broadcasted_iota(
        jnp.int32, (LANES, LANES), 1
    )


def to_column(row):
    return jnp.sum(jnp.where(eye(), row, 0.0), axis=1, keepdims=True)


def to_row(column):
    return jnp.sum(jnp.where(eye(), column, 0.0), axis=0, keepdims=True)


def log_combined(parts):
    top = jnp.max(parts, axis=0)
    return top + jnp.log2(jnp.sum(jnp.exp2(parts - top[None]), axis=0))


def spread(copies_ref, value):
    copies_ref[...] = jnp.broadcast_to(value[None], copies_ref.shape)


def groups_of(ref):
    return ref.shape[0]


def row_sums(base_ref, weight_ref, out_ref):
    for s in range(groups_of(out_ref)):
        held = None
        for c in range(groups_of(weight_ref)):
            tile = base_ref[s * LANES : (s + 1) * LANES, c * LANES : (c + 1) * LANES]
            term = tile * weight_ref[c : c + 1, :]
            held = term if held is None else held + term
        out_ref[s : s + 1, :] = to_row(jnp.sum(held, axis=1, keepdims=True))


def col_sums(base_ref, weight_ref, out_ref):
    held = [None] * groups_of(out_ref)
    for s in range(groups_of(weight_ref)):
        column = jnp.broadcast_to(to_column(weight_ref[s : s + 1, :]), (LANES, LANES))
        for c in range(len(held)):
            tile = base_ref[s * LANES : (s + 1) * LANES, c * LANES : (c + 1) * LANES]
            term = jnp.sum((tile * column).reshape(LANES // 8, 8, LANES), axis=0)
            held[c] = term if held[c] is None else held[c] + term
    for c, term in enumerate(held):
        out_ref[c : c + 1, :] = jnp.sum(term, axis=0, keepdims=True)


def strip_logs(scores):
    highest = jnp.max(scores, axis=1, keepdims=True)
    powers = jnp.exp2(scores - highest)
    return highest, powers, highest + jnp.log2(jnp.sum(powers, axis=1, keepdims=True))


def wide(ref):
    return jnp.concatenate([ref[c : c + 1, :] for c in range(groups_of(ref))], axis=1)


def load_rows(score_ref, tile_ref, group):
    tile_ref[...] = score_ref[pl.ds(pl.multiple_of(group * LANES, LANES), LANES), :]


def slow_row_logs(score_ref, tile_ref, col_ref, out_ref):
    @pl.loop(0, groups_of(out_ref))
    def _(group):
        load_rows(score_ref, tile_ref, group)
        logs = []
        for q in range(LANES // STRIP):
            logs.append(strip_logs(tile_ref[q * STRIP : (q + 1) * STRIP, :] + wide(col_ref))[2])
        out_ref[pl.ds(group, 1), :] = to_row(jnp.concatenate(logs, axis=0))


def slow_col_logs(score_ref, tile_ref, row_ref, out_ref):
    count = groups_of(out_ref)
    tops = tuple(jnp.full((1, LANES), -1e30, F32) for _ in range(count))

    def highest(group, tops):
        load_rows(score_ref, tile_ref, group)
        column = to_column(row_ref[pl.ds(group, 1), :])
        return tuple(
            jnp.maximum(
                tops[c],
                jnp.max(
                    tile_ref[:, c * LANES : (c + 1) * LANES] + column, axis=0, keepdims=True
                ),
            )
            for c in range(count)
        )

    tops = lax.fori_loop(0, groups_of(row_ref), highest, tops)
    sums = tuple(jnp.zeros((1, LANES), F32) for _ in range(count))

    def summed(group, sums):
        load_rows(score_ref, tile_ref, group)
        column = to_column(row_ref[pl.ds(group, 1), :])
        return tuple(
            sums[c]
            + jnp.sum(
                jnp.exp2(tile_ref[:, c * LANES : (c + 1) * LANES] + column - tops[c]),
                axis=0,
                keepdims=True,
            )
            for c in range(count)
        )

    sums = lax.fori_loop(0, groups_of(row_ref), summed, sums)
    for c in range(count):
        out_ref[c : c + 1, :] = tops[c] + jnp.log2(sums[c])


def slow_row_weighted(score_ref, tile_ref, row_ref, col_ref, weight_ref, out_ref):
    @pl.loop(0, groups_of(out_ref))
    def _(group):
        load_rows(score_ref, tile_ref, group)
        column = to_column(row_ref[pl.ds(group, 1), :])
        sums = []
        for q in range(LANES // STRIP):
            part = slice(q * STRIP, (q + 1) * STRIP)
            plan = jnp.exp2(tile_ref[part, :] + column[part] + wide(col_ref))
            sums.append(jnp.sum(plan * wide(weight_ref), axis=1, keepdims=True))
        out_ref[pl.ds(group, 1), :] = to_row(jnp.concatenate(sums, axis=0))


def slow_col_weighted(score_ref, tile_ref, row_ref, col_ref, weight_ref, out_ref):
    count = groups_of(out_ref)
    sums = tuple(jnp.zeros((1, LANES), F32) for _ in range(count))

    def summed(group, sums):
        load_rows(score_ref, tile_ref, group)
        column = to_column(row_ref[pl.ds(group, 1), :])
        weight = to_column(weight_ref[pl.ds(group, 1), :])
        return tuple(
            sums[c]
            + jnp.sum(
                weight
                * jnp.exp2(
                    tile_ref[:, c * LANES : (c + 1) * LANES] + column + col_ref[c : c + 1, :]
                ),
                axis=0,
                keepdims=True,
            )
            for c in range(count)
        )

    sums = lax.fori_loop(0, groups_of(row_ref), summed, sums)
    for c in range(count):
        out_ref[c : c + 1, :] = sums[c]


def first_kernel(
    cost_hbm, src_hbm, tgt_hbm, mask_hbm, dual_hbm, emb_hbm, place_ref, score_ref, base_ref, top_ref,
    copies_ref, turned_ref, cost_ref, src_ref, tgt_ref, mask_ref, dual_ref, emb_ref, allowed_ref,
    log_ref, small_sem, cost_sem, emb_sem,
):
    small = [
        pltpu.make_async_copy(source, target, small_sem.at[at])
        for at, (source, target) in enumerate(
            ((tgt_hbm, tgt_ref), (mask_hbm, mask_ref), (src_hbm, src_ref), (dual_hbm, dual_ref))
        )
    ]
    for copy in small:
        copy.start()
    blocks = []
    for s in range(groups_of(log_ref)):
        rows = pl.ds(s * LANES, LANES)
        blocks.append(
            pltpu.make_async_copy(cost_hbm.at[rows, :], cost_ref.at[rows, :], cost_sem.at[s])
        )
        blocks[-1].start()
    embs = []
    for s in range(emb_ref.shape[0] // LANES):
        rows = pl.ds(s * LANES, LANES)
        embs.append(pltpu.make_async_copy(emb_hbm.at[rows, :], emb_ref.at[rows, :], emb_sem.at[s]))
        embs[-1].start()
    for copy in small:
        copy.wait()
    classes = mask_ref.shape[0]
    mask = mask_ref[...].astype(F32).astype(jnp.bfloat16)
    ids = lax.broadcasted_iota(jnp.int32, (classes, LANES), 0)
    hot = jnp.concatenate(
        [
            jnp.where(tgt_ref[c : c + 1, :] == ids, 1.0, 0.0).astype(jnp.bfloat16)
            for c in range(groups_of(tgt_ref))
        ],
        axis=1,
    )
    allowed_of = jnp.dot(mask, hot, preferred_element_type=F32).astype(jnp.bfloat16)
    lane_ids = lax.broadcasted_iota(jnp.int32, (LANES, classes), 1).astype(F32)
    dual = wide(dual_ref) * SCALE - PENALTY * SCALE
    for s in range(groups_of(log_ref)):
        label = to_column(src_ref[s : s + 1, :].astype(F32))
        src_hot = jnp.where(label == lane_ids, 1.0, 0.0).astype(jnp.bfloat16)
        allowed_ref[...] = jnp.dot(src_hot, allowed_of, preferred_element_type=F32)
        blocks[s].wait()
        embs[s].wait()
        strip = slice(s * LANES, (s + 1) * LANES)
        turned_ref[:, strip] = emb_ref[strip, :].T
        tops, logs = [], []
        for q in range(LANES // STRIP):
            rows = slice(s * LANES + q * STRIP, s * LANES + (q + 1) * STRIP)
            shifted = cost_ref[rows, :].astype(F32) - PENALTY * allowed_ref[
                q * STRIP : (q + 1) * STRIP, :
            ]
            scores = dual - shifted * SCALE
            highest, powers, log = strip_logs(scores)
            score_ref[rows, :] = scores
            base_ref[rows, :] = powers
            tops.append(highest)
            logs.append(log)
        top_ref[s : s + 1, :] = to_row(jnp.concatenate(tops, axis=0))
        log_ref[s : s + 1, :] = to_row(jnp.concatenate(logs, axis=0))
    spread(copies_ref, log_ref[...])


def rebase_kernel(
    log_target, parts_ref, score_ref, base_ref, top_ref, dual_ref, copies_ref, log_ref
):
    dual_ref[...] = log_target - log_combined(parts_ref[...])
    dual = wide(dual_ref)
    for s in range(groups_of(log_ref)):
        tops, logs = [], []
        for q in range(LANES // STRIP):
            rows = slice(s * LANES + q * STRIP, s * LANES + (q + 1) * STRIP)
            highest, powers, log = strip_logs(score_ref[rows, :] + dual)
            base_ref[rows, :] = powers
            tops.append(highest)
            logs.append(log)
        top_ref[s : s + 1, :] = to_row(jnp.concatenate(tops, axis=0))
        log_ref[s : s + 1, :] = to_row(jnp.concatenate(logs, axis=0))
    spread(copies_ref, log_ref[...])


def row_log_kernel(
    log_target, parts_ref, top_ref, base_dual_ref, base_ref, score_ref, dual_ref, copies_ref,
    weight_ref, sum_ref, tile_ref,
):
    dual_ref[...] = log_target - log_combined(parts_ref[...])
    lead = dual_ref[...] - base_dual_ref[...]
    near = jnp.max(jnp.abs(lead)) <= REACH

    @pl.when(near)
    def _():
        weight_ref[...] = jnp.exp2(lead)
        row_sums(base_ref, weight_ref, sum_ref)
        sum_ref[...] = top_ref[...] + jnp.log2(sum_ref[...])

    @pl.when(jnp.logical_not(near))
    def _():
        slow_row_logs(score_ref, tile_ref, dual_ref, sum_ref)

    spread(copies_ref, sum_ref[...])


def col_log_kernel(
    log_source, parts_ref, top_ref, base_dual_ref, base_ref, score_ref, dual_ref, copies_ref,
    weight_ref, sum_ref, tile_ref,
):
    dual_ref[...] = log_source - log_combined(parts_ref[...])
    lead = dual_ref[...] + top_ref[...]
    weight_ref[...] = jnp.exp2(jnp.minimum(lead, 100.0))
    col_sums(base_ref, weight_ref, sum_ref)
    most = jnp.max(lead)
    near = jnp.logical_and(
        most <= 60.0,
        jnp.min(jnp.log2(jnp.maximum(sum_ref[...], 1e-37))) >= jnp.maximum(most, -15.0) - 85.0,
    )

    @pl.when(near)
    def _():
        sum_ref[...] = jnp.log2(sum_ref[...]) - base_dual_ref[...]

    @pl.when(jnp.logical_not(near))
    def _():
        slow_col_logs(score_ref, tile_ref, dual_ref, sum_ref)

    spread(copies_ref, sum_ref[...])


def row_plan_kernel(
    log_target, first, parts_ref, grad_ref, dual_in_ref, row_dual_ref, top_ref, base_dual_ref,
    base_ref, score_ref, out_ref, copies_ref, weight_ref, col_ref, sum_ref, tile_ref,
):
    if first:
        dual = log_target - log_combined(parts_ref[...])
        grad = grad_ref[...]
        out_ref[...] = dual
    else:
        dual = dual_in_ref[...]
        grad = -jnp.sum(parts_ref[...], axis=0)
        out_ref[...] = grad
    lead = dual - base_dual_ref[...]
    row_lead = row_dual_ref[...] + top_ref[...]
    near = jnp.logical_and(jnp.max(jnp.abs(lead)) <= REACH, jnp.max(row_lead) <= 60.0)

    @pl.when(near)
    def _():
        weight_ref[...] = jnp.exp2(lead - log_target) * grad
        row_sums(base_ref, weight_ref, sum_ref)
        sum_ref[...] = sum_ref[...] * jnp.exp2(row_lead)

    @pl.when(jnp.logical_not(near))
    def _():
        col_ref[...] = dual - log_target
        weight_ref[...] = grad
        slow_row_weighted(score_ref, tile_ref, row_dual_ref, col_ref, weight_ref, sum_ref)

    spread(copies_ref, sum_ref[...])


def col_plan_kernel(
    log_source, parts_ref, outer_ref, dual_ref, row_dual_ref, top_ref, base_dual_ref, base_ref,
    score_ref, out_ref, copies_ref, weight_ref, col_ref, sum_ref, tile_ref,
):
    grad = outer_ref[...] - jnp.sum(parts_ref[...], axis=0)
    out_ref[...] = grad
    lead = dual_ref[...] - base_dual_ref[...]
    row_lead = row_dual_ref[...] + top_ref[...]
    near = jnp.logical_and(jnp.max(jnp.abs(lead)) <= REACH, jnp.max(row_lead) <= 60.0)

    @pl.when(near)
    def _():
        weight_ref[...] = jnp.exp2(row_lead) * grad
        col_sums(base_ref, weight_ref, sum_ref)
        sum_ref[...] = sum_ref[...] * jnp.exp2(lead - log_source)

    @pl.when(jnp.logical_not(near))
    def _():
        col_ref[...] = dual_ref[...] - log_source
        weight_ref[...] = grad
        slow_col_weighted(score_ref, tile_ref, row_dual_ref, col_ref, weight_ref, sum_ref)

    spread(copies_ref, sum_ref[...])


def direction(place_ref):
    return 1 - 2 * place_ref[3]


def ring_place(place_ref, axis, offset, count):
    return lax.rem(place_ref[axis] + direction(place_ref) * offset + count, count)


def z_block(place_ref, src_ref, grad_ref, offset, counts):
    x_count, z_count = counts
    width, half = src_ref.shape[0], grad_ref.shape[1] // 2
    owned = width // (x_count * z_count)
    at = ring_place(place_ref, 2, offset, z_count)
    rows = [
        src_ref[pl.ds(pl.multiple_of((x * z_count + at) * owned, owned), owned), :]
        for x in range(x_count)
    ]
    return jnp.dot(
        jnp.concatenate(rows, axis=0), grad_ref[:, half:], preferred_element_type=F32
    )


def x_block(place_ref, src_ref, grad_ref, offset, counts):
    x_count = counts[0]
    width, half = src_ref.shape[0], grad_ref.shape[1] // 2
    owned = width // x_count
    at = ring_place(place_ref, 0, offset, x_count)
    rows = src_ref[pl.ds(pl.multiple_of(at * owned, owned), owned), :]
    return jnp.dot(rows, grad_ref[:, :half], preferred_element_type=F32)


def pieces(value):
    first = value.astype(jnp.bfloat16).astype(F32)
    second = (value - first).astype(jnp.bfloat16).astype(F32)
    return first, second, value - first - second


def grad_kernel(
    log_source, log_target, counts, place_ref, parts_ref, row1, row2, row3, col1, col2, col3,
    fbar2, fbar3, gbar1, gbar2, gbar3, top_ref, base_ref, src_ref, score_ref,
    out_ref, start_ref, z_far_ref, x_far_ref, z_back_ref, x_back_ref, rows_ref, cols_ref, tile_ref,
):
    fbar1 = -jnp.sum(parts_ref[...], axis=0)
    leads = [ref[...] - col1[...] for ref in (col2, col3)]
    row_leads = [ref[...] + top_ref[...] for ref in (row1, row2, row3)]
    near = jnp.logical_and(
        jnp.maximum(jnp.max(jnp.abs(leads[0])), jnp.max(jnp.abs(leads[1]))) <= REACH,
        jnp.logical_and(
            jnp.max(jnp.abs(col1[...])) <= FIRST_REACH,
            jnp.max(jnp.maximum(jnp.maximum(row_leads[0], row_leads[1]), row_leads[2])) <= 60.0,
        ),
    )
    count, groups = groups_of(col1), groups_of(row1)

    @pl.when(near)
    def _():
        powers = [-jnp.exp2(lead) for lead in row_leads]
        factors = [*powers, powers[1] * fbar2[...], powers[2] * fbar3[...], powers[0] * fbar1]
        for k in range(8):
            rows_ref[:, k, :] = factors[k] if k < 6 else jnp.zeros_like(fbar1)
        column_factors = [
            jnp.exp2(jnp.full_like(leads[0], -log_target)) * gbar1[...],
            jnp.exp2(leads[0] - log_target) * gbar2[...],
            jnp.exp2(leads[1] - log_target) * gbar3[...],
            jnp.exp2(jnp.full_like(leads[0], -log_source)),
            jnp.exp2(leads[0] - log_source),
            jnp.exp2(-col1[...] - log_source),
        ]
        cols_ref[...] = jnp.zeros_like(cols_ref)
        for k, factor in enumerate(column_factors):
            for c in range(count):
                cols_ref[k : k + 1, c * LANES : (c + 1) * LANES] = factor[c : c + 1, :]
        b1, b2, b3 = pieces(cols_ref[...])
        right = jnp.concatenate([b1, b2, b1, b2, b3, b1], axis=0).astype(jnp.bfloat16)
        held = [None] * count
        for s in range(groups):
            a1, a2, a3 = pieces(rows_ref[s])
            left = jnp.concatenate([a1, a1, a2, a2, a1, a3], axis=0).astype(jnp.bfloat16)
            tile_ref[...] = lax.dot_general(
                left, right, (((0,), (0,)), ((), ())), preferred_element_type=F32
            )
            column = jnp.broadcast_to(to_column(rows_ref[s, 5:6, :]), (LANES, LANES))
            rows = slice(s * LANES, (s + 1) * LANES)
            for c in range(count):
                lanes = slice(c * LANES, (c + 1) * LANES)
                base = base_ref[rows, lanes]
                out_ref[rows, lanes] = (base * tile_ref[:, lanes]).astype(jnp.bfloat16)
                term = jnp.sum((base * column).reshape(LANES // 8, 8, LANES), axis=0)
                held[c] = term if held[c] is None else held[c] + term
        for c, term in enumerate(held):
            start_ref[c : c + 1, :] = (
                jnp.sum(term, axis=0, keepdims=True) * column_factors[5][c : c + 1, :]
            )

    @pl.when(jnp.logical_not(near))
    def _():
        zero = jnp.zeros_like(fbar1)
        for k, value in enumerate(
            (row1[...], row2[...], row3[...], fbar1, fbar2[...], fbar3[...], zero, zero)
        ):
            rows_ref[:, k, :] = value
        start_ref[...] = jnp.zeros_like(start_ref)
        columns_of = (None, col1, col2, col3)
        grads_of = (None, gbar1, gbar2, gbar3)

        @pl.loop(0, groups)
        def _(group):
            load_rows(score_ref, tile_ref, group)
            taken = rows_ref[group]
            columns = [to_column(taken[k : k + 1, :]) for k in range(6)]
            rows = pl.ds(pl.multiple_of(group * LANES, LANES), LANES)
            for c in range(count):
                lanes = slice(c * LANES, (c + 1) * LANES)
                value = jnp.zeros((LANES, LANES), F32)
                for k in reversed(range(3)):
                    scores = tile_ref[:, lanes] + columns[k]
                    plan_q = jnp.exp2(scores + (columns_of[k + 1][c : c + 1, :] - log_target))
                    value = value + plan_q * grads_of[k + 1][c : c + 1, :]
                    before = columns_of[k][c : c + 1, :] if k else jnp.zeros((1, LANES), F32)
                    term = jnp.exp2(scores + (before - log_source)) * columns[3 + k]
                    value = value + term
                    if not k:
                        start_ref[c : c + 1, :] -= jnp.sum(term, axis=0, keepdims=True)
                out_ref[rows, lanes] = (-value).astype(jnp.bfloat16)

    reach = counts[1] // 2
    put(z_far_ref, z_block(place_ref, src_ref, out_ref, reach, counts), start_ref[...])
    put(z_back_ref, z_block(place_ref, src_ref, out_ref, 1 - reach, counts), start_ref[...])
    x_far_ref[...] = x_block(place_ref, src_ref, out_ref, counts[0] // 2, counts)
    x_back_ref[...] = x_block(place_ref, src_ref, out_ref, -1, counts)


def put(out_ref, block, rider):
    rows = block.shape[0]
    out_ref[:rows, :] = block
    out_ref[rows:, :] = jnp.zeros_like(out_ref[rows:, :])
    out_ref[rows:, :LANES] = rider


def rider(ref):
    return ref[ref.shape[0] - 8 :, :LANES]


def x_part(y_count, place_ref, grad_ref, tgt_ref, sent_ref, kept_ref, order_ref):
    block = tgt_ref.shape[1] // (2 * y_count)
    core, turn = place_ref[3], direction(place_ref)
    for side, out_ref in ((0, sent_ref), (1, kept_ref)):
        for k, offset in enumerate((2, 1, -1, 0)):
            step = offset * (2 * side - 1)
            at = lax.rem(place_ref[1] + turn * step + y_count, y_count)
            owner = at * 2 + (core if side else 1 - core)
            order_ref[:, k * block : (k + 1) * block] = tgt_ref[
                :, pl.ds(pl.multiple_of(owner * block, block), block)
            ]
        out_ref[...] = jnp.dot(grad_ref[...], order_ref[...], preferred_element_type=F32)


def parts_kernel(
    counts, y_count, place_ref, grad_ref, src_ref, tgt_ref, sent_ref, kept_ref, *outs
):
    *outs, order_ref = outs
    x_part(y_count, place_ref, grad_ref, tgt_ref, sent_ref, kept_ref, order_ref)
    reach = counts[1] // 2
    offsets = [*range(reach - 1, 0, -1), *range(2 - reach, 1)]
    for out_ref, offset in zip(outs, offsets):
        out_ref[...] = z_block(place_ref, src_ref, grad_ref, offset, counts)
    for out_ref, offset in zip(outs[len(offsets) :], (1, 0)):
        out_ref[...] = x_block(place_ref, src_ref, grad_ref, offset, counts)


def forward(out_ref, block_ref, arrived_ref):
    rows = block_ref.shape[0]
    out_ref[:rows, :] = block_ref[...] + arrived_ref[:rows, :]
    out_ref[rows:, :] = arrived_ref[rows:, :]


def token(ref):
    ref[...] = jnp.zeros_like(ref)


def z_kernel(up_ref, down_ref, ahead_ref, behind_ref, start_ref, after_ref, z_ref, back_ref, held_ref):
    forward(z_ref, ahead_ref, up_ref)
    forward(back_ref, behind_ref, down_ref)
    held_ref[...] = start_ref[...] + rider(up_ref) + rider(down_ref)


def x_kernel(up_ref, down_ref, one_ref, own_ref, after_ref, pay_ref, sum_ref, token_ref):
    pay_ref[...] = one_ref[...] + up_ref[...]
    sum_ref[...] = own_ref[...] + down_ref[...]
    token(token_ref)


def add_kernel(one_ref, other_ref, after_ref, sum_ref, token_ref):
    sum_ref[...] = one_ref[...] + other_ref[...]
    token(token_ref)


def chip_kernel(arrived_ref, kept_ref, after_ref, *outs):
    block = outs[0].shape[1]
    for k, out_ref in enumerate(outs[:-1]):
        lanes = slice(k * block, (k + 1) * block)
        out_ref[...] = kept_ref[:, lanes] + arrived_ref[:, lanes]
    token(outs[-1])


def last_z_kernel(
    up_ref, down_ref, ahead_ref, own_ref, start_ref, after_ref, z_ref, z_sum_ref, held_ref
):
    forward(z_ref, ahead_ref, up_ref)
    z_sum_ref[...] = own_ref[...] + down_ref[: own_ref.shape[0], :]
    held_ref[...] = start_ref[...] + rider(up_ref) + rider(down_ref)


def split_kernel(
    x_count, place_ref, z_up_ref, z_sum_ref, start_ref, after_ref,
    far_ref, back_ref, one_ref, last_ref, held_ref,
):
    held_ref[...] = start_ref[...] + rider(z_up_ref)
    block = z_sum_ref.shape[0] // x_count
    for out_ref, offset in ((far_ref, 2), (back_ref, -1), (one_ref, 1), (last_ref, 0)):
        at = ring_place(place_ref, 0, offset, x_count)
        rows = pl.ds(pl.multiple_of(at * block, block), block)
        value = z_sum_ref[rows, :] + z_up_ref[rows, :]
        if offset:
            put(out_ref, value, held_ref[...])
        else:
            out_ref[...] = value


def turn_kernel(sum_ref, up_ref, after_ref, out_ref, token_ref):
    for s in range(sum_ref.shape[0] // LANES):
        rows = slice(s * LANES, (s + 1) * LANES)
        out_ref[:, rows] = (sum_ref[rows, :] + up_ref[rows, :]).T
    token(token_ref)


def last_kernel(parts_ref, far_ref, one_ref, back_ref, own_ref, start_ref, out_ref, held_ref):
    rows, half = own_ref.shape
    out_ref[:, :half] = jnp.sum(parts_ref[...], axis=0)
    value, held = own_ref[...], start_ref[...]
    for ref in (far_ref, one_ref, back_ref):
        value = value + ref[:rows, :]
        held = held + rider(ref)
    out_ref[:, half:] = value
    held_ref[...] = held


def call(
    kernel, arguments, outs, scratch=(), in_hbm=(), loose=(), in_smem=(), free=(), last=False, flops=1024, name=None
):
    spaces, values = [], []
    for at, value in enumerate(arguments):
        space = pltpu.VMEM
        if at in in_hbm:
            space = pltpu.HBM
        elif at in loose:
            space = pl.ANY
        elif at in in_smem:
            space = pltpu.SMEM
        if at in in_hbm or (space is pltpu.VMEM and value.size >= PINNED and at not in free):
            value = pltpu.with_memory_space_constraint(value, space)
        spaces.append(space)
        values.append(value)
    return pl.pallas_call(
        kernel,
        out_shape=[
            pltpu.VMEM(out.shape, out.dtype) if math.prod(out.shape) >= PINNED and not last else out
            for out in outs
        ],
        in_specs=[pl.BlockSpec(memory_space=space) for space in spaces],
        out_specs=[pl.BlockSpec(memory_space=pltpu.VMEM)] * len(outs),
        scratch_shapes=list(scratch),
        compiler_params=pltpu.CompilerParams(vmem_limit_bytes=VMEM_BYTES),
        cost_estimate=pl.CostEstimate(flops=flops, bytes_accessed=1024, transcendentals=0),
        name=name,
    )(*values)


def exchanged(copies, axis):
    return lax.all_to_all(copies, axis, 0, 0, tiled=True)


def body(cost, src_label, tgt_label, class_mask, g_start, f_bar, g_bar, src_emb, tgt_emb):
    row_count = lax.axis_size("rows")
    col_count = lax.axis_size("cols")
    src_rows, tgt_cols = cost.shape
    width = src_emb.shape[1]
    log_source = -math.log2(src_rows * row_count)
    log_target = -math.log2(tgt_cols * col_count)
    row_shape = (src_rows // LANES, LANES)
    col_shape = (tgt_cols // LANES, LANES)
    src_label, f_bar = src_label.reshape(row_shape), f_bar.reshape(row_shape)
    tgt_label, g_bar = tgt_label.reshape(col_shape), g_bar.reshape(col_shape)
    g_start = g_start.reshape(col_shape)

    def array(shape, dtype=F32):
        return jax.ShapeDtypeStruct(shape, dtype)

    matrix = array(cost.shape)
    row_vector, col_vector = array(row_shape), array(col_shape)
    row_copies = array((col_count,) + row_shape)
    col_copies = array((row_count,) + col_shape)
    row_held, col_held = pltpu.VMEM(row_shape, F32), pltpu.VMEM(col_shape, F32)
    slow = [pltpu.VMEM((LANES, tgt_cols), F32)]

    x_count, z_count, y_count = 4, row_count // 4, col_count // 2
    counts = (x_count, z_count)
    owned = width // row_count
    row_at, col_at = lax.axis_index("rows"), lax.axis_index("cols")
    place = jnp.stack(
        [row_at // z_count, col_at // 2, row_at % z_count, col_at % 2]
    ).astype(jnp.int32)
    score, start_base, start_top, copies, src_turned = call(
        first_kernel,
        (cost, src_label, tgt_label, class_mask, g_start, src_emb, place),
        [matrix, matrix, row_vector, row_copies, array(src_emb.shape[::-1], src_emb.dtype)],
        [
            pltpu.VMEM(cost.shape, cost.dtype),
            pltpu.VMEM(row_shape, jnp.int32),
            pltpu.VMEM(col_shape, jnp.int32),
            pltpu.VMEM(class_mask.shape, jnp.int32),
            col_held,
            pltpu.VMEM(src_emb.shape, src_emb.dtype),
            pltpu.VMEM((LANES, tgt_cols), F32),
            row_held,
            pltpu.SemaphoreType.DMA((4,)),
            pltpu.SemaphoreType.DMA(row_shape[:1]),
            pltpu.SemaphoreType.DMA(row_shape[:1]),
        ],
        in_hbm=range(6),
        in_smem=(6,),
        name="first_row_logs",
    )

    def col_logs(parts, top, base_dual, base):
        return call(
            functools.partial(col_log_kernel, log_source),
            (parts, top, base_dual, base, score),
            [row_vector, col_copies],
            [row_held, col_held] + slow,
                name="col_logs",
        )

    zero = jnp.zeros(col_shape, F32)
    row1, copies = col_logs(exchanged(copies, "cols"), start_top, zero, start_base)
    base, top, col1, copies = call(
        functools.partial(rebase_kernel, log_target),
        (exchanged(copies, "rows"), score),
        [matrix, row_vector, col_vector, row_copies],
        [row_held],
        name="second_row_logs",
    )
    row2, copies = col_logs(exchanged(copies, "cols"), top, col1, base)
    col2, copies = call(
        functools.partial(row_log_kernel, log_target),
        (exchanged(copies, "rows"), top, col1, base, score),
        [col_vector, row_copies],
        [col_held, row_held] + slow,
        name="third_row_logs",
    )
    row3, copies = col_logs(exchanged(copies, "cols"), top, col1, base)

    def row_plan(first, parts, grad, dual, row):
        return call(
            functools.partial(row_plan_kernel, log_target, first),
            (parts, grad, dual, row, top, col1, base, score),
            [col_vector, row_copies],
            [col_held, col_held, row_held] + slow,
                name="row_plan",
        )

    def col_plan(parts, outer, dual, row):
        return call(
            functools.partial(col_plan_kernel, log_source),
            (parts, outer, dual, row, top, col1, base, score),
            [row_vector, col_copies],
            [row_held, col_held, col_held] + slow,
                name="col_plan",
        )

    none = jnp.zeros(row_shape, F32)
    col3, copies = row_plan(True, exchanged(copies, "rows"), g_bar, col2, row3)
    fbar3, copies = col_plan(exchanged(copies, "cols"), f_bar, col2, row3)
    gbar2, copies = row_plan(False, exchanged(copies, "rows"), g_bar, col2, row2)
    fbar2, copies = col_plan(exchanged(copies, "cols"), none, col1, row2)
    gbar1, copies = row_plan(False, exchanged(copies, "rows"), g_bar, col1, row1)
    parts = exchanged(copies, "cols")
    devices = [
        (x, y, z, core)
        for x in range(x_count)
        for y in range(y_count)
        for z in range(z_count)
        for core in range(2)
    ]

    def number(x, y, z, core):
        spot = (x % x_count * z_count + z % z_count) * y_count + y % y_count
        return spot * 2 + core

    def turn(value, axis, step):
        moves = []
        for device in devices:
            ahead = list(device)
            ahead[axis] += step * (1 - 2 * device[3])
            moves.append((number(*device), number(*ahead)))
        return lax.ppermute(value, ("rows", "cols"), moves)

    half = tgt_cols // 2
    z_rows, x_rows = x_count * owned, z_count * owned
    z_shape, z_riding = array((z_rows, half)), array((z_rows + 8, half))
    x_shape = array((x_rows, half))
    rounded, start, z_far, x_far, z_back, x_back = call(
        functools.partial(grad_kernel, log_source, log_target, counts),
        (
            place, parts, row1, row2, row3, col1, col2, col3, fbar2, fbar3, gbar1, gbar2, g_bar,
            top, base, src_turned, score,
        ),
        [array(cost.shape, jnp.bfloat16), col_vector, z_riding, x_shape, z_riding, x_shape],
        [pltpu.VMEM((row_shape[0], 8, LANES), F32), pltpu.VMEM((8, tgt_cols), F32)] + slow,
        in_smem=(0,),
        name="cost_grad",
    )
    z_up, z_down = turn(z_far, 2, 1), turn(z_back, 2, -1)
    x_up, x_down = turn(x_far, 0, 1), turn(x_back, 0, -1)
    chip_part = array((src_rows, width // 2))
    outs = call(
        functools.partial(parts_kernel, counts, y_count),
        (place, rounded, src_turned, tgt_emb),
        [chip_part] * 2 + [z_shape] * (z_count - 2) + [x_shape] * 2,
        [pltpu.VMEM((tgt_cols, width // 2), jnp.bfloat16)],
        in_smem=(0,),
        free=(3,),
        flops=BIG,
        name="grad_parts",
    )
    sent, kept, z_3, z_2, z_1, z_back2, z_back1, z_own, x_one, x_own = outs
    small = array((8, LANES))

    def step(kernel, arguments, outs, name, last=False, in_smem=()):
        return call(
            kernel,
            arguments,
            outs,
            loose=(len(arguments) - 1,),
            last=last,
            in_smem=in_smem,
            flops=STEP,
            name=name,
        )

    z_pay, z_back, start = step(
        z_kernel,
        (z_up, z_down, z_3, z_back2, start, kept),
        [z_riding, z_riding, small],
        "z_second",
    )
    z_up, z_down = turn(z_pay, 2, 1), turn(z_back, 2, -1)
    arrived = lax.ppermute(sent, "cols", [(at, at ^ 1) for at in range(col_count)])
    x_pay, x_sum, mark = step(
        x_kernel, (x_up, x_down, x_one, x_own, start), [x_shape, x_shape, small], "x_second"
    )
    x_up = turn(x_pay, 0, 1)
    z_pay, z_back, start = step(
        z_kernel,
        (z_up, z_down, z_2, z_back1, start, mark),
        [z_riding, z_riding, small],
        "z_third",
    )
    z_up, z_down = turn(z_pay, 2, 1), turn(z_back, 2, -1)
    y_shape = array((src_rows, width // col_count))
    far, one, back, own, mark = step(
        chip_kernel, (arrived, kept, start), [y_shape] * 4 + [small], "chip_sums"
    )
    y_up, y_down = turn(far, 1, 1), turn(back, 1, -1)
    first, mark = step(add_kernel, (x_sum, x_up, mark), [x_shape, small], "x_last")
    along_z = [[x * z_count + z for z in range(z_count)] for x in range(x_count)]
    first = lax.all_to_all(
        first.reshape(z_count, owned, half), "rows", 0, 0, tiled=True, axis_index_groups=along_z
    )
    z_pay, z_sum, start = step(
        last_z_kernel,
        (z_up, z_down, z_1, z_own, start, mark),
        [z_riding, z_shape, small],
        "z_fourth",
    )
    z_up = turn(z_pay, 2, 1)
    y_pay, y_sum, mark = step(
        x_kernel, (y_up, y_down, one, own, start), [y_shape, y_shape, small], "y_second"
    )
    y_up = turn(y_pay, 1, 1)
    last, riding = array((owned, half)), array((owned + 8, half))
    x_far, x_back, x_one, x_own, start = step(
        functools.partial(split_kernel, x_count),
        (place, z_up, z_sum, start, mark),
        [riding, riding, riding, last, small],
        "x_blocks",
        in_smem=(0,),
    )
    x_far, x_one, x_back = turn(x_far, 0, 2), turn(x_one, 0, 1), turn(x_back, 0, -1)
    grad_x, mark = step(
        turn_kernel,
        (y_sum, y_up, start),
        [array((width // col_count, src_rows)), small],
        "grad_x",
        last=True,
    )
    grad_y, start = call(
        last_kernel,
        (first, x_far, x_one, x_back, x_own, start),
        [array((owned, tgt_cols)), col_vector],
        name="last_step",
    )
    g_start_bar = start.reshape(tgt_cols)
    return (g_start_bar, grad_x, grad_y)


def solution(mesh):
    placed = (
        P("rows", "cols"),
        P("rows"),
        P("cols"),
        P(),
        P("cols"),
        P("rows"),
        P("cols"),
        P("rows", None),
        P("cols", None),
    )
    return jax.shard_map(
        body,
        mesh=mesh,
        in_specs=placed,
        out_specs=(P("cols"), P("cols", "rows"), P("rows", "cols")),
        check_vma=False,
    )
```

```python
import functools
import math

import jax
import jax.numpy as jnp
from jax import lax
from jax.experimental import pallas as pl
from jax.experimental.pallas import tpu as pltpu
from jax.sharding import PartitionSpec as P

K = 3


EPSILON = 0.05
PENALTY = 1.0
SCALE = 1.0 / (EPSILON * math.log(2.0))
LANES = 128
STRIP = 32
REACH = 40.0
FIRST_REACH = 75.0
VMEM_BYTES = 16 * 2**20
PINNED = 2**16
BIG = 2**32
STEP = 2**33
F32 = jnp.float32


def eye():
    return lax.broadcasted_iota(jnp.int32, (LANES, LANES), 0) == lax.broadcasted_iota(
        jnp.int32, (LANES, LANES), 1
    )


def to_column(row):
    return jnp.sum(jnp.where(eye(), row, 0.0), axis=1, keepdims=True)


def to_row(column):
    return jnp.sum(jnp.where(eye(), column, 0.0), axis=0, keepdims=True)


def log_combined(parts):
    top = jnp.max(parts, axis=0)
    return top + jnp.log2(jnp.sum(jnp.exp2(parts - top[None]), axis=0))


def spread(copies_ref, value):
    copies_ref[...] = jnp.broadcast_to(value[None], copies_ref.shape)


def groups_of(ref):
    return ref.shape[0]


def row_sums(base_ref, weight_ref, out_ref):
    for s in range(groups_of(out_ref)):
        held = None
        for c in range(groups_of(weight_ref)):
            tile = base_ref[s * LANES : (s + 1) * LANES, c * LANES : (c + 1) * LANES]
            term = tile * weight_ref[c : c + 1, :]
            held = term if held is None else held + term
        out_ref[s : s + 1, :] = to_row(jnp.sum(held, axis=1, keepdims=True))


def col_sums(base_ref, weight_ref, out_ref):
    held = [None] * groups_of(out_ref)
    for s in range(groups_of(weight_ref)):
        column = jnp.broadcast_to(to_column(weight_ref[s : s + 1, :]), (LANES, LANES))
        for c in range(len(held)):
            tile = base_ref[s * LANES : (s + 1) * LANES, c * LANES : (c + 1) * LANES]
            term = jnp.sum((tile * column).reshape(LANES // 8, 8, LANES), axis=0)
            held[c] = term if held[c] is None else held[c] + term
    for c, term in enumerate(held):
        out_ref[c : c + 1, :] = jnp.sum(term, axis=0, keepdims=True)


def strip_logs(scores):
    highest = jnp.max(scores, axis=1, keepdims=True)
    powers = jnp.exp2(scores - highest)
    return highest, powers, highest + jnp.log2(jnp.sum(powers, axis=1, keepdims=True))


def wide(ref):
    return jnp.concatenate([ref[c : c + 1, :] for c in range(groups_of(ref))], axis=1)


def load_rows(score_ref, tile_ref, group):
    tile_ref[...] = score_ref[pl.ds(pl.multiple_of(group * LANES, LANES), LANES), :]


def slow_row_logs(score_ref, tile_ref, col_ref, out_ref):
    @pl.loop(0, groups_of(out_ref))
    def _(group):
        load_rows(score_ref, tile_ref, group)
        logs = []
        for q in range(LANES // STRIP):
            logs.append(strip_logs(tile_ref[q * STRIP : (q + 1) * STRIP, :] + wide(col_ref))[2])
        out_ref[pl.ds(group, 1), :] = to_row(jnp.concatenate(logs, axis=0))


def slow_col_logs(score_ref, tile_ref, row_ref, out_ref):
    count = groups_of(out_ref)
    tops = tuple(jnp.full((1, LANES), -1e30, F32) for _ in range(count))

    def highest(group, tops):
        load_rows(score_ref, tile_ref, group)
        column = to_column(row_ref[pl.ds(group, 1), :])
        return tuple(
            jnp.maximum(
                tops[c],
                jnp.max(
                    tile_ref[:, c * LANES : (c + 1) * LANES] + column, axis=0, keepdims=True
                ),
            )
            for c in range(count)
        )

    tops = lax.fori_loop(0, groups_of(row_ref), highest, tops)
    sums = tuple(jnp.zeros((1, LANES), F32) for _ in range(count))

    def summed(group, sums):
        load_rows(score_ref, tile_ref, group)
        column = to_column(row_ref[pl.ds(group, 1), :])
        return tuple(
            sums[c]
            + jnp.sum(
                jnp.exp2(tile_ref[:, c * LANES : (c + 1) * LANES] + column - tops[c]),
                axis=0,
                keepdims=True,
            )
            for c in range(count)
        )

    sums = lax.fori_loop(0, groups_of(row_ref), summed, sums)
    for c in range(count):
        out_ref[c : c + 1, :] = tops[c] + jnp.log2(sums[c])


def slow_row_weighted(score_ref, tile_ref, row_ref, col_ref, weight_ref, out_ref):
    @pl.loop(0, groups_of(out_ref))
    def _(group):
        load_rows(score_ref, tile_ref, group)
        column = to_column(row_ref[pl.ds(group, 1), :])
        sums = []
        for q in range(LANES // STRIP):
            part = slice(q * STRIP, (q + 1) * STRIP)
            plan = jnp.exp2(tile_ref[part, :] + column[part] + wide(col_ref))
            sums.append(jnp.sum(plan * wide(weight_ref), axis=1, keepdims=True))
        out_ref[pl.ds(group, 1), :] = to_row(jnp.concatenate(sums, axis=0))


def slow_col_weighted(score_ref, tile_ref, row_ref, col_ref, weight_ref, out_ref):
    count = groups_of(out_ref)
    sums = tuple(jnp.zeros((1, LANES), F32) for _ in range(count))

    def summed(group, sums):
        load_rows(score_ref, tile_ref, group)
        column = to_column(row_ref[pl.ds(group, 1), :])
        weight = to_column(weight_ref[pl.ds(group, 1), :])
        return tuple(
            sums[c]
            + jnp.sum(
                weight
                * jnp.exp2(
                    tile_ref[:, c * LANES : (c + 1) * LANES] + column + col_ref[c : c + 1, :]
                ),
                axis=0,
                keepdims=True,
            )
            for c in range(count)
        )

    sums = lax.fori_loop(0, groups_of(row_ref), summed, sums)
    for c in range(count):
        out_ref[c : c + 1, :] = sums[c]


def first_kernel(
    cost_hbm, src_hbm, tgt_hbm, mask_hbm, dual_hbm, place_ref, score_ref, base_ref, top_ref,
    copies_ref, cost_ref, src_ref, tgt_ref, mask_ref, dual_ref, allowed_ref, log_ref, small_sem,
    cost_sem,
):
    small = [
        pltpu.make_async_copy(source, target, small_sem.at[at])
        for at, (source, target) in enumerate(
            ((tgt_hbm, tgt_ref), (mask_hbm, mask_ref), (src_hbm, src_ref), (dual_hbm, dual_ref))
        )
    ]
    for copy in small:
        copy.start()
    blocks = []
    for s in range(groups_of(log_ref)):
        rows = pl.ds(s * LANES, LANES)
        blocks.append(
            pltpu.make_async_copy(cost_hbm.at[rows, :], cost_ref.at[rows, :], cost_sem.at[s])
        )
        blocks[-1].start()
    for copy in small:
        copy.wait()
    classes = mask_ref.shape[0]
    mask = mask_ref[...].astype(F32).astype(jnp.bfloat16)
    ids = lax.broadcasted_iota(jnp.int32, (classes, LANES), 0)
    hot = jnp.concatenate(
        [
            jnp.where(tgt_ref[c : c + 1, :] == ids, 1.0, 0.0).astype(jnp.bfloat16)
            for c in range(groups_of(tgt_ref))
        ],
        axis=1,
    )
    allowed_of = jnp.dot(mask, hot, preferred_element_type=F32).astype(jnp.bfloat16)
    lane_ids = lax.broadcasted_iota(jnp.int32, (LANES, classes), 1).astype(F32)
    dual = wide(dual_ref) * SCALE - PENALTY * SCALE
    for s in range(groups_of(log_ref)):
        label = to_column(src_ref[s : s + 1, :].astype(F32))
        src_hot = jnp.where(label == lane_ids, 1.0, 0.0).astype(jnp.bfloat16)
        allowed_ref[...] = jnp.dot(src_hot, allowed_of, preferred_element_type=F32)
        blocks[s].wait()
        tops, logs = [], []
        for q in range(LANES // STRIP):
            rows = slice(s * LANES + q * STRIP, s * LANES + (q + 1) * STRIP)
            shifted = cost_ref[rows, :].astype(F32) - PENALTY * allowed_ref[
                q * STRIP : (q + 1) * STRIP, :
            ]
            scores = dual - shifted * SCALE
            highest, powers, log = strip_logs(scores)
            score_ref[rows, :] = scores
            base_ref[rows, :] = powers
            tops.append(highest)
            logs.append(log)
        top_ref[s : s + 1, :] = to_row(jnp.concatenate(tops, axis=0))
        log_ref[s : s + 1, :] = to_row(jnp.concatenate(logs, axis=0))
    spread(copies_ref, log_ref[...])


def rebase_kernel(
    log_target, parts_ref, start_top_ref, start_base_ref, score_ref,
    base_ref, top_ref, dual_ref, copies_ref, log_ref,
):
    dual_ref[...] = log_target - log_combined(parts_ref[...])
    top_ref[...] = start_top_ref[...]
    powers = jnp.exp2(dual_ref[...])
    for s in range(groups_of(log_ref)):
        rows = slice(s * LANES, (s + 1) * LANES)
        held = None
        for c in range(groups_of(dual_ref)):
            lanes = slice(c * LANES, (c + 1) * LANES)
            term = start_base_ref[rows, lanes] * powers[c : c + 1, :]
            base_ref[rows, lanes] = term
            held = term if held is None else held + term
        log_ref[s : s + 1, :] = to_row(jnp.sum(held, axis=1, keepdims=True))
    lowest = jnp.min(jnp.log2(jnp.maximum(log_ref[...], 1e-37)))
    near = jnp.logical_and(
        jnp.max(jnp.abs(dual_ref[...])) <= FIRST_REACH,
        lowest >= jnp.maximum(jnp.max(dual_ref[...]), 0.0) - 92.0,
    )

    @pl.when(near)
    def _():
        log_ref[...] = top_ref[...] + jnp.log2(log_ref[...])

    @pl.when(jnp.logical_not(near))
    def _():
        dual = wide(dual_ref)
        for s in range(groups_of(log_ref)):
            tops, logs = [], []
            for q in range(LANES // STRIP):
                rows = slice(s * LANES + q * STRIP, s * LANES + (q + 1) * STRIP)
                highest, powers, log = strip_logs(score_ref[rows, :] + dual)
                base_ref[rows, :] = powers
                tops.append(highest)
                logs.append(log)
            top_ref[s : s + 1, :] = to_row(jnp.concatenate(tops, axis=0))
            log_ref[s : s + 1, :] = to_row(jnp.concatenate(logs, axis=0))

    spread(copies_ref, log_ref[...])


def row_log_kernel(
    log_target, parts_ref, top_ref, base_dual_ref, base_ref, score_ref, dual_ref, copies_ref,
    weight_ref, sum_ref, tile_ref,
):
    dual_ref[...] = log_target - log_combined(parts_ref[...])
    lead = dual_ref[...] - base_dual_ref[...]
    weight_ref[...] = jnp.exp2(jnp.minimum(lead, 100.0))
    row_sums(base_ref, weight_ref, sum_ref)
    lowest = jnp.min(jnp.log2(jnp.maximum(sum_ref[...], 1e-37)))
    most = jnp.maximum(jnp.max(base_dual_ref[...]), 0.0) + jnp.maximum(jnp.max(lead), 0.0)
    near = jnp.logical_and(jnp.max(jnp.abs(lead)) <= REACH, lowest >= most - 92.0)

    @pl.when(near)
    def _():
        sum_ref[...] = top_ref[...] + jnp.log2(sum_ref[...])

    @pl.when(jnp.logical_not(near))
    def _():
        slow_row_logs(score_ref, tile_ref, dual_ref, sum_ref)

    spread(copies_ref, sum_ref[...])


def col_log_kernel(
    log_source, parts_ref, top_ref, base_dual_ref, base_ref, score_ref, dual_ref, copies_ref,
    weight_ref, sum_ref, tile_ref,
):
    dual_ref[...] = log_source - log_combined(parts_ref[...])
    lead = dual_ref[...] + top_ref[...]
    weight_ref[...] = jnp.exp2(jnp.minimum(lead, 100.0))
    col_sums(base_ref, weight_ref, sum_ref)
    most = jnp.max(lead)
    near = jnp.logical_and(
        most <= 60.0,
        jnp.min(
            jnp.log2(jnp.maximum(sum_ref[...], 1e-37)) - jnp.maximum(base_dual_ref[...], 0.0)
        )
        >= jnp.maximum(most, -15.0) - 85.0,
    )

    @pl.when(near)
    def _():
        sum_ref[...] = jnp.log2(sum_ref[...]) - base_dual_ref[...]

    @pl.when(jnp.logical_not(near))
    def _():
        slow_col_logs(score_ref, tile_ref, dual_ref, sum_ref)

    spread(copies_ref, sum_ref[...])


def row_plan_kernel(
    log_target, first, parts_ref, grad_ref, dual_in_ref, row_dual_ref, top_ref, base_dual_ref,
    base_ref, score_ref, out_ref, copies_ref, weight_ref, col_ref, sum_ref, tile_ref,
):
    if first:
        dual = log_target - log_combined(parts_ref[...])
        grad = grad_ref[...]
        out_ref[...] = dual
    else:
        dual = dual_in_ref[...]
        grad = -jnp.sum(parts_ref[...], axis=0)
        out_ref[...] = grad
    lead = dual - base_dual_ref[...]
    row_lead = row_dual_ref[...] + top_ref[...]
    most = jnp.max(row_lead) + jnp.maximum(jnp.max(base_dual_ref[...]), 0.0)
    near = jnp.logical_and(
        jnp.max(jnp.abs(lead)) <= REACH, most + jnp.maximum(jnp.max(lead), 0.0) <= 70.0
    )

    @pl.when(near)
    def _():
        weight_ref[...] = jnp.exp2(lead - log_target) * grad
        row_sums(base_ref, weight_ref, sum_ref)
        sum_ref[...] = sum_ref[...] * jnp.exp2(row_lead)

    @pl.when(jnp.logical_not(near))
    def _():
        col_ref[...] = dual - log_target
        weight_ref[...] = grad
        slow_row_weighted(score_ref, tile_ref, row_dual_ref, col_ref, weight_ref, sum_ref)

    spread(copies_ref, sum_ref[...])


def col_plan_kernel(
    log_source, parts_ref, outer_ref, dual_ref, row_dual_ref, top_ref, base_dual_ref, base_ref,
    score_ref, out_ref, copies_ref, weight_ref, col_ref, sum_ref, tile_ref,
):
    grad = outer_ref[...] - jnp.sum(parts_ref[...], axis=0)
    out_ref[...] = grad
    lead = dual_ref[...] - base_dual_ref[...]
    row_lead = row_dual_ref[...] + top_ref[...]
    most = jnp.max(row_lead) + jnp.maximum(jnp.max(base_dual_ref[...]), 0.0)
    near = jnp.logical_and(
        jnp.max(jnp.abs(lead)) <= REACH, most + jnp.maximum(jnp.max(lead), 0.0) <= 70.0
    )

    @pl.when(near)
    def _():
        weight_ref[...] = jnp.exp2(row_lead) * grad
        col_sums(base_ref, weight_ref, sum_ref)
        sum_ref[...] = sum_ref[...] * jnp.exp2(lead - log_source)

    @pl.when(jnp.logical_not(near))
    def _():
        col_ref[...] = dual_ref[...] - log_source
        weight_ref[...] = grad
        slow_col_weighted(score_ref, tile_ref, row_dual_ref, col_ref, weight_ref, sum_ref)

    spread(copies_ref, sum_ref[...])


def direction(place_ref):
    return 1 - 2 * place_ref[3]


def ring_place(place_ref, axis, offset, count):
    return lax.rem(place_ref[axis] + direction(place_ref) * offset + count, count)


def z_block(place_ref, src_ref, grad_ref, offset, counts):
    x_count, z_count = counts
    width, half = src_ref.shape[0], grad_ref.shape[1] // 2
    owned = width // (x_count * z_count)
    at = ring_place(place_ref, 2, offset, z_count)
    rows = [
        src_ref[pl.ds(pl.multiple_of((x * z_count + at) * owned, owned), owned), :]
        for x in range(x_count)
    ]
    return jnp.dot(
        jnp.concatenate(rows, axis=0), grad_ref[:, half:], preferred_element_type=F32
    )


def x_block(place_ref, src_ref, grad_ref, offset, counts):
    x_count = counts[0]
    width, half = src_ref.shape[0], grad_ref.shape[1] // 2
    owned = width // x_count
    at = ring_place(place_ref, 0, offset, x_count)
    rows = src_ref[pl.ds(pl.multiple_of(at * owned, owned), owned), :]
    return jnp.dot(rows, grad_ref[:, :half], preferred_element_type=F32)


def pieces(value):
    first = value.astype(jnp.bfloat16).astype(F32)
    second = (value - first).astype(jnp.bfloat16).astype(F32)
    return first, second, value - first - second


def grad_kernel(
    log_source, log_target, counts, place_ref, parts_ref, row1, row2, row3, col1, col2, col3,
    fbar2, fbar3, gbar1, gbar2, gbar3, top_ref, base_ref, emb_ref, score_ref,
    out_ref, src_ref, start_ref, z_far_ref, x_far_ref, z_back_ref, x_back_ref, rows_ref, cols_ref, tile_ref,
):
    fbar1 = -jnp.sum(parts_ref[...], axis=0)
    leads = [ref[...] - col1[...] for ref in (col2, col3)]
    row_leads = [ref[...] + top_ref[...] for ref in (row1, row2, row3)]
    most = jnp.max(jnp.maximum(jnp.maximum(row_leads[0], row_leads[1]), row_leads[2]))
    most = most + jnp.maximum(jnp.max(col1[...]), 0.0)
    ahead = jnp.maximum(jnp.max(jnp.maximum(leads[0], leads[1])), 0.0)
    near = jnp.logical_and(
        jnp.maximum(jnp.max(jnp.abs(leads[0])), jnp.max(jnp.abs(leads[1]))) <= REACH,
        jnp.logical_and(jnp.max(jnp.abs(col1[...])) <= FIRST_REACH, most + ahead <= 70.0),
    )
    count, groups = groups_of(col1), groups_of(row1)

    @pl.when(near)
    def _():
        powers = [-jnp.exp2(lead) for lead in row_leads]
        factors = [*powers, powers[1] * fbar2[...], powers[2] * fbar3[...], powers[0] * fbar1]
        for k in range(8):
            rows_ref[:, k, :] = factors[k] if k < 6 else jnp.zeros_like(fbar1)
        column_factors = [
            jnp.exp2(jnp.full_like(leads[0], -log_target)) * gbar1[...],
            jnp.exp2(leads[0] - log_target) * gbar2[...],
            jnp.exp2(leads[1] - log_target) * gbar3[...],
            jnp.exp2(jnp.full_like(leads[0], -log_source)),
            jnp.exp2(leads[0] - log_source),
            jnp.exp2(-col1[...] - log_source),
        ]
        cols_ref[...] = jnp.zeros_like(cols_ref)
        for k, factor in enumerate(column_factors):
            for c in range(count):
                cols_ref[k : k + 1, c * LANES : (c + 1) * LANES] = factor[c : c + 1, :]
        b1, b2, b3 = pieces(cols_ref[...])
        right = jnp.concatenate([b1, b2, b1, b2, b3, b1], axis=0).astype(jnp.bfloat16)
        held = [None] * count
        for s in range(groups):
            a1, a2, a3 = pieces(rows_ref[s])
            left = jnp.concatenate([a1, a1, a2, a2, a1, a3], axis=0).astype(jnp.bfloat16)
            tile_ref[...] = lax.dot_general(
                left, right, (((0,), (0,)), ((), ())), preferred_element_type=F32
            )
            column = jnp.broadcast_to(to_column(rows_ref[s, 5:6, :]), (LANES, LANES))
            rows = slice(s * LANES, (s + 1) * LANES)
            src_ref[:, rows] = emb_ref[rows, :].T
            for c in range(count):
                lanes = slice(c * LANES, (c + 1) * LANES)
                base = base_ref[rows, lanes]
                out_ref[rows, lanes] = (base * tile_ref[:, lanes]).astype(jnp.bfloat16)
                term = jnp.sum((base * column).reshape(LANES // 8, 8, LANES), axis=0)
                held[c] = term if held[c] is None else held[c] + term
        for c, term in enumerate(held):
            start_ref[c : c + 1, :] = (
                jnp.sum(term, axis=0, keepdims=True) * column_factors[5][c : c + 1, :]
            )

    @pl.when(jnp.logical_not(near))
    def _():
        zero = jnp.zeros_like(fbar1)
        for k, value in enumerate(
            (row1[...], row2[...], row3[...], fbar1, fbar2[...], fbar3[...], zero, zero)
        ):
            rows_ref[:, k, :] = value
        start_ref[...] = jnp.zeros_like(start_ref)
        for s in range(groups):
            src_ref[:, s * LANES : (s + 1) * LANES] = emb_ref[s * LANES : (s + 1) * LANES, :].T
        columns_of = (None, col1, col2, col3)
        grads_of = (None, gbar1, gbar2, gbar3)

        @pl.loop(0, groups)
        def _(group):
            load_rows(score_ref, tile_ref, group)
            taken = rows_ref[group]
            columns = [to_column(taken[k : k + 1, :]) for k in range(6)]
            rows = pl.ds(pl.multiple_of(group * LANES, LANES), LANES)
            for c in range(count):
                lanes = slice(c * LANES, (c + 1) * LANES)
                value = jnp.zeros((LANES, LANES), F32)
                for k in reversed(range(3)):
                    scores = tile_ref[:, lanes] + columns[k]
                    plan_q = jnp.exp2(scores + (columns_of[k + 1][c : c + 1, :] - log_target))
                    value = value + plan_q * grads_of[k + 1][c : c + 1, :]
                    before = columns_of[k][c : c + 1, :] if k else jnp.zeros((1, LANES), F32)
                    term = jnp.exp2(scores + (before - log_source)) * columns[3 + k]
                    value = value + term
                    if not k:
                        start_ref[c : c + 1, :] -= jnp.sum(term, axis=0, keepdims=True)
                out_ref[rows, lanes] = (-value).astype(jnp.bfloat16)

    reach = counts[1] // 2
    put(z_far_ref, z_block(place_ref, src_ref, out_ref, reach, counts), start_ref[...])
    put(z_back_ref, z_block(place_ref, src_ref, out_ref, 1 - reach, counts), start_ref[...])
    x_far_ref[...] = x_block(place_ref, src_ref, out_ref, counts[0] // 2, counts)
    x_back_ref[...] = x_block(place_ref, src_ref, out_ref, -1, counts)


def put(out_ref, block, rider):
    rows = block.shape[0]
    out_ref[:rows, :] = block
    out_ref[rows:, :] = jnp.zeros_like(out_ref[rows:, :])
    out_ref[rows:, :LANES] = rider


def rider(ref):
    return ref[ref.shape[0] - 8 :, :LANES]


def x_part(y_count, place_ref, grad_ref, tgt_ref, sent_ref, kept_ref, order_ref):
    block = tgt_ref.shape[1] // (2 * y_count)
    core, turn = place_ref[3], direction(place_ref)
    for side, out_ref in ((0, sent_ref), (1, kept_ref)):
        for k, offset in enumerate((2, 1, -1, 0)):
            step = offset * (2 * side - 1)
            at = lax.rem(place_ref[1] + turn * step + y_count, y_count)
            owner = at * 2 + (core if side else 1 - core)
            order_ref[:, k * block : (k + 1) * block] = tgt_ref[
                :, pl.ds(pl.multiple_of(owner * block, block), block)
            ]
        out_ref[...] = jnp.dot(grad_ref[...], order_ref[...], preferred_element_type=F32)


def parts_kernel(
    counts, y_count, place_ref, grad_ref, src_ref, tgt_ref, sent_ref, kept_ref, *outs
):
    *outs, order_ref = outs
    x_part(y_count, place_ref, grad_ref, tgt_ref, sent_ref, kept_ref, order_ref)
    reach = counts[1] // 2
    offsets = [*range(reach - 1, 0, -1), *range(2 - reach, 1)]
    for out_ref, offset in zip(outs, offsets):
        out_ref[...] = z_block(place_ref, src_ref, grad_ref, offset, counts)
    for out_ref, offset in zip(outs[len(offsets) :], (1, 0)):
        out_ref[...] = x_block(place_ref, src_ref, grad_ref, offset, counts)


def forward(out_ref, block_ref, arrived_ref):
    rows = block_ref.shape[0]
    out_ref[:rows, :] = block_ref[...] + arrived_ref[:rows, :]
    out_ref[rows:, :] = arrived_ref[rows:, :]


def token(ref):
    ref[...] = jnp.zeros_like(ref)


def z_kernel(up_ref, down_ref, ahead_ref, behind_ref, start_ref, after_ref, z_ref, back_ref, held_ref):
    forward(z_ref, ahead_ref, up_ref)
    forward(back_ref, behind_ref, down_ref)
    held_ref[...] = start_ref[...] + rider(up_ref) + rider(down_ref)


def x_kernel(up_ref, down_ref, one_ref, own_ref, after_ref, pay_ref, sum_ref, token_ref):
    pay_ref[...] = one_ref[...] + up_ref[...]
    sum_ref[...] = own_ref[...] + down_ref[...]
    token(token_ref)


def add_kernel(one_ref, other_ref, after_ref, sum_ref, token_ref):
    sum_ref[...] = one_ref[...] + other_ref[...]
    token(token_ref)


def chip_kernel(arrived_ref, kept_ref, after_ref, *outs):
    block = outs[0].shape[1]
    for k, out_ref in enumerate(outs[:-1]):
        lanes = slice(k * block, (k + 1) * block)
        out_ref[...] = kept_ref[:, lanes] + arrived_ref[:, lanes]
    token(outs[-1])


def last_z_kernel(
    up_ref, down_ref, ahead_ref, own_ref, start_ref, after_ref, z_ref, z_sum_ref, held_ref
):
    forward(z_ref, ahead_ref, up_ref)
    z_sum_ref[...] = own_ref[...] + down_ref[: own_ref.shape[0], :]
    held_ref[...] = start_ref[...] + rider(up_ref) + rider(down_ref)


def split_kernel(
    x_count, place_ref, z_up_ref, z_sum_ref, start_ref, after_ref,
    far_ref, back_ref, one_ref, last_ref, held_ref,
):
    held_ref[...] = start_ref[...] + rider(z_up_ref)
    block = z_sum_ref.shape[0] // x_count
    for out_ref, offset in ((far_ref, 2), (back_ref, -1), (one_ref, 1), (last_ref, 0)):
        at = ring_place(place_ref, 0, offset, x_count)
        rows = pl.ds(pl.multiple_of(at * block, block), block)
        value = z_sum_ref[rows, :] + z_up_ref[rows, :]
        if offset:
            put(out_ref, value, held_ref[...])
        else:
            out_ref[...] = value


def turn_kernel(sum_ref, up_ref, after_ref, out_ref, token_ref):
    for s in range(sum_ref.shape[0] // LANES):
        rows = slice(s * LANES, (s + 1) * LANES)
        out_ref[:, rows] = (sum_ref[rows, :] + up_ref[rows, :]).T
    token(token_ref)


def last_kernel(parts_ref, far_ref, one_ref, back_ref, own_ref, start_ref, out_ref, held_ref):
    rows, half = own_ref.shape
    out_ref[:, :half] = jnp.sum(parts_ref[...], axis=0)
    value, held = own_ref[...], start_ref[...]
    for ref in (far_ref, one_ref, back_ref):
        value = value + ref[:rows, :]
        held = held + rider(ref)
    out_ref[:, half:] = value
    held_ref[...] = held


def call(
    kernel, arguments, outs, scratch=(), in_hbm=(), loose=(), in_smem=(), free=(), last=False, flops=1024, name=None
):
    spaces, values = [], []
    for at, value in enumerate(arguments):
        space = pltpu.VMEM
        if at in in_hbm:
            space = pltpu.HBM
        elif at in loose:
            space = pl.ANY
        elif at in in_smem:
            space = pltpu.SMEM
        if at in in_hbm or (space is pltpu.VMEM and value.size >= PINNED and at not in free):
            value = pltpu.with_memory_space_constraint(value, space)
        spaces.append(space)
        values.append(value)
    return pl.pallas_call(
        kernel,
        out_shape=[
            pltpu.VMEM(out.shape, out.dtype) if math.prod(out.shape) >= PINNED and not last else out
            for out in outs
        ],
        in_specs=[pl.BlockSpec(memory_space=space) for space in spaces],
        out_specs=[pl.BlockSpec(memory_space=pltpu.VMEM)] * len(outs),
        scratch_shapes=list(scratch),
        compiler_params=pltpu.CompilerParams(vmem_limit_bytes=VMEM_BYTES),
        cost_estimate=pl.CostEstimate(flops=flops, bytes_accessed=1024, transcendentals=0),
        name=name,
    )(*values)


def exchanged(copies, axis):
    return lax.all_to_all(copies, axis, 0, 0, tiled=True)


def body(cost, src_label, tgt_label, class_mask, g_start, f_bar, g_bar, src_emb, tgt_emb):
    row_count = lax.axis_size("rows")
    col_count = lax.axis_size("cols")
    src_rows, tgt_cols = cost.shape
    width = src_emb.shape[1]
    log_source = -math.log2(src_rows * row_count)
    log_target = -math.log2(tgt_cols * col_count)
    row_shape = (src_rows // LANES, LANES)
    col_shape = (tgt_cols // LANES, LANES)
    src_label, f_bar = src_label.reshape(row_shape), f_bar.reshape(row_shape)
    tgt_label, g_bar = tgt_label.reshape(col_shape), g_bar.reshape(col_shape)
    g_start = g_start.reshape(col_shape)

    def array(shape, dtype=F32):
        return jax.ShapeDtypeStruct(shape, dtype)

    matrix = array(cost.shape)
    row_vector, col_vector = array(row_shape), array(col_shape)
    row_copies = array((col_count,) + row_shape)
    col_copies = array((row_count,) + col_shape)
    row_held, col_held = pltpu.VMEM(row_shape, F32), pltpu.VMEM(col_shape, F32)
    slow = [pltpu.VMEM((LANES, tgt_cols), F32)]

    x_count, z_count, y_count = 4, row_count // 4, col_count // 2
    counts = (x_count, z_count)
    owned = width // row_count
    row_at, col_at = lax.axis_index("rows"), lax.axis_index("cols")
    place = jnp.stack(
        [row_at // z_count, col_at // 2, row_at % z_count, col_at % 2]
    ).astype(jnp.int32)
    score, start_base, start_top, copies = call(
        first_kernel,
        (cost, src_label, tgt_label, class_mask, g_start, place),
        [matrix, matrix, row_vector, row_copies],
        [
            pltpu.VMEM(cost.shape, cost.dtype),
            pltpu.VMEM(row_shape, jnp.int32),
            pltpu.VMEM(col_shape, jnp.int32),
            pltpu.VMEM(class_mask.shape, jnp.int32),
            col_held,
            pltpu.VMEM((LANES, tgt_cols), F32),
            row_held,
            pltpu.SemaphoreType.DMA((4,)),
            pltpu.SemaphoreType.DMA(row_shape[:1]),
        ],
        in_hbm=range(5),
        in_smem=(5,),
        name="first_row_logs",
    )

    def col_logs(parts, top, base_dual, base):
        return call(
            functools.partial(col_log_kernel, log_source),
            (parts, top, base_dual, base, score),
            [row_vector, col_copies],
            [row_held, col_held] + slow,
                name="col_logs",
        )

    zero = jnp.zeros(col_shape, F32)
    row1, copies = col_logs(exchanged(copies, "cols"), start_top, zero, start_base)
    base, top, col1, copies = call(
        functools.partial(rebase_kernel, log_target),
        (exchanged(copies, "rows"), start_top, start_base, score),
        [matrix, row_vector, col_vector, row_copies],
        [row_held],
        name="second_row_logs",
    )
    row2, copies = col_logs(exchanged(copies, "cols"), top, col1, base)
    col2, copies = call(
        functools.partial(row_log_kernel, log_target),
        (exchanged(copies, "rows"), top, col1, base, score),
        [col_vector, row_copies],
        [col_held, row_held] + slow,
        name="third_row_logs",
    )
    row3, copies = col_logs(exchanged(copies, "cols"), top, col1, base)

    def row_plan(first, parts, grad, dual, row):
        return call(
            functools.partial(row_plan_kernel, log_target, first),
            (parts, grad, dual, row, top, col1, base, score),
            [col_vector, row_copies],
            [col_held, col_held, row_held] + slow,
                name="row_plan",
        )

    def col_plan(parts, outer, dual, row):
        return call(
            functools.partial(col_plan_kernel, log_source),
            (parts, outer, dual, row, top, col1, base, score),
            [row_vector, col_copies],
            [row_held, col_held, col_held] + slow,
                name="col_plan",
        )

    none = jnp.zeros(row_shape, F32)
    col3, copies = row_plan(True, exchanged(copies, "rows"), g_bar, col2, row3)
    fbar3, copies = col_plan(exchanged(copies, "cols"), f_bar, col2, row3)
    gbar2, copies = row_plan(False, exchanged(copies, "rows"), g_bar, col2, row2)
    fbar2, copies = col_plan(exchanged(copies, "cols"), none, col1, row2)
    gbar1, copies = row_plan(False, exchanged(copies, "rows"), g_bar, col1, row1)
    parts = exchanged(copies, "cols")
    devices = [
        (x, y, z, core)
        for x in range(x_count)
        for y in range(y_count)
        for z in range(z_count)
        for core in range(2)
    ]

    def number(x, y, z, core):
        spot = (x % x_count * z_count + z % z_count) * y_count + y % y_count
        return spot * 2 + core

    def turn(value, axis, step):
        moves = []
        for device in devices:
            ahead = list(device)
            ahead[axis] += step * (1 - 2 * device[3])
            moves.append((number(*device), number(*ahead)))
        return lax.ppermute(value, ("rows", "cols"), moves)

    half = tgt_cols // 2
    z_rows, x_rows = x_count * owned, z_count * owned
    z_shape, z_riding = array((z_rows, half)), array((z_rows + 8, half))
    x_shape = array((x_rows, half))
    rounded, src_turned, start, z_far, x_far, z_back, x_back = call(
        functools.partial(grad_kernel, log_source, log_target, counts),
        (
            place, parts, row1, row2, row3, col1, col2, col3, fbar2, fbar3, gbar1, gbar2, g_bar,
            top, base, src_emb, score,
        ),
        [
            array(cost.shape, jnp.bfloat16),
            array(src_emb.shape[::-1], src_emb.dtype),
            col_vector,
            z_riding,
            x_shape,
            z_riding,
            x_shape,
        ],
        [pltpu.VMEM((row_shape[0], 8, LANES), F32), pltpu.VMEM((8, tgt_cols), F32)] + slow,
        free=(15,),
        in_smem=(0,),
        name="cost_grad",
    )
    z_up, z_down = turn(z_far, 2, 1), turn(z_back, 2, -1)
    x_up, x_down = turn(x_far, 0, 1), turn(x_back, 0, -1)
    chip_part = array((src_rows, width // 2))
    outs = call(
        functools.partial(parts_kernel, counts, y_count),
        (place, rounded, src_turned, tgt_emb),
        [chip_part] * 2 + [z_shape] * (z_count - 2) + [x_shape] * 2,
        [pltpu.VMEM((tgt_cols, width // 2), jnp.bfloat16)],
        in_smem=(0,),
        free=(3,),
        flops=BIG,
        name="grad_parts",
    )
    sent, kept, z_3, z_2, z_1, z_back2, z_back1, z_own, x_one, x_own = outs
    small = array((8, LANES))

    def step(kernel, arguments, outs, name, last=False, in_smem=()):
        return call(
            kernel,
            arguments,
            outs,
            loose=(len(arguments) - 1,),
            last=last,
            in_smem=in_smem,
            flops=STEP,
            name=name,
        )

    z_pay, z_back, start = step(
        z_kernel,
        (z_up, z_down, z_3, z_back2, start, kept),
        [z_riding, z_riding, small],
        "z_second",
    )
    z_up, z_down = turn(z_pay, 2, 1), turn(z_back, 2, -1)
    arrived = lax.ppermute(sent, "cols", [(at, at ^ 1) for at in range(col_count)])
    x_pay, x_sum, mark = step(
        x_kernel, (x_up, x_down, x_one, x_own, start), [x_shape, x_shape, small], "x_second"
    )
    x_up = turn(x_pay, 0, 1)
    z_pay, z_back, start = step(
        z_kernel,
        (z_up, z_down, z_2, z_back1, start, mark),
        [z_riding, z_riding, small],
        "z_third",
    )
    z_up, z_down = turn(z_pay, 2, 1), turn(z_back, 2, -1)
    y_shape = array((src_rows, width // col_count))
    far, one, back, own, mark = step(
        chip_kernel, (arrived, kept, start), [y_shape] * 4 + [small], "chip_sums"
    )
    y_up, y_down = turn(far, 1, 1), turn(back, 1, -1)
    first, mark = step(add_kernel, (x_sum, x_up, mark), [x_shape, small], "x_last")
    along_z = [[x * z_count + z for z in range(z_count)] for x in range(x_count)]
    first = lax.all_to_all(
        first.reshape(z_count, owned, half), "rows", 0, 0, tiled=True, axis_index_groups=along_z
    )
    z_pay, z_sum, start = step(
        last_z_kernel,
        (z_up, z_down, z_1, z_own, start, mark),
        [z_riding, z_shape, small],
        "z_fourth",
    )
    z_up = turn(z_pay, 2, 1)
    y_pay, y_sum, mark = step(
        x_kernel, (y_up, y_down, one, own, start), [y_shape, y_shape, small], "y_second"
    )
    y_up = turn(y_pay, 1, 1)
    last, riding = array((owned, half)), array((owned + 8, half))
    x_far, x_back, x_one, x_own, start = step(
        functools.partial(split_kernel, x_count),
        (place, z_up, z_sum, start, mark),
        [riding, riding, riding, last, small],
        "x_blocks",
        in_smem=(0,),
    )
    x_far, x_one, x_back = turn(x_far, 0, 2), turn(x_one, 0, 1), turn(x_back, 0, -1)
    grad_x, mark = step(
        turn_kernel,
        (y_sum, y_up, start),
        [array((width // col_count, src_rows)), small],
        "grad_x",
        last=True,
    )
    grad_y, start = call(
        last_kernel,
        (first, x_far, x_one, x_back, x_own, start),
        [array((owned, tgt_cols)), col_vector],
        name="last_step",
    )
    g_start_bar = start.reshape(tgt_cols)
    return (g_start_bar, grad_x, grad_y)


def solution(mesh):
    placed = (
        P("rows", "cols"),
        P("rows"),
        P("cols"),
        P(),
        P("cols"),
        P("rows"),
        P("cols"),
        P("rows", None),
        P("cols", None),
    )
    return jax.shard_map(
        body,
        mesh=mesh,
        in_specs=placed,
        out_specs=(P("cols"), P("cols", "rows"), P("rows", "cols")),
        check_vma=False,
    )
```

```python
import functools
import math

import jax
import jax.numpy as jnp
from jax import lax
from jax.experimental import pallas as pl
from jax.experimental.pallas import tpu as pltpu
from jax.sharding import PartitionSpec as P

K = 3


EPSILON = 0.05
PENALTY = 1.0
SCALE = 1.0 / (EPSILON * math.log(2.0))
LANES = 128
STRIP = 32
REACH = 40.0
FIRST_REACH = 75.0
VMEM_BYTES = 16 * 2**20
PINNED = 2**16
BIG = 2**32
STEP = 2**33
F32 = jnp.float32


def eye():
    return lax.broadcasted_iota(jnp.int32, (LANES, LANES), 0) == lax.broadcasted_iota(
        jnp.int32, (LANES, LANES), 1
    )


def to_column(row):
    return jnp.sum(jnp.where(eye(), row, 0.0), axis=1, keepdims=True)


def to_row(column):
    return jnp.sum(jnp.where(eye(), column, 0.0), axis=0, keepdims=True)


def log_combined(parts):
    top = jnp.max(parts, axis=0)
    return top + jnp.log2(jnp.sum(jnp.exp2(parts - top[None]), axis=0))


def spread(copies_ref, value):
    copies_ref[...] = jnp.broadcast_to(value[None], copies_ref.shape)


def groups_of(ref):
    return ref.shape[0]


def row_sums(base_ref, weight_ref, out_ref):
    for s in range(groups_of(out_ref)):
        held = None
        for c in range(groups_of(weight_ref)):
            tile = base_ref[s * LANES : (s + 1) * LANES, c * LANES : (c + 1) * LANES]
            term = tile * weight_ref[c : c + 1, :]
            held = term if held is None else held + term
        out_ref[s : s + 1, :] = to_row(jnp.sum(held, axis=1, keepdims=True))


def col_sums(base_ref, weight_ref, out_ref):
    held = [None] * groups_of(out_ref)
    for s in range(groups_of(weight_ref)):
        column = jnp.broadcast_to(to_column(weight_ref[s : s + 1, :]), (LANES, LANES))
        for c in range(len(held)):
            tile = base_ref[s * LANES : (s + 1) * LANES, c * LANES : (c + 1) * LANES]
            term = jnp.sum((tile * column).reshape(LANES // 8, 8, LANES), axis=0)
            held[c] = term if held[c] is None else held[c] + term
    for c, term in enumerate(held):
        out_ref[c : c + 1, :] = jnp.sum(term, axis=0, keepdims=True)


def strip_logs(scores):
    highest = jnp.max(scores, axis=1, keepdims=True)
    powers = jnp.exp2(scores - highest)
    return highest, powers, highest + jnp.log2(jnp.sum(powers, axis=1, keepdims=True))


def wide(ref):
    return jnp.concatenate([ref[c : c + 1, :] for c in range(groups_of(ref))], axis=1)


def load_rows(score_ref, tile_ref, group):
    tile_ref[...] = score_ref[pl.ds(pl.multiple_of(group * LANES, LANES), LANES), :]


def slow_row_logs(score_ref, tile_ref, col_ref, out_ref):
    @pl.loop(0, groups_of(out_ref))
    def _(group):
        load_rows(score_ref, tile_ref, group)
        logs = []
        for q in range(LANES // STRIP):
            logs.append(strip_logs(tile_ref[q * STRIP : (q + 1) * STRIP, :] + wide(col_ref))[2])
        out_ref[pl.ds(group, 1), :] = to_row(jnp.concatenate(logs, axis=0))


def slow_col_logs(score_ref, tile_ref, row_ref, out_ref):
    count = groups_of(out_ref)
    tops = tuple(jnp.full((1, LANES), -1e30, F32) for _ in range(count))

    def highest(group, tops):
        load_rows(score_ref, tile_ref, group)
        column = to_column(row_ref[pl.ds(group, 1), :])
        return tuple(
            jnp.maximum(
                tops[c],
                jnp.max(
                    tile_ref[:, c * LANES : (c + 1) * LANES] + column, axis=0, keepdims=True
                ),
            )
            for c in range(count)
        )

    tops = lax.fori_loop(0, groups_of(row_ref), highest, tops)
    sums = tuple(jnp.zeros((1, LANES), F32) for _ in range(count))

    def summed(group, sums):
        load_rows(score_ref, tile_ref, group)
        column = to_column(row_ref[pl.ds(group, 1), :])
        return tuple(
            sums[c]
            + jnp.sum(
                jnp.exp2(tile_ref[:, c * LANES : (c + 1) * LANES] + column - tops[c]),
                axis=0,
                keepdims=True,
            )
            for c in range(count)
        )

    sums = lax.fori_loop(0, groups_of(row_ref), summed, sums)
    for c in range(count):
        out_ref[c : c + 1, :] = tops[c] + jnp.log2(sums[c])


def slow_row_weighted(score_ref, tile_ref, row_ref, col_ref, weight_ref, out_ref):
    @pl.loop(0, groups_of(out_ref))
    def _(group):
        load_rows(score_ref, tile_ref, group)
        column = to_column(row_ref[pl.ds(group, 1), :])
        sums = []
        for q in range(LANES // STRIP):
            part = slice(q * STRIP, (q + 1) * STRIP)
            plan = jnp.exp2(tile_ref[part, :] + column[part] + wide(col_ref))
            sums.append(jnp.sum(plan * wide(weight_ref), axis=1, keepdims=True))
        out_ref[pl.ds(group, 1), :] = to_row(jnp.concatenate(sums, axis=0))


def slow_col_weighted(score_ref, tile_ref, row_ref, col_ref, weight_ref, out_ref):
    count = groups_of(out_ref)
    sums = tuple(jnp.zeros((1, LANES), F32) for _ in range(count))

    def summed(group, sums):
        load_rows(score_ref, tile_ref, group)
        column = to_column(row_ref[pl.ds(group, 1), :])
        weight = to_column(weight_ref[pl.ds(group, 1), :])
        return tuple(
            sums[c]
            + jnp.sum(
                weight
                * jnp.exp2(
                    tile_ref[:, c * LANES : (c + 1) * LANES] + column + col_ref[c : c + 1, :]
                ),
                axis=0,
                keepdims=True,
            )
            for c in range(count)
        )

    sums = lax.fori_loop(0, groups_of(row_ref), summed, sums)
    for c in range(count):
        out_ref[c : c + 1, :] = sums[c]


def first_kernel(
    cost_hbm, src_hbm, tgt_hbm, mask_hbm, dual_hbm, score_ref, base_ref, top_ref,
    copies_ref, cost_ref, src_ref, tgt_ref, mask_ref, dual_ref, allowed_ref, log_ref, small_sem,
    cost_sem,
):
    small = [
        pltpu.make_async_copy(source, target, small_sem.at[at])
        for at, (source, target) in enumerate(
            ((tgt_hbm, tgt_ref), (mask_hbm, mask_ref), (src_hbm, src_ref), (dual_hbm, dual_ref))
        )
    ]
    for copy in small:
        copy.start()
    blocks = []
    for s in range(groups_of(log_ref)):
        rows = pl.ds(s * LANES, LANES)
        blocks.append(
            pltpu.make_async_copy(cost_hbm.at[rows, :], cost_ref.at[rows, :], cost_sem.at[s])
        )
        blocks[-1].start()
    for copy in small:
        copy.wait()
    classes = mask_ref.shape[0]
    mask = mask_ref[...].astype(F32).astype(jnp.bfloat16)
    ids = lax.broadcasted_iota(jnp.int32, (classes, LANES), 0)
    hot = jnp.concatenate(
        [
            jnp.where(tgt_ref[c : c + 1, :] == ids, 1.0, 0.0).astype(jnp.bfloat16)
            for c in range(groups_of(tgt_ref))
        ],
        axis=1,
    )
    allowed_of = jnp.dot(mask, hot, preferred_element_type=F32).astype(jnp.bfloat16)
    lane_ids = lax.broadcasted_iota(jnp.int32, (LANES, classes), 1).astype(F32)
    dual = wide(dual_ref) * SCALE - PENALTY * SCALE
    for s in range(groups_of(log_ref)):
        label = to_column(src_ref[s : s + 1, :].astype(F32))
        src_hot = jnp.where(label == lane_ids, 1.0, 0.0).astype(jnp.bfloat16)
        allowed_ref[...] = jnp.dot(src_hot, allowed_of, preferred_element_type=F32)
        blocks[s].wait()
        tops, logs = [], []
        for q in range(LANES // STRIP):
            rows = slice(s * LANES + q * STRIP, s * LANES + (q + 1) * STRIP)
            shifted = cost_ref[rows, :].astype(F32) - PENALTY * allowed_ref[
                q * STRIP : (q + 1) * STRIP, :
            ]
            scores = dual - shifted * SCALE
            highest, powers, log = strip_logs(scores)
            score_ref[rows, :] = scores
            base_ref[rows, :] = powers
            tops.append(highest)
            logs.append(log)
        top_ref[s : s + 1, :] = to_row(jnp.concatenate(tops, axis=0))
        log_ref[s : s + 1, :] = to_row(jnp.concatenate(logs, axis=0))
    spread(copies_ref, log_ref[...])


def rebase_kernel(
    log_target, parts_ref, start_top_ref, start_base_ref, score_ref,
    base_ref, top_ref, dual_ref, copies_ref, log_ref,
):
    dual_ref[...] = log_target - log_combined(parts_ref[...])
    top_ref[...] = start_top_ref[...]
    powers = jnp.exp2(dual_ref[...])
    for s in range(groups_of(log_ref)):
        rows = slice(s * LANES, (s + 1) * LANES)
        held = None
        for c in range(groups_of(dual_ref)):
            lanes = slice(c * LANES, (c + 1) * LANES)
            term = start_base_ref[rows, lanes] * powers[c : c + 1, :]
            base_ref[rows, lanes] = term
            held = term if held is None else held + term
        log_ref[s : s + 1, :] = to_row(jnp.sum(held, axis=1, keepdims=True))
    lowest = jnp.min(jnp.log2(jnp.maximum(log_ref[...], 1e-37)))
    near = jnp.logical_and(
        jnp.max(jnp.abs(dual_ref[...])) <= FIRST_REACH,
        lowest >= jnp.maximum(jnp.max(dual_ref[...]), 0.0) - 92.0,
    )

    @pl.when(near)
    def _():
        log_ref[...] = top_ref[...] + jnp.log2(log_ref[...])

    @pl.when(jnp.logical_not(near))
    def _():
        dual = wide(dual_ref)
        for s in range(groups_of(log_ref)):
            tops, logs = [], []
            for q in range(LANES // STRIP):
                rows = slice(s * LANES + q * STRIP, s * LANES + (q + 1) * STRIP)
                highest, powers, log = strip_logs(score_ref[rows, :] + dual)
                base_ref[rows, :] = powers
                tops.append(highest)
                logs.append(log)
            top_ref[s : s + 1, :] = to_row(jnp.concatenate(tops, axis=0))
            log_ref[s : s + 1, :] = to_row(jnp.concatenate(logs, axis=0))

    spread(copies_ref, log_ref[...])


def row_log_kernel(
    log_target, parts_ref, top_ref, base_dual_ref, base_ref, score_ref, dual_ref, copies_ref,
    weight_ref, sum_ref, tile_ref,
):
    dual_ref[...] = log_target - log_combined(parts_ref[...])
    lead = dual_ref[...] - base_dual_ref[...]
    weight_ref[...] = jnp.exp2(jnp.minimum(lead, 100.0))
    row_sums(base_ref, weight_ref, sum_ref)
    lowest = jnp.min(jnp.log2(jnp.maximum(sum_ref[...], 1e-37)))
    most = jnp.maximum(jnp.max(base_dual_ref[...]), 0.0) + jnp.maximum(jnp.max(lead), 0.0)
    near = jnp.logical_and(jnp.max(jnp.abs(lead)) <= REACH, lowest >= most - 92.0)

    @pl.when(near)
    def _():
        sum_ref[...] = top_ref[...] + jnp.log2(sum_ref[...])

    @pl.when(jnp.logical_not(near))
    def _():
        slow_row_logs(score_ref, tile_ref, dual_ref, sum_ref)

    spread(copies_ref, sum_ref[...])


def col_log_kernel(
    log_source, parts_ref, top_ref, base_dual_ref, base_ref, score_ref, dual_ref, copies_ref,
    weight_ref, sum_ref, tile_ref,
):
    dual_ref[...] = log_source - log_combined(parts_ref[...])
    lead = dual_ref[...] + top_ref[...]
    weight_ref[...] = jnp.exp2(jnp.minimum(lead, 100.0))
    col_sums(base_ref, weight_ref, sum_ref)
    most = jnp.max(lead)
    near = jnp.logical_and(
        most <= 60.0,
        jnp.min(
            jnp.log2(jnp.maximum(sum_ref[...], 1e-37)) - jnp.maximum(base_dual_ref[...], 0.0)
        )
        >= jnp.maximum(most, -15.0) - 85.0,
    )

    @pl.when(near)
    def _():
        sum_ref[...] = jnp.log2(sum_ref[...]) - base_dual_ref[...]

    @pl.when(jnp.logical_not(near))
    def _():
        slow_col_logs(score_ref, tile_ref, dual_ref, sum_ref)

    spread(copies_ref, sum_ref[...])


def row_plan_kernel(
    log_target, first, parts_ref, grad_ref, dual_in_ref, row_dual_ref, top_ref, base_dual_ref,
    base_ref, score_ref, out_ref, copies_ref, weight_ref, col_ref, sum_ref, tile_ref,
):
    if first:
        dual = log_target - log_combined(parts_ref[...])
        grad = grad_ref[...]
        out_ref[...] = dual
    else:
        dual = dual_in_ref[...]
        grad = -jnp.sum(parts_ref[...], axis=0)
        out_ref[...] = grad
    lead = dual - base_dual_ref[...]
    row_lead = row_dual_ref[...] + top_ref[...]
    most = jnp.max(row_lead) + jnp.maximum(jnp.max(base_dual_ref[...]), 0.0)
    near = jnp.logical_and(
        jnp.max(jnp.abs(lead)) <= REACH, most + jnp.maximum(jnp.max(lead), 0.0) <= 70.0
    )

    weight_ref[...] = jnp.exp2(lead - log_target) * grad
    row_sums(base_ref, weight_ref, sum_ref)
    sum_ref[...] = sum_ref[...] * jnp.exp2(row_lead)

    @pl.when(jnp.logical_not(near))
    def _():
        col_ref[...] = dual - log_target
        weight_ref[...] = grad
        slow_row_weighted(score_ref, tile_ref, row_dual_ref, col_ref, weight_ref, sum_ref)

    spread(copies_ref, sum_ref[...])


def col_plan_kernel(
    log_source, parts_ref, outer_ref, dual_ref, row_dual_ref, top_ref, base_dual_ref, base_ref,
    score_ref, out_ref, copies_ref, weight_ref, col_ref, sum_ref, tile_ref,
):
    grad = outer_ref[...] - jnp.sum(parts_ref[...], axis=0)
    out_ref[...] = grad
    lead = dual_ref[...] - base_dual_ref[...]
    row_lead = row_dual_ref[...] + top_ref[...]
    most = jnp.max(row_lead) + jnp.maximum(jnp.max(base_dual_ref[...]), 0.0)
    near = jnp.logical_and(
        jnp.max(jnp.abs(lead)) <= REACH, most + jnp.maximum(jnp.max(lead), 0.0) <= 70.0
    )

    weight_ref[...] = jnp.exp2(row_lead) * grad
    col_sums(base_ref, weight_ref, sum_ref)
    sum_ref[...] = sum_ref[...] * jnp.exp2(lead - log_source)

    @pl.when(jnp.logical_not(near))
    def _():
        col_ref[...] = dual_ref[...] - log_source
        weight_ref[...] = grad
        slow_col_weighted(score_ref, tile_ref, row_dual_ref, col_ref, weight_ref, sum_ref)

    spread(copies_ref, sum_ref[...])


def place_of(counts):
    row_at, col_at = lax.axis_index("rows"), lax.axis_index("cols")
    return row_at // counts[1], col_at // 2, row_at % counts[1], col_at % 2


def direction(place_ref):
    return 1 - 2 * place_ref[3]


def ring_place(place_ref, axis, offset, count):
    return lax.rem(place_ref[axis] + direction(place_ref) * offset + count, count)


def z_block(place_ref, src_ref, grad_ref, offset, counts):
    x_count, z_count = counts
    width, half = src_ref.shape[0], grad_ref.shape[1] // 2
    owned = width // (x_count * z_count)
    at = ring_place(place_ref, 2, offset, z_count)
    rows = [
        src_ref[pl.ds(pl.multiple_of((x * z_count + at) * owned, owned), owned), :]
        for x in range(x_count)
    ]
    return jnp.dot(
        jnp.concatenate(rows, axis=0), grad_ref[:, half:], preferred_element_type=F32
    )


def x_block(place_ref, src_ref, grad_ref, offset, counts):
    x_count = counts[0]
    width, half = src_ref.shape[0], grad_ref.shape[1] // 2
    owned = width // x_count
    at = ring_place(place_ref, 0, offset, x_count)
    rows = src_ref[pl.ds(pl.multiple_of(at * owned, owned), owned), :]
    return jnp.dot(rows, grad_ref[:, :half], preferred_element_type=F32)


def pieces(value):
    first = value.astype(jnp.bfloat16).astype(F32)
    second = (value - first).astype(jnp.bfloat16).astype(F32)
    return first, second, value - first - second


def grad_kernel(
    log_source, log_target, counts, parts_ref, row1, row2, row3, col1, col2, col3,
    fbar2, fbar3, gbar1, gbar2, gbar3, top_ref, base_ref, emb_ref, score_ref,
    out_ref, src_ref, start_ref, z_far_ref, x_far_ref, z_back_ref, x_back_ref, rows_ref, cols_ref, tile_ref,
):
    place_ref = place_of(counts)
    fbar1 = -jnp.sum(parts_ref[...], axis=0)
    leads = [ref[...] - col1[...] for ref in (col2, col3)]
    row_leads = [ref[...] + top_ref[...] for ref in (row1, row2, row3)]
    most = jnp.max(jnp.maximum(jnp.maximum(row_leads[0], row_leads[1]), row_leads[2]))
    most = most + jnp.maximum(jnp.max(col1[...]), 0.0)
    ahead = jnp.maximum(jnp.max(jnp.maximum(leads[0], leads[1])), 0.0)
    near = jnp.logical_and(
        jnp.maximum(jnp.max(jnp.abs(leads[0])), jnp.max(jnp.abs(leads[1]))) <= REACH,
        jnp.logical_and(jnp.max(jnp.abs(col1[...])) <= FIRST_REACH, most + ahead <= 70.0),
    )
    count, groups = groups_of(col1), groups_of(row1)

    @pl.when(near)
    def _():
        powers = [-jnp.exp2(lead) for lead in row_leads]
        factors = [*powers, powers[1] * fbar2[...], powers[2] * fbar3[...], powers[0] * fbar1]
        for k in range(8):
            rows_ref[:, k, :] = factors[k] if k < 6 else jnp.zeros_like(fbar1)
        column_factors = [
            jnp.exp2(jnp.full_like(leads[0], -log_target)) * gbar1[...],
            jnp.exp2(leads[0] - log_target) * gbar2[...],
            jnp.exp2(leads[1] - log_target) * gbar3[...],
            jnp.exp2(jnp.full_like(leads[0], -log_source)),
            jnp.exp2(leads[0] - log_source),
            jnp.exp2(-col1[...] - log_source),
        ]
        cols_ref[...] = jnp.zeros_like(cols_ref)
        for k, factor in enumerate(column_factors):
            for c in range(count):
                cols_ref[k : k + 1, c * LANES : (c + 1) * LANES] = factor[c : c + 1, :]
        b1, b2, b3 = pieces(cols_ref[...])
        right = jnp.concatenate([b1, b2, b1, b2, b3, b1], axis=0).astype(jnp.bfloat16)
        held = [None] * count
        for s in range(groups):
            a1, a2, a3 = pieces(rows_ref[s])
            left = jnp.concatenate([a1, a1, a2, a2, a1, a3], axis=0).astype(jnp.bfloat16)
            tile_ref[...] = lax.dot_general(
                left, right, (((0,), (0,)), ((), ())), preferred_element_type=F32
            )
            column = jnp.broadcast_to(to_column(rows_ref[s, 5:6, :]), (LANES, LANES))
            rows = slice(s * LANES, (s + 1) * LANES)
            src_ref[:, rows] = emb_ref[rows, :].T
            for c in range(count):
                lanes = slice(c * LANES, (c + 1) * LANES)
                base = base_ref[rows, lanes]
                out_ref[rows, lanes] = (base * tile_ref[:, lanes]).astype(jnp.bfloat16)
                term = jnp.sum((base * column).reshape(LANES // 8, 8, LANES), axis=0)
                held[c] = term if held[c] is None else held[c] + term
        for c, term in enumerate(held):
            start_ref[c : c + 1, :] = (
                jnp.sum(term, axis=0, keepdims=True) * column_factors[5][c : c + 1, :]
            )

    @pl.when(jnp.logical_not(near))
    def _():
        zero = jnp.zeros_like(fbar1)
        for k, value in enumerate(
            (row1[...], row2[...], row3[...], fbar1, fbar2[...], fbar3[...], zero, zero)
        ):
            rows_ref[:, k, :] = value
        start_ref[...] = jnp.zeros_like(start_ref)
        for s in range(groups):
            src_ref[:, s * LANES : (s + 1) * LANES] = emb_ref[s * LANES : (s + 1) * LANES, :].T
        columns_of = (None, col1, col2, col3)
        grads_of = (None, gbar1, gbar2, gbar3)

        @pl.loop(0, groups)
        def _(group):
            load_rows(score_ref, tile_ref, group)
            taken = rows_ref[group]
            columns = [to_column(taken[k : k + 1, :]) for k in range(6)]
            rows = pl.ds(pl.multiple_of(group * LANES, LANES), LANES)
            for c in range(count):
                lanes = slice(c * LANES, (c + 1) * LANES)
                value = jnp.zeros((LANES, LANES), F32)
                for k in reversed(range(3)):
                    scores = tile_ref[:, lanes] + columns[k]
                    plan_q = jnp.exp2(scores + (columns_of[k + 1][c : c + 1, :] - log_target))
                    value = value + plan_q * grads_of[k + 1][c : c + 1, :]
                    before = columns_of[k][c : c + 1, :] if k else jnp.zeros((1, LANES), F32)
                    term = jnp.exp2(scores + (before - log_source)) * columns[3 + k]
                    value = value + term
                    if not k:
                        start_ref[c : c + 1, :] -= jnp.sum(term, axis=0, keepdims=True)
                out_ref[rows, lanes] = (-value).astype(jnp.bfloat16)

    reach = counts[1] // 2
    put(z_far_ref, z_block(place_ref, src_ref, out_ref, reach, counts), start_ref[...])
    put(z_back_ref, z_block(place_ref, src_ref, out_ref, 1 - reach, counts), start_ref[...])
    x_far_ref[...] = x_block(place_ref, src_ref, out_ref, counts[0] // 2, counts)
    x_back_ref[...] = x_block(place_ref, src_ref, out_ref, -1, counts)


def put(out_ref, block, rider):
    rows = block.shape[0]
    out_ref[:rows, :] = block
    out_ref[rows:, :] = jnp.zeros_like(out_ref[rows:, :])
    out_ref[rows:, :LANES] = rider


def rider(ref):
    return ref[ref.shape[0] - 8 :, :LANES]


def x_part(y_count, place_ref, grad_ref, tgt_ref, sent_ref, kept_ref, order_ref):
    block = tgt_ref.shape[1] // (2 * y_count)
    core, turn = place_ref[3], direction(place_ref)
    for side, out_ref in ((0, sent_ref), (1, kept_ref)):
        for k, offset in enumerate((2, 1, -1, 0)):
            step = offset * (2 * side - 1)
            at = lax.rem(place_ref[1] + turn * step + y_count, y_count)
            owner = at * 2 + (core if side else 1 - core)
            order_ref[:, k * block : (k + 1) * block] = tgt_ref[
                :, pl.ds(pl.multiple_of(owner * block, block), block)
            ]
        out_ref[...] = jnp.dot(grad_ref[...], order_ref[...], preferred_element_type=F32)


def parts_kernel(
    counts, y_count, grad_ref, src_ref, tgt_ref, sent_ref, kept_ref, *outs
):
    place_ref = place_of(counts)
    *outs, order_ref = outs
    x_part(y_count, place_ref, grad_ref, tgt_ref, sent_ref, kept_ref, order_ref)
    reach = counts[1] // 2
    offsets = [*range(reach - 1, 0, -1), *range(2 - reach, 1)]
    for out_ref, offset in zip(outs, offsets):
        out_ref[...] = z_block(place_ref, src_ref, grad_ref, offset, counts)
    for out_ref, offset in zip(outs[len(offsets) :], (1, 0)):
        out_ref[...] = x_block(place_ref, src_ref, grad_ref, offset, counts)


def forward(out_ref, block_ref, arrived_ref):
    rows = block_ref.shape[0]
    out_ref[:rows, :] = block_ref[...] + arrived_ref[:rows, :]
    out_ref[rows:, :] = arrived_ref[rows:, :]


def token(ref):
    ref[...] = jnp.zeros_like(ref)


def z_kernel(up_ref, down_ref, ahead_ref, behind_ref, start_ref, after_ref, z_ref, back_ref, held_ref):
    forward(z_ref, ahead_ref, up_ref)
    forward(back_ref, behind_ref, down_ref)
    held_ref[...] = start_ref[...] + rider(up_ref) + rider(down_ref)


def x_kernel(up_ref, down_ref, one_ref, own_ref, after_ref, pay_ref, sum_ref, token_ref):
    pay_ref[...] = one_ref[...] + up_ref[...]
    sum_ref[...] = own_ref[...] + down_ref[...]
    token(token_ref)


def y_kernel(
    up_ref, down_ref, one_ref, own_ref, x_up_ref, x_sum_ref, after_ref, pay_ref, sum_ref, x_ref,
    token_ref,
):
    x_kernel(up_ref, down_ref, one_ref, own_ref, after_ref, pay_ref, sum_ref, token_ref)
    x_ref[...] = x_sum_ref[...] + x_up_ref[...]


def chip_kernel(arrived_ref, kept_ref, after_ref, *outs):
    block = outs[0].shape[1]
    for k, out_ref in enumerate(outs[:-1]):
        lanes = slice(k * block, (k + 1) * block)
        out_ref[...] = kept_ref[:, lanes] + arrived_ref[:, lanes]
    token(outs[-1])


def last_z_kernel(
    up_ref, down_ref, ahead_ref, own_ref, start_ref, after_ref, z_ref, z_sum_ref, held_ref
):
    forward(z_ref, ahead_ref, up_ref)
    z_sum_ref[...] = own_ref[...] + down_ref[: own_ref.shape[0], :]
    held_ref[...] = start_ref[...] + rider(up_ref) + rider(down_ref)


def split_kernel(
    counts, z_up_ref, z_sum_ref, start_ref, after_ref,
    far_ref, back_ref, one_ref, last_ref, held_ref,
):
    x_count, place_ref = counts[0], place_of(counts)
    held_ref[...] = start_ref[...] + rider(z_up_ref)
    block = z_sum_ref.shape[0] // x_count
    for out_ref, offset in ((far_ref, 2), (back_ref, -1), (one_ref, 1), (last_ref, 0)):
        at = ring_place(place_ref, 0, offset, x_count)
        rows = pl.ds(pl.multiple_of(at * block, block), block)
        value = z_sum_ref[rows, :] + z_up_ref[rows, :]
        if offset:
            put(out_ref, value, held_ref[...])
        else:
            out_ref[...] = value


def turn_kernel(sum_ref, up_ref, after_ref, out_ref, token_ref):
    for s in range(sum_ref.shape[0] // LANES):
        rows = slice(s * LANES, (s + 1) * LANES)
        out_ref[:, rows] = (sum_ref[rows, :] + up_ref[rows, :]).T
    token(token_ref)


def last_kernel(parts_ref, far_ref, one_ref, back_ref, own_ref, start_ref, out_ref, held_ref):
    rows, half = own_ref.shape
    out_ref[:, :half] = jnp.sum(parts_ref[...], axis=0)
    value, held = own_ref[...], start_ref[...]
    for ref in (far_ref, one_ref, back_ref):
        value = value + ref[:rows, :]
        held = held + rider(ref)
    out_ref[:, half:] = value
    held_ref[...] = held


def call(
    kernel, arguments, outs, scratch=(), in_hbm=(), loose=(), free=(), last=False, flops=1024, name=None
):
    spaces, values = [], []
    for at, value in enumerate(arguments):
        space = pltpu.VMEM
        if at in in_hbm:
            space = pltpu.HBM
        elif at in loose:
            space = pl.ANY
        if at in in_hbm or (space is pltpu.VMEM and value.size >= PINNED and at not in free):
            value = pltpu.with_memory_space_constraint(value, space)
        spaces.append(space)
        values.append(value)
    return pl.pallas_call(
        kernel,
        out_shape=[
            pltpu.VMEM(out.shape, out.dtype) if math.prod(out.shape) >= PINNED and not last else out
            for out in outs
        ],
        in_specs=[pl.BlockSpec(memory_space=space) for space in spaces],
        out_specs=[pl.BlockSpec(memory_space=pltpu.VMEM)] * len(outs),
        scratch_shapes=list(scratch),
        compiler_params=pltpu.CompilerParams(vmem_limit_bytes=VMEM_BYTES),
        cost_estimate=pl.CostEstimate(flops=flops, bytes_accessed=1024, transcendentals=0),
        name=name,
    )(*values)


def exchanged(copies, axis):
    return lax.all_to_all(copies, axis, 0, 0, tiled=True)


def body(cost, src_label, tgt_label, class_mask, g_start, f_bar, g_bar, src_emb, tgt_emb):
    row_count = lax.axis_size("rows")
    col_count = lax.axis_size("cols")
    src_rows, tgt_cols = cost.shape
    width = src_emb.shape[1]
    log_source = -math.log2(src_rows * row_count)
    log_target = -math.log2(tgt_cols * col_count)
    row_shape = (src_rows // LANES, LANES)
    col_shape = (tgt_cols // LANES, LANES)
    src_label, f_bar = src_label.reshape(row_shape), f_bar.reshape(row_shape)
    tgt_label, g_bar = tgt_label.reshape(col_shape), g_bar.reshape(col_shape)
    g_start = g_start.reshape(col_shape)

    def array(shape, dtype=F32):
        return jax.ShapeDtypeStruct(shape, dtype)

    matrix = array(cost.shape)
    row_vector, col_vector = array(row_shape), array(col_shape)
    row_copies = array((col_count,) + row_shape)
    col_copies = array((row_count,) + col_shape)
    row_held, col_held = pltpu.VMEM(row_shape, F32), pltpu.VMEM(col_shape, F32)
    slow = [pltpu.VMEM((LANES, tgt_cols), F32)]

    x_count, z_count, y_count = 4, row_count // 4, col_count // 2
    counts = (x_count, z_count)
    owned = width // row_count
    score, start_base, start_top, copies = call(
        first_kernel,
        (cost, src_label, tgt_label, class_mask, g_start),
        [matrix, matrix, row_vector, row_copies],
        [
            pltpu.VMEM(cost.shape, cost.dtype),
            pltpu.VMEM(row_shape, jnp.int32),
            pltpu.VMEM(col_shape, jnp.int32),
            pltpu.VMEM(class_mask.shape, jnp.int32),
            col_held,
            pltpu.VMEM((LANES, tgt_cols), F32),
            row_held,
            pltpu.SemaphoreType.DMA((4,)),
            pltpu.SemaphoreType.DMA(row_shape[:1]),
        ],
        in_hbm=range(5),
        name="first_row_logs",
    )

    def col_logs(parts, top, base_dual, base):
        return call(
            functools.partial(col_log_kernel, log_source),
            (parts, top, base_dual, base, score),
            [row_vector, col_copies],
            [row_held, col_held] + slow,
                name="col_logs",
        )

    zero = jnp.zeros(col_shape, F32)
    row1, copies = col_logs(exchanged(copies, "cols"), start_top, zero, start_base)
    base, top, col1, copies = call(
        functools.partial(rebase_kernel, log_target),
        (exchanged(copies, "rows"), start_top, start_base, score),
        [matrix, row_vector, col_vector, row_copies],
        [row_held],
        name="second_row_logs",
    )
    row2, copies = col_logs(exchanged(copies, "cols"), top, col1, base)
    col2, copies = call(
        functools.partial(row_log_kernel, log_target),
        (exchanged(copies, "rows"), top, col1, base, score),
        [col_vector, row_copies],
        [col_held, row_held] + slow,
        name="third_row_logs",
    )
    row3, copies = col_logs(exchanged(copies, "cols"), top, col1, base)

    def row_plan(first, parts, grad, dual, row):
        return call(
            functools.partial(row_plan_kernel, log_target, first),
            (parts, grad, dual, row, top, col1, base, score),
            [col_vector, row_copies],
            [col_held, col_held, row_held] + slow,
                name="row_plan",
        )

    def col_plan(parts, outer, dual, row):
        return call(
            functools.partial(col_plan_kernel, log_source),
            (parts, outer, dual, row, top, col1, base, score),
            [row_vector, col_copies],
            [row_held, col_held, col_held] + slow,
                name="col_plan",
        )

    none = jnp.zeros(row_shape, F32)
    col3, copies = row_plan(True, exchanged(copies, "rows"), g_bar, col2, row3)
    fbar3, copies = col_plan(exchanged(copies, "cols"), f_bar, col2, row3)
    gbar2, copies = row_plan(False, exchanged(copies, "rows"), g_bar, col2, row2)
    fbar2, copies = col_plan(exchanged(copies, "cols"), none, col1, row2)
    gbar1, copies = row_plan(False, exchanged(copies, "rows"), g_bar, col1, row1)
    parts = exchanged(copies, "cols")
    devices = [
        (x, y, z, core)
        for x in range(x_count)
        for y in range(y_count)
        for z in range(z_count)
        for core in range(2)
    ]

    def number(x, y, z, core):
        spot = (x % x_count * z_count + z % z_count) * y_count + y % y_count
        return spot * 2 + core

    def turn(value, axis, step):
        moves = []
        for device in devices:
            ahead = list(device)
            ahead[axis] += step * (1 - 2 * device[3])
            moves.append((number(*device), number(*ahead)))
        return lax.ppermute(value, ("rows", "cols"), moves)

    half = tgt_cols // 2
    z_rows, x_rows = x_count * owned, z_count * owned
    z_shape, z_riding = array((z_rows, half)), array((z_rows + 8, half))
    x_shape = array((x_rows, half))
    rounded, src_turned, start, z_far, x_far, z_back, x_back = call(
        functools.partial(grad_kernel, log_source, log_target, counts),
        (
            parts, row1, row2, row3, col1, col2, col3, fbar2, fbar3, gbar1, gbar2, g_bar,
            top, base, src_emb, score,
        ),
        [
            array(cost.shape, jnp.bfloat16),
            array(src_emb.shape[::-1], src_emb.dtype),
            col_vector,
            z_riding,
            x_shape,
            z_riding,
            x_shape,
        ],
        [pltpu.VMEM((row_shape[0], 8, LANES), F32), pltpu.VMEM((8, tgt_cols), F32)] + slow,
        free=(14,),
        name="cost_grad",
    )
    z_up, z_down = turn(z_far, 2, 1), turn(z_back, 2, -1)
    x_up, x_down = turn(x_far, 0, 1), turn(x_back, 0, -1)
    chip_part = array((src_rows, width // 2))
    outs = call(
        functools.partial(parts_kernel, counts, y_count),
        (rounded, src_turned, tgt_emb),
        [chip_part] * 2 + [z_shape] * (z_count - 2) + [x_shape] * 2,
        [pltpu.VMEM((tgt_cols, width // 2), jnp.bfloat16)],
        free=(2,),
        flops=BIG,
        name="grad_parts",
    )
    sent, kept, z_3, z_2, z_1, z_back2, z_back1, z_own, x_one, x_own = outs
    small = array((8, LANES))

    def step(kernel, arguments, outs, name, last=False, flops=STEP):
        return call(
            kernel,
            arguments,
            outs,
            loose=(len(arguments) - 1,),
            last=last,
            flops=flops,
            name=name,
        )

    z_pay, z_back, start = step(
        z_kernel,
        (z_up, z_down, z_3, z_back2, start, kept),
        [z_riding, z_riding, small],
        "z_second",
    )
    z_up, z_down = turn(z_pay, 2, 1), turn(z_back, 2, -1)
    arrived = lax.ppermute(sent, "cols", [(at, at ^ 1) for at in range(col_count)])
    x_pay, x_sum, mark = step(
        x_kernel, (x_up, x_down, x_one, x_own, start), [x_shape, x_shape, small], "x_second",
        flops=2**34
    )
    x_up = turn(x_pay, 0, 1)
    y_shape = array((src_rows, width // col_count))
    far, one, back, own, mark = step(
        chip_kernel, (arrived, kept, mark), [y_shape] * 4 + [small], "chip_sums"
    )
    y_up, y_down = turn(far, 1, 1), turn(back, 1, -1)
    z_pay, z_back, start = step(
        z_kernel,
        (z_up, z_down, z_2, z_back1, start, mark),
        [z_riding, z_riding, small],
        "z_third",
        flops=2**31,
    )
    z_up, z_down = turn(z_pay, 2, 1), turn(z_back, 2, -1)
    z_pay, z_sum, start = step(
        last_z_kernel,
        (z_up, z_down, z_1, z_own, start, start),
        [z_riding, z_shape, small],
        "z_fourth",
        flops=2**31,
    )
    z_up = turn(z_pay, 2, 1)
    y_pay, y_sum, first, mark = step(
        y_kernel,
        (y_up, y_down, one, own, x_up, x_sum, start),
        [y_shape, y_shape, x_shape, small],
        "y_second",
    )
    along_z = [[x * z_count + z for z in range(z_count)] for x in range(x_count)]
    first = lax.all_to_all(
        first.reshape(z_count, owned, half), "rows", 0, 0, tiled=True, axis_index_groups=along_z
    )
    y_up = turn(y_pay, 1, 1)
    last, riding = array((owned, half)), array((owned + 8, half))
    x_far, x_back, x_one, x_own, start = step(
        functools.partial(split_kernel, counts),
        (z_up, z_sum, start, mark),
        [riding, riding, riding, last, small],
        "x_blocks",
    )
    x_far, x_one, x_back = turn(x_far, 0, 2), turn(x_one, 0, 1), turn(x_back, 0, -1)
    grad_x, mark = step(
        turn_kernel,
        (y_sum, y_up, start),
        [array((width // col_count, src_rows)), small],
        "grad_x",
        last=True,
    )
    grad_y, start = call(
        last_kernel,
        (first, x_far, x_one, x_back, x_own, start),
        [array((owned, tgt_cols)), col_vector],
        name="last_step",
    )
    g_start_bar = start.reshape(tgt_cols)
    return (g_start_bar, grad_x, grad_y)


def solution(mesh):
    placed = (
        P("rows", "cols"),
        P("rows"),
        P("cols"),
        P(),
        P("cols"),
        P("rows"),
        P("cols"),
        P("rows", None),
        P("cols", None),
    )
    return jax.shard_map(
        body,
        mesh=mesh,
        in_specs=placed,
        out_specs=(P("cols"), P("cols", "rows"), P("rows", "cols")),
        check_vma=False,
    )
```

```python
import functools
import math

import jax
import jax.numpy as jnp
from jax import lax
from jax.experimental import pallas as pl
from jax.experimental.pallas import tpu as pltpu
from jax.sharding import PartitionSpec as P

K = 3


EPSILON = 0.05
PENALTY = 1.0
SCALE = 1.0 / (EPSILON * math.log(2.0))
LANES = 128
STRIP = 32
REACH = 40.0
FIRST_REACH = 75.0
VMEM_BYTES = 16 * 2**20
PINNED = 2**16
BIG = 2**32
STEP = 2**33
F32 = jnp.float32


def eye():
    return lax.broadcasted_iota(jnp.int32, (LANES, LANES), 0) == lax.broadcasted_iota(
        jnp.int32, (LANES, LANES), 1
    )


def to_column(row):
    return jnp.sum(jnp.where(eye(), row, 0.0), axis=1, keepdims=True)


def to_row(column):
    return jnp.sum(jnp.where(eye(), column, 0.0), axis=0, keepdims=True)


def log_combined(parts):
    top = jnp.max(parts, axis=0)
    return top + jnp.log2(jnp.sum(jnp.exp2(parts - top[None]), axis=0))


def spread(copies_ref, value):
    copies_ref[...] = jnp.broadcast_to(value[None], copies_ref.shape)


def groups_of(ref):
    return ref.shape[0]


def row_sums(base_ref, weight_ref, out_ref):
    for s in range(groups_of(out_ref)):
        held = None
        for c in range(groups_of(weight_ref)):
            tile = base_ref[s * LANES : (s + 1) * LANES, c * LANES : (c + 1) * LANES]
            term = tile * weight_ref[c : c + 1, :]
            held = term if held is None else held + term
        out_ref[s : s + 1, :] = to_row(jnp.sum(held, axis=1, keepdims=True))


def col_sums(base_ref, weight_ref, out_ref):
    held = [None] * groups_of(out_ref)
    for s in range(groups_of(weight_ref)):
        column = jnp.broadcast_to(to_column(weight_ref[s : s + 1, :]), (LANES, LANES))
        for c in range(len(held)):
            tile = base_ref[s * LANES : (s + 1) * LANES, c * LANES : (c + 1) * LANES]
            term = jnp.sum((tile * column).reshape(LANES // 8, 8, LANES), axis=0)
            held[c] = term if held[c] is None else held[c] + term
    for c, term in enumerate(held):
        out_ref[c : c + 1, :] = jnp.sum(term, axis=0, keepdims=True)


def strip_logs(scores):
    highest = jnp.max(scores, axis=1, keepdims=True)
    powers = jnp.exp2(scores - highest)
    return highest, powers, highest + jnp.log2(jnp.sum(powers, axis=1, keepdims=True))


def wide(ref):
    return jnp.concatenate([ref[c : c + 1, :] for c in range(groups_of(ref))], axis=1)


def load_rows(score_ref, tile_ref, group):
    tile_ref[...] = score_ref[pl.ds(pl.multiple_of(group * LANES, LANES), LANES), :]


def slow_row_logs(score_ref, tile_ref, col_ref, out_ref):
    @pl.loop(0, groups_of(out_ref))
    def _(group):
        load_rows(score_ref, tile_ref, group)
        logs = []
        for q in range(LANES // STRIP):
            logs.append(strip_logs(tile_ref[q * STRIP : (q + 1) * STRIP, :] + wide(col_ref))[2])
        out_ref[pl.ds(group, 1), :] = to_row(jnp.concatenate(logs, axis=0))


def slow_col_logs(score_ref, tile_ref, row_ref, out_ref):
    count = groups_of(out_ref)
    tops = tuple(jnp.full((1, LANES), -1e30, F32) for _ in range(count))

    def highest(group, tops):
        load_rows(score_ref, tile_ref, group)
        column = to_column(row_ref[pl.ds(group, 1), :])
        return tuple(
            jnp.maximum(
                tops[c],
                jnp.max(
                    tile_ref[:, c * LANES : (c + 1) * LANES] + column, axis=0, keepdims=True
                ),
            )
            for c in range(count)
        )

    tops = lax.fori_loop(0, groups_of(row_ref), highest, tops)
    sums = tuple(jnp.zeros((1, LANES), F32) for _ in range(count))

    def summed(group, sums):
        load_rows(score_ref, tile_ref, group)
        column = to_column(row_ref[pl.ds(group, 1), :])
        return tuple(
            sums[c]
            + jnp.sum(
                jnp.exp2(tile_ref[:, c * LANES : (c + 1) * LANES] + column - tops[c]),
                axis=0,
                keepdims=True,
            )
            for c in range(count)
        )

    sums = lax.fori_loop(0, groups_of(row_ref), summed, sums)
    for c in range(count):
        out_ref[c : c + 1, :] = tops[c] + jnp.log2(sums[c])


def slow_row_weighted(score_ref, tile_ref, row_ref, col_ref, weight_ref, out_ref):
    @pl.loop(0, groups_of(out_ref))
    def _(group):
        load_rows(score_ref, tile_ref, group)
        column = to_column(row_ref[pl.ds(group, 1), :])
        sums = []
        for q in range(LANES // STRIP):
            part = slice(q * STRIP, (q + 1) * STRIP)
            plan = jnp.exp2(tile_ref[part, :] + column[part] + wide(col_ref))
            sums.append(jnp.sum(plan * wide(weight_ref), axis=1, keepdims=True))
        out_ref[pl.ds(group, 1), :] = to_row(jnp.concatenate(sums, axis=0))


def slow_col_weighted(score_ref, tile_ref, row_ref, col_ref, weight_ref, out_ref):
    count = groups_of(out_ref)
    sums = tuple(jnp.zeros((1, LANES), F32) for _ in range(count))

    def summed(group, sums):
        load_rows(score_ref, tile_ref, group)
        column = to_column(row_ref[pl.ds(group, 1), :])
        weight = to_column(weight_ref[pl.ds(group, 1), :])
        return tuple(
            sums[c]
            + jnp.sum(
                weight
                * jnp.exp2(
                    tile_ref[:, c * LANES : (c + 1) * LANES] + column + col_ref[c : c + 1, :]
                ),
                axis=0,
                keepdims=True,
            )
            for c in range(count)
        )

    sums = lax.fori_loop(0, groups_of(row_ref), summed, sums)
    for c in range(count):
        out_ref[c : c + 1, :] = sums[c]


def first_kernel(
    cost_hbm, src_hbm, tgt_hbm, mask_hbm, dual_hbm, score_ref, base_ref, top_ref,
    copies_ref, cost_ref, src_ref, tgt_ref, mask_ref, dual_ref, allowed_ref, log_ref, small_sem,
    cost_sem,
):
    small = [
        pltpu.make_async_copy(source, target, small_sem.at[at])
        for at, (source, target) in enumerate(
            ((tgt_hbm, tgt_ref), (mask_hbm, mask_ref), (src_hbm, src_ref), (dual_hbm, dual_ref))
        )
    ]
    for copy in small:
        copy.start()
    blocks = []
    for s in range(groups_of(log_ref)):
        rows = pl.ds(s * LANES, LANES)
        blocks.append(
            pltpu.make_async_copy(cost_hbm.at[rows, :], cost_ref.at[rows, :], cost_sem.at[s])
        )
        blocks[-1].start()
    for copy in small:
        copy.wait()
    classes = mask_ref.shape[0]
    mask = mask_ref[...].astype(F32).astype(jnp.bfloat16)
    ids = lax.broadcasted_iota(jnp.int32, (classes, LANES), 0)
    hot = jnp.concatenate(
        [
            jnp.where(tgt_ref[c : c + 1, :] == ids, 1.0, 0.0).astype(jnp.bfloat16)
            for c in range(groups_of(tgt_ref))
        ],
        axis=1,
    )
    allowed_of = jnp.dot(mask, hot, preferred_element_type=F32).astype(jnp.bfloat16)
    lane_ids = lax.broadcasted_iota(jnp.int32, (LANES, classes), 1).astype(F32)
    dual = wide(dual_ref) * SCALE - PENALTY * SCALE
    for s in range(groups_of(log_ref)):
        label = to_column(src_ref[s : s + 1, :].astype(F32))
        src_hot = jnp.where(label == lane_ids, 1.0, 0.0).astype(jnp.bfloat16)
        allowed_ref[...] = jnp.dot(src_hot, allowed_of, preferred_element_type=F32)
        blocks[s].wait()
        tops, logs = [], []
        for q in range(LANES // STRIP):
            rows = slice(s * LANES + q * STRIP, s * LANES + (q + 1) * STRIP)
            shifted = cost_ref[rows, :].astype(F32) - PENALTY * allowed_ref[
                q * STRIP : (q + 1) * STRIP, :
            ]
            scores = dual - shifted * SCALE
            highest, powers, log = strip_logs(scores)
            score_ref[rows, :] = scores
            base_ref[rows, :] = powers
            tops.append(highest)
            logs.append(log)
        top_ref[s : s + 1, :] = to_row(jnp.concatenate(tops, axis=0))
        log_ref[s : s + 1, :] = to_row(jnp.concatenate(logs, axis=0))
    spread(copies_ref, log_ref[...])


def rebase_kernel(
    log_target, parts_ref, start_top_ref, start_base_ref, score_ref,
    base_ref, top_ref, dual_ref, copies_ref, log_ref,
):
    dual_ref[...] = log_target - log_combined(parts_ref[...])
    top_ref[...] = start_top_ref[...]
    powers = jnp.exp2(dual_ref[...])
    for s in range(groups_of(log_ref)):
        rows = slice(s * LANES, (s + 1) * LANES)
        held = None
        for c in range(groups_of(dual_ref)):
            lanes = slice(c * LANES, (c + 1) * LANES)
            term = start_base_ref[rows, lanes] * powers[c : c + 1, :]
            base_ref[rows, lanes] = term
            held = term if held is None else held + term
        log_ref[s : s + 1, :] = to_row(jnp.sum(held, axis=1, keepdims=True))
    lowest = jnp.min(jnp.log2(jnp.maximum(log_ref[...], 1e-37)))
    near = jnp.logical_and(
        jnp.max(jnp.abs(dual_ref[...])) <= FIRST_REACH,
        lowest >= jnp.maximum(jnp.max(dual_ref[...]), 0.0) - 92.0,
    )

    @pl.when(near)
    def _():
        log_ref[...] = top_ref[...] + jnp.log2(log_ref[...])

    @pl.when(jnp.logical_not(near))
    def _():
        dual = wide(dual_ref)
        for s in range(groups_of(log_ref)):
            tops, logs = [], []
            for q in range(LANES // STRIP):
                rows = slice(s * LANES + q * STRIP, s * LANES + (q + 1) * STRIP)
                highest, powers, log = strip_logs(score_ref[rows, :] + dual)
                base_ref[rows, :] = powers
                tops.append(highest)
                logs.append(log)
            top_ref[s : s + 1, :] = to_row(jnp.concatenate(tops, axis=0))
            log_ref[s : s + 1, :] = to_row(jnp.concatenate(logs, axis=0))

    spread(copies_ref, log_ref[...])


def row_log_kernel(
    log_target, parts_ref, top_ref, base_dual_ref, base_ref, score_ref, dual_ref, copies_ref,
    weight_ref, sum_ref, tile_ref,
):
    dual_ref[...] = log_target - log_combined(parts_ref[...])
    lead = dual_ref[...] - base_dual_ref[...]
    weight_ref[...] = jnp.exp2(jnp.minimum(lead, 100.0))
    row_sums(base_ref, weight_ref, sum_ref)
    lowest = jnp.min(jnp.log2(jnp.maximum(sum_ref[...], 1e-37)))
    most = jnp.maximum(jnp.max(base_dual_ref[...]), 0.0) + jnp.maximum(jnp.max(lead), 0.0)
    near = jnp.logical_and(jnp.max(jnp.abs(lead)) <= REACH, lowest >= most - 92.0)

    @pl.when(near)
    def _():
        sum_ref[...] = top_ref[...] + jnp.log2(sum_ref[...])

    @pl.when(jnp.logical_not(near))
    def _():
        slow_row_logs(score_ref, tile_ref, dual_ref, sum_ref)

    spread(copies_ref, sum_ref[...])


def col_log_kernel(
    log_source, parts_ref, top_ref, base_dual_ref, base_ref, score_ref, dual_ref, copies_ref,
    weight_ref, sum_ref, tile_ref,
):
    dual_ref[...] = log_source - log_combined(parts_ref[...])
    lead = dual_ref[...] + top_ref[...]
    weight_ref[...] = jnp.exp2(jnp.minimum(lead, 100.0))
    col_sums(base_ref, weight_ref, sum_ref)
    most = jnp.max(lead)
    near = jnp.logical_and(
        most <= 60.0,
        jnp.min(
            jnp.log2(jnp.maximum(sum_ref[...], 1e-37)) - jnp.maximum(base_dual_ref[...], 0.0)
        )
        >= jnp.maximum(most, -15.0) - 85.0,
    )

    @pl.when(near)
    def _():
        sum_ref[...] = jnp.log2(sum_ref[...]) - base_dual_ref[...]

    @pl.when(jnp.logical_not(near))
    def _():
        slow_col_logs(score_ref, tile_ref, dual_ref, sum_ref)

    spread(copies_ref, sum_ref[...])


def row_plan_kernel(
    log_target, first, parts_ref, grad_ref, dual_in_ref, row_dual_ref, top_ref, base_dual_ref,
    base_ref, score_ref, out_ref, copies_ref, weight_ref, col_ref, sum_ref, tile_ref,
):
    if first:
        dual = log_target - log_combined(parts_ref[...])
        grad = grad_ref[...]
        out_ref[...] = dual
    else:
        dual = dual_in_ref[...]
        grad = -jnp.sum(parts_ref[...], axis=0)
        out_ref[...] = grad
    lead = dual - base_dual_ref[...]
    row_lead = row_dual_ref[...] + top_ref[...]
    most = jnp.max(row_lead) + jnp.maximum(jnp.max(base_dual_ref[...]), 0.0)
    near = jnp.logical_and(
        jnp.max(jnp.abs(lead)) <= REACH, most + jnp.maximum(jnp.max(lead), 0.0) <= 70.0
    )

    weight_ref[...] = jnp.exp2(lead - log_target) * grad
    row_sums(base_ref, weight_ref, sum_ref)
    sum_ref[...] = sum_ref[...] * jnp.exp2(row_lead)

    @pl.when(jnp.logical_not(near))
    def _():
        col_ref[...] = dual - log_target
        weight_ref[...] = grad
        slow_row_weighted(score_ref, tile_ref, row_dual_ref, col_ref, weight_ref, sum_ref)

    spread(copies_ref, sum_ref[...])


def col_plan_kernel(
    log_source, parts_ref, outer_ref, dual_ref, row_dual_ref, top_ref, base_dual_ref, base_ref,
    score_ref, out_ref, copies_ref, weight_ref, col_ref, sum_ref, tile_ref,
):
    grad = outer_ref[...] - jnp.sum(parts_ref[...], axis=0)
    out_ref[...] = grad
    lead = dual_ref[...] - base_dual_ref[...]
    row_lead = row_dual_ref[...] + top_ref[...]
    most = jnp.max(row_lead) + jnp.maximum(jnp.max(base_dual_ref[...]), 0.0)
    near = jnp.logical_and(
        jnp.max(jnp.abs(lead)) <= REACH, most + jnp.maximum(jnp.max(lead), 0.0) <= 70.0
    )

    weight_ref[...] = jnp.exp2(row_lead) * grad
    col_sums(base_ref, weight_ref, sum_ref)
    sum_ref[...] = sum_ref[...] * jnp.exp2(lead - log_source)

    @pl.when(jnp.logical_not(near))
    def _():
        col_ref[...] = dual_ref[...] - log_source
        weight_ref[...] = grad
        slow_col_weighted(score_ref, tile_ref, row_dual_ref, col_ref, weight_ref, sum_ref)

    spread(copies_ref, sum_ref[...])


def place_of(counts):
    row_at, col_at = lax.axis_index("rows"), lax.axis_index("cols")
    return row_at // counts[1], col_at // 2, row_at % counts[1], col_at % 2


def direction(place_ref):
    return 1 - 2 * place_ref[3]


def ring_place(place_ref, axis, offset, count):
    return lax.rem(place_ref[axis] + direction(place_ref) * offset + count, count)


def z_block(place_ref, src_ref, grad_ref, offset, counts):
    x_count, z_count = counts
    width, half = src_ref.shape[0], grad_ref.shape[1] // 2
    owned = width // (x_count * z_count)
    at = ring_place(place_ref, 2, offset, z_count)
    rows = [
        src_ref[pl.ds(pl.multiple_of((x * z_count + at) * owned, owned), owned), :]
        for x in range(x_count)
    ]
    return jnp.dot(
        jnp.concatenate(rows, axis=0), grad_ref[:, half:], preferred_element_type=F32
    )


def x_block(place_ref, src_ref, grad_ref, offset, counts):
    x_count = counts[0]
    width, half = src_ref.shape[0], grad_ref.shape[1] // 2
    owned = width // x_count
    at = ring_place(place_ref, 0, offset, x_count)
    rows = src_ref[pl.ds(pl.multiple_of(at * owned, owned), owned), :]
    return jnp.dot(rows, grad_ref[:, :half], preferred_element_type=F32)


def pieces(value):
    first = value.astype(jnp.bfloat16).astype(F32)
    second = (value - first).astype(jnp.bfloat16).astype(F32)
    return first, second, value - first - second


def grad_kernel(
    log_source, log_target, counts, parts_ref, row1, row2, row3, col1, col2, col3,
    fbar2, fbar3, gbar1, gbar2, gbar3, top_ref, base_ref, emb_ref, score_ref,
    out_ref, src_ref, start_ref, z_far_ref, x_far_ref, z_back_ref, x_back_ref, rows_ref, cols_ref, tile_ref,
):
    place_ref = place_of(counts)
    fbar1 = -jnp.sum(parts_ref[...], axis=0)
    leads = [ref[...] - col1[...] for ref in (col2, col3)]
    row_leads = [ref[...] + top_ref[...] for ref in (row1, row2, row3)]
    most = jnp.max(jnp.maximum(jnp.maximum(row_leads[0], row_leads[1]), row_leads[2]))
    most = most + jnp.maximum(jnp.max(col1[...]), 0.0)
    ahead = jnp.maximum(jnp.max(jnp.maximum(leads[0], leads[1])), 0.0)
    near = jnp.logical_and(
        jnp.maximum(jnp.max(jnp.abs(leads[0])), jnp.max(jnp.abs(leads[1]))) <= REACH,
        jnp.logical_and(jnp.max(jnp.abs(col1[...])) <= FIRST_REACH, most + ahead <= 70.0),
    )
    count, groups = groups_of(col1), groups_of(row1)

    @pl.when(near)
    def _():
        powers = [-jnp.exp2(lead) for lead in row_leads]
        factors = [*powers, powers[1] * fbar2[...], powers[2] * fbar3[...], powers[0] * fbar1]
        for k in range(8):
            rows_ref[:, k, :] = factors[k] if k < 6 else jnp.zeros_like(fbar1)
        column_factors = [
            jnp.exp2(jnp.full_like(leads[0], -log_target)) * gbar1[...],
            jnp.exp2(leads[0] - log_target) * gbar2[...],
            jnp.exp2(leads[1] - log_target) * gbar3[...],
            jnp.exp2(jnp.full_like(leads[0], -log_source)),
            jnp.exp2(leads[0] - log_source),
            jnp.exp2(-col1[...] - log_source),
        ]
        cols_ref[...] = jnp.zeros_like(cols_ref)
        for k, factor in enumerate(column_factors):
            for c in range(count):
                cols_ref[k : k + 1, c * LANES : (c + 1) * LANES] = factor[c : c + 1, :]
        b1, b2, b3 = pieces(cols_ref[...])
        right = jnp.concatenate([b1, b2, b1, b2, b3, b1], axis=0).astype(jnp.bfloat16)
        held = [None] * count
        for s in range(groups):
            a1, a2, a3 = pieces(rows_ref[s])
            left = jnp.concatenate([a1, a1, a2, a2, a1, a3], axis=0).astype(jnp.bfloat16)
            tile_ref[...] = lax.dot_general(
                left, right, (((0,), (0,)), ((), ())), preferred_element_type=F32
            )
            column = jnp.broadcast_to(to_column(rows_ref[s, 5:6, :]), (LANES, LANES))
            rows = slice(s * LANES, (s + 1) * LANES)
            src_ref[:, rows] = emb_ref[rows, :].T
            for c in range(count):
                lanes = slice(c * LANES, (c + 1) * LANES)
                base = base_ref[rows, lanes]
                out_ref[rows, lanes] = (base * tile_ref[:, lanes]).astype(jnp.bfloat16)
                term = jnp.sum((base * column).reshape(LANES // 8, 8, LANES), axis=0)
                held[c] = term if held[c] is None else held[c] + term
        for c, term in enumerate(held):
            start_ref[c : c + 1, :] = (
                jnp.sum(term, axis=0, keepdims=True) * column_factors[5][c : c + 1, :]
            )

    @pl.when(jnp.logical_not(near))
    def _():
        zero = jnp.zeros_like(fbar1)
        for k, value in enumerate(
            (row1[...], row2[...], row3[...], fbar1, fbar2[...], fbar3[...], zero, zero)
        ):
            rows_ref[:, k, :] = value
        start_ref[...] = jnp.zeros_like(start_ref)
        for s in range(groups):
            src_ref[:, s * LANES : (s + 1) * LANES] = emb_ref[s * LANES : (s + 1) * LANES, :].T
        columns_of = (None, col1, col2, col3)
        grads_of = (None, gbar1, gbar2, gbar3)

        @pl.loop(0, groups)
        def _(group):
            load_rows(score_ref, tile_ref, group)
            taken = rows_ref[group]
            columns = [to_column(taken[k : k + 1, :]) for k in range(6)]
            rows = pl.ds(pl.multiple_of(group * LANES, LANES), LANES)
            for c in range(count):
                lanes = slice(c * LANES, (c + 1) * LANES)
                value = jnp.zeros((LANES, LANES), F32)
                for k in reversed(range(3)):
                    scores = tile_ref[:, lanes] + columns[k]
                    plan_q = jnp.exp2(scores + (columns_of[k + 1][c : c + 1, :] - log_target))
                    value = value + plan_q * grads_of[k + 1][c : c + 1, :]
                    before = columns_of[k][c : c + 1, :] if k else jnp.zeros((1, LANES), F32)
                    term = jnp.exp2(scores + (before - log_source)) * columns[3 + k]
                    value = value + term
                    if not k:
                        start_ref[c : c + 1, :] -= jnp.sum(term, axis=0, keepdims=True)
                out_ref[rows, lanes] = (-value).astype(jnp.bfloat16)

    reach = counts[1] // 2
    put(z_far_ref, z_block(place_ref, src_ref, out_ref, reach, counts), start_ref[...])
    put(z_back_ref, z_block(place_ref, src_ref, out_ref, 1 - reach, counts), start_ref[...])
    x_far_ref[...] = x_block(place_ref, src_ref, out_ref, counts[0] // 2, counts)
    x_back_ref[...] = x_block(place_ref, src_ref, out_ref, -1, counts)


def put(out_ref, block, rider):
    rows = block.shape[0]
    out_ref[:rows, :] = block
    out_ref[rows:, :] = jnp.zeros_like(out_ref[rows:, :])
    out_ref[rows:, :LANES] = rider


def rider(ref):
    return ref[ref.shape[0] - 8 :, :LANES]


def x_part(y_count, place_ref, grad_ref, tgt_ref, side, out_ref, order_ref):
    block = tgt_ref.shape[1] // (2 * y_count)
    core, turn = place_ref[3], direction(place_ref)
    for k, offset in enumerate((2, 1, -1, 0)):
        step = offset * (2 * side - 1)
        at = lax.rem(place_ref[1] + turn * step + y_count, y_count)
        owner = at * 2 + (core if side else 1 - core)
        order_ref[:, k * block : (k + 1) * block] = tgt_ref[
            :, pl.ds(pl.multiple_of(owner * block, block), block)
        ]
    out_ref[...] = jnp.dot(grad_ref[...], order_ref[...], preferred_element_type=F32)


def first_parts_kernel(counts, y_count, grad_ref, src_ref, tgt_ref, *outs):
    sent_ref, z_ref, z_back_ref, one_ref, own_ref, order_ref = outs
    place_ref = place_of(counts)
    reach = counts[1] // 2
    z_ref[...] = z_block(place_ref, src_ref, grad_ref, reach - 1, counts)
    z_back_ref[...] = z_block(place_ref, src_ref, grad_ref, 2 - reach, counts)
    for out_ref, offset in ((one_ref, 1), (own_ref, 0)):
        out_ref[...] = x_block(place_ref, src_ref, grad_ref, offset, counts)
    x_part(y_count, place_ref, grad_ref, tgt_ref, 0, sent_ref, order_ref)


def other_parts_kernel(counts, y_count, grad_ref, src_ref, tgt_ref, after_ref, kept_ref, *outs):
    *outs, order_ref = outs
    place_ref = place_of(counts)
    x_part(y_count, place_ref, grad_ref, tgt_ref, 1, kept_ref, order_ref)
    reach = counts[1] // 2
    for out_ref, offset in zip(outs, [*range(reach - 2, 0, -1), *range(3 - reach, 1)]):
        out_ref[...] = z_block(place_ref, src_ref, grad_ref, offset, counts)


def forward(out_ref, block_ref, arrived_ref):
    rows = block_ref.shape[0]
    out_ref[:rows, :] = block_ref[...] + arrived_ref[:rows, :]
    out_ref[rows:, :] = arrived_ref[rows:, :]


def token(ref):
    ref[...] = jnp.zeros_like(ref)


def z_kernel(up_ref, down_ref, ahead_ref, behind_ref, start_ref, after_ref, z_ref, back_ref, held_ref):
    forward(z_ref, ahead_ref, up_ref)
    forward(back_ref, behind_ref, down_ref)
    held_ref[...] = start_ref[...] + rider(up_ref) + rider(down_ref)


def x_kernel(up_ref, down_ref, one_ref, own_ref, after_ref, pay_ref, sum_ref, token_ref):
    pay_ref[...] = one_ref[...] + up_ref[...]
    sum_ref[...] = own_ref[...] + down_ref[...]
    token(token_ref)


def y_kernel(
    up_ref, down_ref, one_ref, own_ref, x_up_ref, x_sum_ref, after_ref, pay_ref, sum_ref, x_ref,
    token_ref,
):
    x_kernel(up_ref, down_ref, one_ref, own_ref, after_ref, pay_ref, sum_ref, token_ref)
    x_ref[...] = x_sum_ref[...] + x_up_ref[...]


def chip_kernel(arrived_ref, kept_ref, after_ref, *outs):
    block = outs[0].shape[1]
    for k, out_ref in enumerate(outs[:-1]):
        lanes = slice(k * block, (k + 1) * block)
        out_ref[...] = kept_ref[:, lanes] + arrived_ref[:, lanes]
    token(outs[-1])


def last_z_kernel(
    up_ref, down_ref, ahead_ref, own_ref, start_ref, after_ref, z_ref, z_sum_ref, held_ref
):
    forward(z_ref, ahead_ref, up_ref)
    z_sum_ref[...] = own_ref[...] + down_ref[: own_ref.shape[0], :]
    held_ref[...] = start_ref[...] + rider(up_ref) + rider(down_ref)


def split_kernel(
    counts, z_up_ref, z_sum_ref, start_ref, after_ref,
    far_ref, back_ref, one_ref, last_ref, held_ref,
):
    x_count, place_ref = counts[0], place_of(counts)
    held_ref[...] = start_ref[...] + rider(z_up_ref)
    block = z_sum_ref.shape[0] // x_count
    for out_ref, offset in ((far_ref, 2), (back_ref, -1), (one_ref, 1), (last_ref, 0)):
        at = ring_place(place_ref, 0, offset, x_count)
        rows = pl.ds(pl.multiple_of(at * block, block), block)
        value = z_sum_ref[rows, :] + z_up_ref[rows, :]
        if offset:
            put(out_ref, value, held_ref[...])
        else:
            out_ref[...] = value


def turn_kernel(sum_ref, up_ref, after_ref, out_ref, token_ref):
    for s in range(sum_ref.shape[0] // LANES):
        rows = slice(s * LANES, (s + 1) * LANES)
        out_ref[:, rows] = (sum_ref[rows, :] + up_ref[rows, :]).T
    token(token_ref)


def last_kernel(parts_ref, far_ref, one_ref, back_ref, own_ref, start_ref, out_ref, held_ref):
    rows, half = own_ref.shape
    out_ref[:, :half] = jnp.sum(parts_ref[...], axis=0)
    value, held = own_ref[...], start_ref[...]
    for ref in (far_ref, one_ref, back_ref):
        value = value + ref[:rows, :]
        held = held + rider(ref)
    out_ref[:, half:] = value
    held_ref[...] = held


def call(
    kernel, arguments, outs, scratch=(), in_hbm=(), loose=(), free=(), last=False, flops=1024, name=None
):
    spaces, values = [], []
    for at, value in enumerate(arguments):
        space = pltpu.VMEM
        if at in in_hbm:
            space = pltpu.HBM
        elif at in loose:
            space = pl.ANY
        if at in in_hbm or (space is pltpu.VMEM and value.size >= PINNED and at not in free):
            value = pltpu.with_memory_space_constraint(value, space)
        spaces.append(space)
        values.append(value)
    return pl.pallas_call(
        kernel,
        out_shape=[
            pltpu.VMEM(out.shape, out.dtype) if math.prod(out.shape) >= PINNED and not last else out
            for out in outs
        ],
        in_specs=[pl.BlockSpec(memory_space=space) for space in spaces],
        out_specs=[pl.BlockSpec(memory_space=pltpu.VMEM)] * len(outs),
        scratch_shapes=list(scratch),
        compiler_params=pltpu.CompilerParams(vmem_limit_bytes=VMEM_BYTES),
        cost_estimate=pl.CostEstimate(flops=flops, bytes_accessed=1024, transcendentals=0),
        name=name,
    )(*values)


def exchanged(copies, axis):
    return lax.all_to_all(copies, axis, 0, 0, tiled=True)


def body(cost, src_label, tgt_label, class_mask, g_start, f_bar, g_bar, src_emb, tgt_emb):
    row_count = lax.axis_size("rows")
    col_count = lax.axis_size("cols")
    src_rows, tgt_cols = cost.shape
    width = src_emb.shape[1]
    log_source = -math.log2(src_rows * row_count)
    log_target = -math.log2(tgt_cols * col_count)
    row_shape = (src_rows // LANES, LANES)
    col_shape = (tgt_cols // LANES, LANES)
    src_label, f_bar = src_label.reshape(row_shape), f_bar.reshape(row_shape)
    tgt_label, g_bar = tgt_label.reshape(col_shape), g_bar.reshape(col_shape)
    g_start = g_start.reshape(col_shape)

    def array(shape, dtype=F32):
        return jax.ShapeDtypeStruct(shape, dtype)

    matrix = array(cost.shape)
    row_vector, col_vector = array(row_shape), array(col_shape)
    row_copies = array((col_count,) + row_shape)
    col_copies = array((row_count,) + col_shape)
    row_held, col_held = pltpu.VMEM(row_shape, F32), pltpu.VMEM(col_shape, F32)
    slow = [pltpu.VMEM((LANES, tgt_cols), F32)]

    x_count, z_count, y_count = 4, row_count // 4, col_count // 2
    counts = (x_count, z_count)
    owned = width // row_count
    score, start_base, start_top, copies = call(
        first_kernel,
        (cost, src_label, tgt_label, class_mask, g_start),
        [matrix, matrix, row_vector, row_copies],
        [
            pltpu.VMEM(cost.shape, cost.dtype),
            pltpu.VMEM(row_shape, jnp.int32),
            pltpu.VMEM(col_shape, jnp.int32),
            pltpu.VMEM(class_mask.shape, jnp.int32),
            col_held,
            pltpu.VMEM((LANES, tgt_cols), F32),
            row_held,
            pltpu.SemaphoreType.DMA((4,)),
            pltpu.SemaphoreType.DMA(row_shape[:1]),
        ],
        in_hbm=range(5),
        name="first_row_logs",
    )

    def col_logs(parts, top, base_dual, base):
        return call(
            functools.partial(col_log_kernel, log_source),
            (parts, top, base_dual, base, score),
            [row_vector, col_copies],
            [row_held, col_held] + slow,
                name="col_logs",
        )

    zero = jnp.zeros(col_shape, F32)
    row1, copies = col_logs(exchanged(copies, "cols"), start_top, zero, start_base)
    base, top, col1, copies = call(
        functools.partial(rebase_kernel, log_target),
        (exchanged(copies, "rows"), start_top, start_base, score),
        [matrix, row_vector, col_vector, row_copies],
        [row_held],
        name="second_row_logs",
    )
    row2, copies = col_logs(exchanged(copies, "cols"), top, col1, base)
    col2, copies = call(
        functools.partial(row_log_kernel, log_target),
        (exchanged(copies, "rows"), top, col1, base, score),
        [col_vector, row_copies],
        [col_held, row_held] + slow,
        name="third_row_logs",
    )
    row3, copies = col_logs(exchanged(copies, "cols"), top, col1, base)

    def row_plan(first, parts, grad, dual, row):
        return call(
            functools.partial(row_plan_kernel, log_target, first),
            (parts, grad, dual, row, top, col1, base, score),
            [col_vector, row_copies],
            [col_held, col_held, row_held] + slow,
                name="row_plan",
        )

    def col_plan(parts, outer, dual, row):
        return call(
            functools.partial(col_plan_kernel, log_source),
            (parts, outer, dual, row, top, col1, base, score),
            [row_vector, col_copies],
            [row_held, col_held, col_held] + slow,
                name="col_plan",
        )

    none = jnp.zeros(row_shape, F32)
    col3, copies = row_plan(True, exchanged(copies, "rows"), g_bar, col2, row3)
    fbar3, copies = col_plan(exchanged(copies, "cols"), f_bar, col2, row3)
    gbar2, copies = row_plan(False, exchanged(copies, "rows"), g_bar, col2, row2)
    fbar2, copies = col_plan(exchanged(copies, "cols"), none, col1, row2)
    gbar1, copies = row_plan(False, exchanged(copies, "rows"), g_bar, col1, row1)
    parts = exchanged(copies, "cols")
    devices = [
        (x, y, z, core)
        for x in range(x_count)
        for y in range(y_count)
        for z in range(z_count)
        for core in range(2)
    ]

    def number(x, y, z, core):
        spot = (x % x_count * z_count + z % z_count) * y_count + y % y_count
        return spot * 2 + core

    def turn(value, axis, step):
        moves = []
        for device in devices:
            ahead = list(device)
            ahead[axis] += step * (1 - 2 * device[3])
            moves.append((number(*device), number(*ahead)))
        return lax.ppermute(value, ("rows", "cols"), moves)

    half = tgt_cols // 2
    z_rows, x_rows = x_count * owned, z_count * owned
    z_shape, z_riding = array((z_rows, half)), array((z_rows + 8, half))
    x_shape = array((x_rows, half))
    rounded, src_turned, start, z_far, x_far, z_back, x_back = call(
        functools.partial(grad_kernel, log_source, log_target, counts),
        (
            parts, row1, row2, row3, col1, col2, col3, fbar2, fbar3, gbar1, gbar2, g_bar,
            top, base, src_emb, score,
        ),
        [
            array(cost.shape, jnp.bfloat16),
            array(src_emb.shape[::-1], src_emb.dtype),
            col_vector,
            z_riding,
            x_shape,
            z_riding,
            x_shape,
        ],
        [pltpu.VMEM((row_shape[0], 8, LANES), F32), pltpu.VMEM((8, tgt_cols), F32)] + slow,
        free=(14,),
        name="cost_grad",
    )
    z_up, z_down = turn(z_far, 2, 1), turn(z_back, 2, -1)
    x_up, x_down = turn(x_far, 0, 1), turn(x_back, 0, -1)
    chip_part = array((src_rows, width // 2))
    order = [pltpu.VMEM((tgt_cols, width // 2), jnp.bfloat16)]
    sent, z_3, z_back2, x_one, x_own = call(
        functools.partial(first_parts_kernel, counts, y_count),
        (rounded, src_turned, tgt_emb),
        [chip_part, z_shape, z_shape, x_shape, x_shape],
        order,
        free=(2,),
        flops=BIG,
        name="first_parts",
    )
    small = array((8, LANES))

    def step(kernel, arguments, outs, name, last=False, flops=STEP):
        return call(
            kernel,
            arguments,
            outs,
            loose=(len(arguments) - 1,),
            last=last,
            flops=flops,
            name=name,
        )

    z_pay, z_back, start = step(
        z_kernel,
        (z_up, z_down, z_3, z_back2, start, sent),
        [z_riding, z_riding, small],
        "z_second",
    )
    z_up, z_down = turn(z_pay, 2, 1), turn(z_back, 2, -1)
    arrived = lax.ppermute(sent, "cols", [(at, at ^ 1) for at in range(col_count)])
    kept, z_2, z_1, z_back1, z_own = call(
        functools.partial(other_parts_kernel, counts, y_count),
        (rounded, src_turned, tgt_emb, start),
        [chip_part] + [z_shape] * 4,
        order,
        free=(2,),
        loose=(3,),
        flops=BIG,
        name="other_parts",
    )
    x_pay, x_sum, mark = step(
        x_kernel, (x_up, x_down, x_one, x_own, z_own), [x_shape, x_shape, small], "x_second",
        flops=2**34
    )
    x_up = turn(x_pay, 0, 1)
    y_shape = array((src_rows, width // col_count))
    far, one, back, own, mark = step(
        chip_kernel, (arrived, kept, mark), [y_shape] * 4 + [small], "chip_sums"
    )
    y_up, y_down = turn(far, 1, 1), turn(back, 1, -1)
    z_pay, z_back, start = step(
        z_kernel,
        (z_up, z_down, z_2, z_back1, start, mark),
        [z_riding, z_riding, small],
        "z_third",
        flops=2**31,
    )
    z_up, z_down = turn(z_pay, 2, 1), turn(z_back, 2, -1)
    z_pay, z_sum, start = step(
        last_z_kernel,
        (z_up, z_down, z_1, z_own, start, start),
        [z_riding, z_shape, small],
        "z_fourth",
        flops=2**31,
    )
    z_up = turn(z_pay, 2, 1)
    y_pay, y_sum, first, mark = step(
        y_kernel,
        (y_up, y_down, one, own, x_up, x_sum, start),
        [y_shape, y_shape, x_shape, small],
        "y_second",
    )
    along_z = [[x * z_count + z for z in range(z_count)] for x in range(x_count)]
    first = lax.all_to_all(
        first.reshape(z_count, owned, half), "rows", 0, 0, tiled=True, axis_index_groups=along_z
    )
    y_up = turn(y_pay, 1, 1)
    last, riding = array((owned, half)), array((owned + 8, half))
    x_far, x_back, x_one, x_own, start = step(
        functools.partial(split_kernel, counts),
        (z_up, z_sum, start, mark),
        [riding, riding, riding, last, small],
        "x_blocks",
    )
    x_far, x_one, x_back = turn(x_far, 0, 2), turn(x_one, 0, 1), turn(x_back, 0, -1)
    grad_x, mark = step(
        turn_kernel,
        (y_sum, y_up, start),
        [array((width // col_count, src_rows)), small],
        "grad_x",
        last=True,
    )
    grad_y, start = call(
        last_kernel,
        (first, x_far, x_one, x_back, x_own, start),
        [array((owned, tgt_cols)), col_vector],
        name="last_step",
    )
    g_start_bar = start.reshape(tgt_cols)
    return (g_start_bar, grad_x, grad_y)


def solution(mesh):
    placed = (
        P("rows", "cols"),
        P("rows"),
        P("cols"),
        P(),
        P("cols"),
        P("rows"),
        P("cols"),
        P("rows", None),
        P("cols", None),
    )
    return jax.shard_map(
        body,
        mesh=mesh,
        in_specs=placed,
        out_specs=(P("cols"), P("cols", "rows"), P("rows", "cols")),
        check_vma=False,
    )
```
